128 devices in a mesh: px: 8 (over x, core), py: 16 (over y, z).
Axes of the slice: x: 4, y: 4, z: 4, core: 2. Of those that a mesh axis runs over, the one named last changes fastest.
Arguments:
- field: float32 [512, 512, 256], P('px', 'py'), may hold values from -6 to 6
- diffusivity: bfloat16 [512, 512, 256], P('px', 'py'), may hold values from 0.049804688 to 1
- velocity: bfloat16 [3, 512, 512, 256], P(None, 'px', 'py'), may hold values from -4 to 4
- margin: int32 [8, 2], P('px'), may hold values from 0 to 4, as said below
Outputs:
- advected: float32 [512, 512, 256], P('px', 'py')
- controls: float32 [256, 256, 128], P('px', 'py')
The draws below stay inside these ranges and needn't reach their ends.
Inputs may be any that keep to these rules, and one draw needn't show every extreme that they name: One subdomain has an upper margin of 0 and one has a lower margin of 4.
All inputs are finite; a program needn't handle non-finite values.
Results may differ from the reference program's by a relative error of at most 0.0003.
Values may be sent and summed in bfloat16 or wider, within the bound.
No kernel may reach another device: no remote copies, remote signals or barrier semaphores. Data moves between devices by JAX's collectives and lax.ppermute only.
A program may use at most 192 MiB of HBM per device.

```python
import math
import jax
import jax.numpy as jnp
from jax import lax

CX = 64
NZ = 256
STEPS = 4
SWEEPS = 2
OVMAX = 4
NX = 512
NY = 512
N_PX = 8


def draw_margin(key, part):
    first_key, second_key, third_key = jax.random.split(jax.random.fold_in(key, 71), 3)
    values = jax.random.randint(first_key, (N_PX, 2), 0, OVMAX + 1)
    lower_owner = jax.random.randint(second_key, (), 0, N_PX)
    upper_owner = jax.random.randint(third_key, (), 0, N_PX)
    values = values.at[lower_owner, 0].set(OVMAX)
    values = values.at[upper_owner, 1].set(0)
    return values.astype(jnp.int32)


def steps_of(stream_key, dims, cuts, smallest, largest):
    def one(axis_at, parts):
        steps = jax.random.uniform(jax.random.fold_in(jax.random.fold_in(stream_key, 6), axis_at), (parts,), jnp.float32, smallest / len(cuts), largest / len(cuts))
        return jnp.repeat(jnp.exp(steps), dims[axis_at] // parts).reshape((-1,) + (1,) * (len(dims) - axis_at - 1))

    factor_of = one(*cuts[0])
    for cut in cuts[1:]:
        factor_of = factor_of * one(*cut)
    return factor_of


def scatter_about(own_key, shape, spread, limit, shards=(), kind=jnp.bfloat16):
    factor_of = steps_of(own_key, shape, shards, -0.22, 0.18) if shards else 1.0
    result = jax.random.normal(own_key, shape, jnp.float32) * spread * factor_of
    return jnp.minimum(jnp.maximum(result, -limit), limit).astype(kind)


def setup_inputs(seed: int = 0) -> dict:
    key_of = jax.random.split(jax.random.key(seed), 5)
    return {
        "field": scatter_about(key_of[0], (NX, NY, NZ), 1.0, 6.0, ((0, 8), (1, 16)), jnp.float32),
        "diffusivity": jnp.clip(jnp.exp(math.log(1.0) - 2.9996462 * jax.random.uniform(key_of[1], (NX, NY, NZ), jnp.float32) ** steps_of(key_of[1], (NX, NY, NZ), ((0, 8), (1, 16)), -0.2, 0.2)), 0.049804688, 1.0).astype(jnp.bfloat16),
        "velocity": scatter_about(key_of[2], (3, NX, NY, NZ), 1.0, 4.0, ((1, 8), (2, 16))),
        "margin": draw_margin(jax.random.fold_in(key_of[4], 71), 0),
    }


HIGH = lax.Precision.HIGHEST

def bspline(offset):
    magnitude = jnp.abs(offset)
    inner_part = (4.0 - 6.0 * magnitude * magnitude + 3.0 * magnitude ** 3) / 6.0
    outer_part = jnp.maximum(2.0 - magnitude, 0.0) ** 3 / 6.0
    return jnp.where(magnitude < 1.0, inner_part, outer_part)

def basis(samples, knots, samp_total, ctrl_total):
    position = samples[:, None].astype(jnp.float32) - 2.0 * knots[None, :].astype(jnp.float32) - 0.5
    values = bspline(0.5 * position)
    valid = (samples[:, None] >= 0) & (samples[:, None] < samp_total) & (knots[None, :] >= 0) & (knots[None, :] < ctrl_total)
    return jnp.where(valid, values, 0.0)

def gram(row_knots, col_knots, first, count, samp_total, ctrl_total):
    window = first + jnp.arange(count, dtype=jnp.int32)
    left_basis = basis(window, row_knots, samp_total, ctrl_total)
    right_basis = basis(window, col_knots, samp_total, ctrl_total)
    return jnp.dot(left_basis.T.astype(jnp.float32), right_basis.astype(jnp.float32), precision=HIGH, preferred_element_type=jnp.float32)

def chol_solve(lower, rhs_block):
    middle = lax.linalg.triangular_solve(lower, rhs_block, left_side=True, lower=True)
    return lax.linalg.triangular_solve(lower, middle, left_side=True, lower=True, transpose_a=True)

def sub_gram(start, left, right, block, samp_total, ctrl_total):
    width = block + 2 * OVMAX
    knots = start - OVMAX + jnp.arange(width, dtype=jnp.int32)
    full = gram(knots, knots, 2 * (start - OVMAX) - 4, 2 * width + 8, samp_total, ctrl_total)
    inside = (knots >= start - left) & (knots < start + block + right) & (knots >= 0) & (knots < ctrl_total)
    weight = inside.astype(jnp.float32)
    return (full * weight[:, None] * weight[None, :] + jnp.diag(1.0 - weight), weight)

def inner(array, shift_x, shift_y, shift_z):
    size_x, size_y, size_z = array.shape[-3:]
    return array[..., 1 + shift_x:size_x - 1 + shift_x, 1 + shift_y:size_y - 1 + shift_y, 1 + shift_z:size_z - 1 + shift_z]

def update(padded, kappa_pad, velo_pad):
    centre = inner(padded, 0, 0, 0)
    kappa_mid = inner(kappa_pad, 0, 0, 0)
    flux = velo_pad * (0.5 * padded * padded)[None]
    tendency = jnp.zeros_like(centre)
    for axis_index in range(3):
        plus = [0, 0, 0]
        minus = [0, 0, 0]
        plus[axis_index] = 1
        minus[axis_index] = -1
        upper = inner(padded, *plus)
        lower = inner(padded, *minus)
        kappa_up = inner(kappa_pad, *plus)
        kappa_low = inner(kappa_pad, *minus)
        flux_up = inner(flux[axis_index], *plus)
        flux_low = inner(flux[axis_index], *minus)
        tendency = tendency + 0.5 * (kappa_mid + kappa_up) * (upper - centre) - 0.5 * (kappa_mid + kappa_low) * (centre - lower) - 0.5 * (flux_up - flux_low)
    return centre + 0.1 * tendency

def fit_matrix(samp_total):
    ctrl_total = samp_total // 2
    table = basis(jnp.arange(samp_total, dtype=jnp.int32), jnp.arange(ctrl_total, dtype=jnp.int32), samp_total, ctrl_total)
    normal = jnp.dot(table.T.astype(jnp.float32), table.astype(jnp.float32), precision=HIGH, preferred_element_type=jnp.float32)
    return chol_solve(jnp.linalg.cholesky(normal), table.T)

def reference(field, diffusivity, velocity, margin):
    size_x, size_y, size_z = field.shape
    kappa_pad = jnp.pad(diffusivity.astype(jnp.float32), 1)
    velo_pad = jnp.pad(velocity.astype(jnp.float32), ((0, 0), (1, 1), (1, 1), (1, 1)))
    current = field
    for step_index in range(STEPS):
        current = update(jnp.pad(current, 1), kappa_pad, velo_pad)
    advected = current
    z_fit = fit_matrix(size_z)
    zfit = jnp.einsum('xyz,mz->xym', advected, z_fit, precision=HIGH)
    y_fit = fit_matrix(size_y)
    yfit = jnp.einsum('my,xyz->xmz', y_fit, zfit, precision=HIGH)
    samples = yfit.reshape(size_x, -1)
    ctrl_x = size_x // 2
    x_table = basis(jnp.arange(size_x, dtype=jnp.int32), jnp.arange(ctrl_x, dtype=jnp.int32), size_x, ctrl_x)
    rhs_all = jnp.dot(x_table.T.astype(jnp.float32), samples.astype(jnp.float32), precision=HIGH, preferred_element_type=jnp.float32)
    gram_all = jnp.dot(x_table.T.astype(jnp.float32), x_table.astype(jnp.float32), precision=HIGH, preferred_element_type=jnp.float32)
    block = CX // 2
    fitted = jnp.zeros_like(rhs_all)
    for sweep_index in range(SWEEPS):
        resid = rhs_all - jnp.dot(gram_all.astype(jnp.float32), fitted.astype(jnp.float32), precision=HIGH, preferred_element_type=jnp.float32)
        pieces = []
        for owner in range(N_PX):
            start = owner * block
            local_gram, weight = sub_gram(start, margin[owner, 0], margin[owner, 1], block, size_x, ctrl_x)
            knots = start - OVMAX + jnp.arange(block + 2 * OVMAX, dtype=jnp.int32)
            local_rhs = resid[jnp.clip(knots, 0, ctrl_x - 1)] * weight[:, None]
            correct = chol_solve(jnp.linalg.cholesky(local_gram), local_rhs)
            pieces.append(correct[OVMAX:OVMAX + block])
        fitted = fitted + jnp.concatenate(pieces, axis=0)
    return (advected, fitted.reshape(ctrl_x, size_y // 2, size_z // 2))
```

```python
import functools

import jax
import jax.numpy as jnp
import numpy as np
from jax import lax
from jax.experimental import pallas as pl
from jax.experimental.pallas import tpu as pltpu
from jax.sharding import PartitionSpec as P

STEPS = 4
OVMAX = 4
BX = 64
BY = 32
NZ = 256
MZ = 128
W = 4
EX = BX + 2 * W
EY = BY + 2 * W
HIGH = lax.Precision.HIGHEST


def bspline(t):
    m = np.abs(t)
    inner = (4.0 - 6.0 * m * m + 3.0 * m**3) / 6.0
    outer = np.maximum(2.0 - m, 0.0) ** 3 / 6.0
    return np.where(m < 1.0, inner, outer)


def basis(n):
    j = np.arange(n)[:, None]
    k = np.arange(n // 2)[None, :]
    return bspline((j - 2.0 * k - 0.5) / 2.0)


def fit_matrix(n):
    b = basis(n)
    return np.linalg.solve(b.T @ b, b.T)


def y_tables(count):
    total = count * BY
    s = fit_matrix(total)
    own = BY // 2
    diag = np.zeros((count, own, BY))
    up = np.zeros((count, 3, BY))
    down = np.zeros((count, 3, BY))
    couple = np.zeros((count, own, count, 3))
    for q in range(count):
        cols = s[:, q * BY : (q + 1) * BY]
        diag[q] = cols[q * own : (q + 1) * own]
        if q < count - 1:
            below = cols[(q + 1) * own :]
            u, sv, vt = np.linalg.svd(below, full_matrices=False)
            assert sv[3] < 1e-10 * sv[0]
            up[q] = vt[:3]
            left = u[:, :3] * sv[:3]
            for t in range(q + 1, count):
                couple[t, :, q] = left[(t - q - 1) * own : (t - q) * own]
        if q > 0:
            above = cols[: q * own]
            u, sv, vt = np.linalg.svd(above, full_matrices=False)
            assert sv[3] < 1e-10 * sv[0]
            down[q] = vt[:3]
            left = u[:, :3] * sv[:3]
            for t in range(q):
                couple[t, :, q] = left[t * own : (t + 1) * own]
    return [a.astype(np.float32) for a in (diag, up, down, couple.reshape(count, own, count * 3))]


def x_tables(count):
    total = count * BX
    block = BX // 2
    ctrl = total // 2
    b = basis(total)
    g = b.T @ b
    width = block + 2 * OVMAX
    gpad = np.zeros((ctrl + 16, ctrl + 16))
    gpad[8:-8, 8:-8] = g
    inverse = np.zeros((3, OVMAX + 1, OVMAX + 1, block, width))
    band = np.zeros((3, width, width + 6))
    for cls, p in enumerate((0, 1, count - 1)):
        start = p * block
        knots = start - OVMAX + np.arange(width)
        lo = start - OVMAX + 8
        full = gpad[lo : lo + width, lo : lo + width]
        band[cls] = gpad[lo : lo + width, lo - 3 : lo + width + 3]
        for m0 in range(OVMAX + 1):
            for m1 in range(OVMAX + 1):
                inside = (knots >= start - m0) & (knots < start + block + m1) & (knots >= 0) & (knots < ctrl)
                w = inside.astype(np.float64)
                mat = full * w[:, None] * w[None, :] + np.diag(1.0 - w)
                inverse[cls, m0, m1] = (np.linalg.inv(mat) * w[None, :])[OVMAX : OVMAX + block]
    bt = np.zeros((block + 4, BX))
    for r in range(block + 4):
        bt[r] = bspline((np.arange(BX) - 2.0 * (r - 2) - 0.5) / 2.0)
    return inverse.reshape(-1, block, width).astype(np.float32), band.astype(np.float32), bt.astype(np.float32)


def stencil_body(mask_ref, f_ref, k_ref, v_ref, yl_ref, yh_ref, xl_ref, xh_ref, dll_ref, dlh_ref, dhl_ref, dhh_ref,
                 fit_hi_ref, fit_lo_ref, adv_ref, zfit_ref, u_s, v0_s, v1_s, v2_s, kx_s, ky_s, kyd_s, kz_s, kzd_s, c_s):
    f32 = jnp.float32
    from_low_x = mask_ref[0]
    from_high_x = mask_ref[1]
    from_low_y = mask_ref[2]
    from_high_y = mask_ref[3]
    dest = (u_s, c_s, v0_s, v1_s, v2_s)

    def own_planes(group, carry):
        at = group * 4
        ul = yl_ref[BX + group].astype(f32) * from_low_y
        uh = yh_ref[BX + group].astype(f32) * from_high_y
        for i in range(4):
            x = at + i
            kl = yl_ref[x].astype(f32) * from_low_y
            kh = yh_ref[x].astype(f32) * from_high_y
            u_s[x + W, 0:BY] = f_ref[x]
            u_s[x + W, BY:EY] = jnp.concatenate([uh[4 * i : 4 * i + 4], ul[4 * i : 4 * i + 4]], axis=0)
            for n in range(4):
                ref = dest[1 + n]
                ref[x + W, 0:BY] = (k_ref[x] if n == 0 else v_ref[n - 1, x]).astype(f32)
                ref[x + W, BY:EY] = jnp.concatenate([kh[4 * n : 4 * n + 4], kl[4 * n : 4 * n + 4]], axis=0)
        return carry

    lax.fori_loop(0, BX // 4, own_planes, 0)
    for n in range(5):
        for base, ref, below, above, scale in (
            (0, xl_ref, dll_ref, dlh_ref, from_low_x),
            (BX + W, xh_ref, dhl_ref, dhh_ref, from_high_x),
        ):
            low = below[n].astype(f32) * (scale * from_low_y)
            high = above[n].astype(f32) * (scale * from_high_y)
            for i in range(W):
                dest[n][base + i, 0:BY] = ref[n * W + i].astype(f32) * scale
                dest[n][base + i, BY:EY] = jnp.concatenate([high[4 * i : 4 * i + 4], low[4 * i : 4 * i + 4]], axis=0)

    lane = lax.broadcasted_iota(jnp.int32, (EY, 128), 1)
    first = lane == 0
    final = lane == 127

    def z_up(a):
        lo = pltpu.roll(a[:, :128], 1, 1)
        hi = pltpu.roll(a[:, 128:], 1, 1)
        return jnp.concatenate([jnp.where(first, 0.0, lo), jnp.where(first, lo, hi)], axis=1)

    def z_down(a):
        lo = pltpu.roll(a[:, :128], 127, 1)
        hi = pltpu.roll(a[:, 128:], 127, 1)
        return jnp.concatenate([jnp.where(final, hi, lo), jnp.where(final, 0.0, hi)], axis=1)

    def coefficients(x, carry):
        k, kx_low = carry
        k_next = c_s[jnp.minimum(x + 1, EX - 1)]
        kx = 0.05 * (k + k_next)
        ky = 0.05 * (k + pltpu.roll(k, EY - 1, 0))
        kyd = pltpu.roll(ky, 1, 0)
        kz = 0.05 * (k + z_down(k))
        kzd = 0.05 * (k + z_up(k))
        kx_s[x] = kx
        ky_s[x] = ky
        kyd_s[x] = kyd
        kz_s[x] = kz
        kzd_s[x] = kzd
        c_s[x] = 1.0 - ((kx + kx_low) + (ky + kyd) + (kz + kzd))
        return k_next, kx

    lax.fori_loop(0, EX, coefficients, (c_s[0], jnp.zeros((EY, NZ), f32)))

    row = lax.broadcasted_iota(jnp.int32, (EY, NZ), 0)
    row_mask = jnp.where(row < BY, 1.0, jnp.where(row < BY + W, from_high_y, from_low_y))

    for step in range(STEPS):
        lo = step
        hi = EX - 1 - step

        def one_plane(x, carry, step=step):
            partial, up = carry
            u = u_s[x]
            w = 0.025 * u
            g0 = v0_s[x] * w
            g1 = v1_s[x] * w
            g2 = v2_s[x] * w
            done = partial + u * (kx_s[x - 1] - g0)
            prev = x - 1
            plane_mask = jnp.where(prev < W, from_low_x, jnp.where(prev >= BX + W, from_high_x, 1.0))
            u_s[prev] = done * (row_mask * plane_mask)
            up_next = u * (kx_s[x] + g0)
            total = u * c_s[x] + up
            total = total + pltpu.roll(u * (ky_s[x] + g1), 1, 0)
            total = total + pltpu.roll(u * (kyd_s[x] - g1), EY - 1, 0)
            total = total + z_up(u * (kz_s[x] + g2))
            total = total + z_down(u * (kzd_s[x] - g2))
            return total, up_next

        first_u = u_s[lo]
        first_up = first_u * (kx_s[lo] + v0_s[lo] * (0.025 * first_u))
        lax.fori_loop(lo + 1, hi + 1, one_plane, (jnp.zeros((EY, NZ), f32), first_up))

    fit_hi = fit_hi_ref[...]
    fit_lo = fit_lo_ref[...]

    def fit_planes(group, carry):
        at = group * 8
        part = u_s[pl.ds(at + W, 8), 0:BY]
        adv_ref[pl.ds(at, 8)] = part
        flat = part.reshape(8 * BY, NZ)
        flat_hi = flat.astype(jnp.bfloat16)
        flat_lo = (flat - flat_hi.astype(f32)).astype(jnp.bfloat16)
        dot = functools.partial(jnp.dot, preferred_element_type=f32)
        out = dot(flat_hi, fit_hi) + (dot(flat_hi, fit_lo) + dot(flat_lo, fit_hi))
        zfit_ref[pl.ds(at, 8)] = out.reshape(8, BY, MZ)
        return carry

    lax.fori_loop(0, BX // 8, fit_planes, 0)


def time_steps(masks, field, diffusivity, velocity, halos, fit_hi, fit_lo):
    vmem = pl.BlockSpec(memory_space=pltpu.VMEM)
    return pl.pallas_call(
        stencil_body,
        out_shape=(
            jax.ShapeDtypeStruct((BX, BY, NZ), jnp.float32),
            jax.ShapeDtypeStruct((BX, BY, MZ), jnp.float32),
        ),
        in_specs=[pl.BlockSpec(memory_space=pltpu.SMEM)] + [vmem] * 13,
        out_specs=(vmem, vmem),
        scratch_shapes=[pltpu.VMEM((EX, EY, NZ), jnp.float32)] * 10,
        compiler_params=pltpu.CompilerParams(vmem_limit_bytes=60 * 1024 * 1024),
        name="time_steps",
    )(masks, field, diffusivity, velocity, *halos, fit_hi, fit_lo)


def ring(n, d):
    return [(i, (i + d) % n) for i in range(n)]


def shift(a, axis, d):
    return lax.ppermute(a, axis, ring(lax.axis_size(axis), d))


def shift_both(a, dx, dy):
    nx = lax.axis_size("px")
    ny = lax.axis_size("py")
    pairs = [(i * ny + j, ((i + dx) % nx) * ny + (j + dy) % ny) for i in range(nx) for j in range(ny)]
    return lax.ppermute(a, ("px", "py"), pairs)


def halo_parts(field, diffusivity, velocity):
    u = field.astype(jnp.bfloat16)

    def y_face(rows):
        kv = jnp.concatenate([diffusivity[:, rows]] + [velocity[n][:, rows] for n in range(3)], axis=1)
        return jnp.concatenate([kv, u[:, rows].reshape(BX // 4, 16, NZ)], axis=0)

    def x_face(planes):
        return jnp.concatenate([u[planes], diffusivity[planes]] + [velocity[n][planes] for n in range(3)], axis=0)

    def corner(planes, rows):
        return jnp.stack(
            [a[planes, rows].reshape(16, NZ) for a in (u, diffusivity, velocity[0], velocity[1], velocity[2])]
        )

    head = slice(0, W)
    ty = slice(BY - W, BY)
    tx = slice(BX - W, BX)
    yl = shift(y_face(ty), "py", 1)
    yh = shift(y_face(head), "py", -1)
    xl = shift(x_face(tx), "px", 1)
    xh = shift(x_face(head), "px", -1)
    dll = shift_both(corner(tx, ty), 1, 1)
    dlh = shift_both(corner(tx, head), 1, -1)
    dhl = shift_both(corner(head, ty), -1, 1)
    dhh = shift_both(corner(head, head), -1, -1)
    return yl, yh, xl, xh, dll, dlh, dhl, dhh


def mm(a, b):
    return jnp.dot(a, b, precision=HIGH, preferred_element_type=jnp.float32)


def x_operator(margin, tables, p, count):
    inverse, band, bt = tables
    margins = lax.all_gather(margin[0], "px")

    def rows_of(owner):
        own = jnp.clip(owner, 0, count - 1)
        cls = jnp.where(own == 0, 0, jnp.where(own == count - 1, 2, 1))
        m = lax.dynamic_index_in_dim(margins, own, 0, keepdims=False)
        m = jnp.clip(m, 0, OVMAX)
        n = OVMAX + 1
        found = lax.dynamic_index_in_dim(inverse, (cls * n + m[0]) * n + m[1], 0, keepdims=False)
        return found * ((owner >= 0) & (owner < count)).astype(jnp.float32), cls

    inverse = jnp.asarray(inverse)
    e, cls = rows_of(p)
    e_low, _ = rows_of(p - 1)
    e_high, _ = rows_of(p + 1)
    block = BX // 2
    g = lax.dynamic_index_in_dim(jnp.asarray(band), cls, 0, keepdims=False)
    has_low = (p > 0).astype(jnp.float32)
    has_high = (p < count - 1).astype(jnp.float32)
    q = mm(e, g)
    ql = q[:, :7] * has_low
    q0 = q[:, 7 : 7 + block]
    qr = q[:, 7 + block :] * has_high
    a = 2.0 * e - mm(q0, e)
    ql_e = mm(ql, e_low[block - 7 :])
    qr_e = mm(qr, e_high[:7])
    w = a[:, 2 : block + 6]
    w = w - jnp.pad(ql_e[:, block + 2 : block + 8], ((0, 0), (0, block - 2)))
    w = w - jnp.pad(qr_e[:, 0:6], ((0, 0), (block - 2, 0)))
    bt = jnp.asarray(bt)
    full = jnp.concatenate(
        [
            mm(w, bt),
            a[:, 0:6] * has_low,
            -ql,
            a[:, block + 2 :] * has_high,
            -qr,
            -ql_e[:, 0:6] * (p > 1).astype(jnp.float32),
            -qr_e[:, block + 2 :] * (p < count - 2).astype(jnp.float32),
        ],
        axis=1,
    )
    kappa = mm(jnp.concatenate([e[block - 7 :, 2 : block + 6], e[:7, 2 : block + 6]], axis=0), bt)
    send = jnp.concatenate([bt[block - 2 :], kappa[:7], bt[:6], kappa[7:]], axis=0)
    return send, full


def per_device(field, diffusivity, velocity, margin):
    count_x = lax.axis_size("px")
    count_y = lax.axis_size("py")
    p = lax.axis_index("px")
    q = lax.axis_index("py")
    masks = jnp.stack([p > 0, p < count_x - 1, q > 0, q < count_y - 1]).astype(jnp.float32)
    s_z = fit_matrix(NZ).T.astype(np.float32)
    fit_hi = s_z.astype(jnp.bfloat16)
    fit_lo = (s_z - fit_hi.astype(np.float32)).astype(jnp.bfloat16)
    halos = halo_parts(field, diffusivity, velocity)
    send, full = x_operator(margin, x_tables(count_x), p, count_x)
    diag, up, down, couple = [
        lax.dynamic_index_in_dim(jnp.asarray(t), q, 0, keepdims=False) for t in y_tables(count_y)
    ]
    advected, zfit = time_steps(masks, field, diffusivity, velocity, halos, jnp.asarray(fit_hi), jnp.asarray(fit_lo))

    lines = zfit.reshape(BX, BY * MZ)
    out = mm(send, lines)
    from_low = shift(out[:13], "px", 1)
    from_high = shift(out[13:], "px", -1)
    from_low2 = shift(out[:6].astype(jnp.bfloat16), "px", 2)
    from_high2 = shift(out[13:19].astype(jnp.bfloat16), "px", -2)
    stacked = jnp.concatenate(
        [lines, from_low, from_high, from_low2.astype(jnp.float32), from_high2.astype(jnp.float32)], axis=0
    )
    xfit = mm(full, stacked).reshape(BX // 2, BY, MZ)

    both = jnp.einsum("cy,xyz->cxz", jnp.concatenate([up, down], axis=0), xfit, precision=HIGH)
    target = jnp.arange(count_y)[:, None, None, None]
    carries = jnp.where(target > q, both[None, :3], both[None, 3:])
    got = lax.all_to_all(carries, "py", split_axis=0, concat_axis=0, tiled=True)
    controls = jnp.einsum("my,xyz->xmz", diag, xfit, precision=HIGH)
    controls = controls + jnp.einsum(
        "mc,cxz->xmz", couple, got.reshape(count_y * 3, BX // 2, MZ), precision=HIGH
    )
    return advected, controls


def solution(mesh):
    placed = (P("px", "py", None), P("px", "py", None), P(None, "px", "py", None), P("px", None))
    return jax.shard_map(
        per_device,
        mesh=mesh,
        in_specs=placed,
        out_specs=(P("px", "py", None), P("px", "py", None)),
        check_vma=False,
    )
```

```python
import functools

import jax
import jax.numpy as jnp
import numpy as np
from jax import lax
from jax.experimental import pallas as pl
from jax.experimental.pallas import tpu as pltpu
from jax.sharding import PartitionSpec as P

STEPS = 4
OVMAX = 4
BX = 64
BY = 32
NZ = 256
MZ = 128
W = 4
EX = BX + 2 * W
EY = BY + 2 * W
HIGH = lax.Precision.HIGHEST


def bspline(t):
    m = np.abs(t)
    inner = (4.0 - 6.0 * m * m + 3.0 * m**3) / 6.0
    outer = np.maximum(2.0 - m, 0.0) ** 3 / 6.0
    return np.where(m < 1.0, inner, outer)


def basis(n):
    j = np.arange(n)[:, None]
    k = np.arange(n // 2)[None, :]
    return bspline((j - 2.0 * k - 0.5) / 2.0)


def fit_matrix(n):
    b = basis(n)
    return np.linalg.solve(b.T @ b, b.T)


def y_tables(count):
    total = count * BY
    s = fit_matrix(total)
    own = BY // 2
    diag = np.zeros((count, own, BY))
    up = np.zeros((count, 3, BY))
    down = np.zeros((count, 3, BY))
    couple = np.zeros((count, own, count, 3))
    for q in range(count):
        cols = s[:, q * BY : (q + 1) * BY]
        diag[q] = cols[q * own : (q + 1) * own]
        if q < count - 1:
            below = cols[(q + 1) * own :]
            u, sv, vt = np.linalg.svd(below, full_matrices=False)
            assert sv[3] < 1e-10 * sv[0]
            up[q] = vt[:3]
            left = u[:, :3] * sv[:3]
            for t in range(q + 1, count):
                couple[t, :, q] = left[(t - q - 1) * own : (t - q) * own]
        if q > 0:
            above = cols[: q * own]
            u, sv, vt = np.linalg.svd(above, full_matrices=False)
            assert sv[3] < 1e-10 * sv[0]
            down[q] = vt[:3]
            left = u[:, :3] * sv[:3]
            for t in range(q):
                couple[t, :, q] = left[t * own : (t + 1) * own]
    return [a.astype(np.float32) for a in (diag, up, down, np.concatenate([couple, couple[..., :1]], axis=3).reshape(count, own, count * 4))]


def x_tables(count):
    total = count * BX
    block = BX // 2
    ctrl = total // 2
    b = basis(total)
    width = block + 2 * OVMAX
    gpad = np.zeros((ctrl + 16, ctrl + 16))
    gpad[8:-8, 8:-8] = b.T @ b
    bt = bspline((np.arange(BX)[None] - 2.0 * (np.arange(block + 4)[:, None] - 2) - 0.5) / 2.0)
    base, send, near = [], [], []
    for cls, p in enumerate((0, 1, count - 1)):
        has_low = float(cls != 0)
        has_high = float(cls != 2)
        start = p * block
        knots = start - OVMAX + np.arange(width)
        lo = start - OVMAX + 8
        full = gpad[lo : lo + width, lo : lo + width]
        band = gpad[lo : lo + width, lo - 3 : lo + width + 3]
        for m0 in range(OVMAX + 1):
            for m1 in range(OVMAX + 1):
                inside = (knots >= start - m0) & (knots < start + block + m1) & (knots >= 0) & (knots < ctrl)
                w = inside.astype(np.float64)
                mat = full * w[:, None] * w[None, :] + np.diag(1.0 - w)
                e = (np.linalg.inv(mat) * w[None, :])[OVMAX : OVMAX + block]
                q = e @ band
                ql = q[:, :7] * has_low
                qr = q[:, 7 + block :] * has_high
                two = 2.0 * e - q[:, 7 : 7 + block] @ e
                low = two[:, 0:6] * has_low
                high = two[:, block + 2 :] * has_high
                base.append(np.concatenate([two[:, 2 : block + 6] @ bt, low, -ql, high, -qr], axis=1))
                send.append(
                    np.concatenate(
                        [bt[block - 2 :], e[block - 7 :, 2 : block + 6] @ bt, bt[:6], e[:7, 2 : block + 6] @ bt]
                    )
                )
                zero = np.zeros((7, 6))
                as_low = np.concatenate(
                    [e[block - 7 :, block + 2 :] @ bt[0:6], np.zeros((7, 26)), e[block - 7 :, 0:6] * has_low, zero], axis=1
                )
                as_high = np.concatenate(
                    [e[:7, 0:6] @ bt[block - 2 :], np.zeros((7, 26)), zero, e[:7, block + 2 :] * has_high], axis=1
                )
                near.append(np.stack([as_low, as_high]))
    return [np.stack(t).astype(np.float32) for t in (base, send, near)]


def stencil_body(mask_ref, f_ref, k_ref, v_ref, yl_ref, yh_ref, xl_ref, xh_ref, dll_ref, dlh_ref, dhl_ref, dhh_ref,
                 fit_hi_ref, fit_lo_ref, adv_ref, zfit_ref, u_s, v0_s, v1_s, v2_s, kx_s, ky_s, kyd_s, kz_s, kzd_s, c_s):
    f32 = jnp.float32
    from_low_x = mask_ref[0]
    from_high_x = mask_ref[1]
    from_low_y = mask_ref[2]
    from_high_y = mask_ref[3]
    dest = (u_s, c_s, v0_s, v1_s, v2_s)

    def own_planes(group, carry):
        at = group * 4
        ul = yl_ref[group, 4].astype(f32) * from_low_y
        uh = yh_ref[group, 4].astype(f32) * from_high_y
        gap = jnp.zeros((4, NZ), f32)
        for i in range(4):
            x = at + i
            kl = yl_ref[group, i].astype(f32) * from_low_y
            kh = yh_ref[group, i].astype(f32) * from_high_y
            u_s[x + W, 0:BY] = f_ref[x]
            rest = jnp.concatenate([kh[7:8], kh[15:16], gap, kl[12:13], kl[4:5]], axis=0)
            u_s[x + W, BY:EY] = rest + jnp.concatenate([uh[4 * i : 4 * i + 4], ul[4 * i : 4 * i + 4]], axis=0)
            for n in range(4):
                ref = dest[1 + n]
                ref[x + W, 0:BY] = (k_ref[x] if n == 0 else v_ref[n - 1, x]).astype(f32)
                ref[x + W, BY:EY] = jnp.concatenate([kh[4 * n : 4 * n + 4], kl[4 * n : 4 * n + 4]], axis=0)
        return carry

    lax.fori_loop(0, BX // 4, own_planes, 0)
    for n in range(5):
        for base, ref, below, above, scale, near, outer in (
            (0, xl_ref, dll_ref, dlh_ref, from_low_x, (W - 1, W - 2), 0),
            (BX + W, xh_ref, dhl_ref, dhh_ref, from_high_x, (0, 1), W - 1),
        ):
            low = below[n].astype(f32) * (scale * from_low_y)
            high = above[n].astype(f32) * (scale * from_high_y)
            for i in range(W):
                value = ref[n * W + i].astype(f32)
                if n == 0 and i in near:
                    value = value + ref[(3 + near.index(i)) * W + outer].astype(f32)
                dest[n][base + i, 0:BY] = value * scale
                dest[n][base + i, BY:EY] = jnp.concatenate([high[4 * i : 4 * i + 4], low[4 * i : 4 * i + 4]], axis=0)

    lane = lax.broadcasted_iota(jnp.int32, (EY, 128), 1)
    first = lane == 0
    final = lane == 127

    def z_up(a):
        lo = pltpu.roll(a[:, :128], 1, 1)
        hi = pltpu.roll(a[:, 128:], 1, 1)
        return jnp.concatenate([jnp.where(first, 0.0, lo), jnp.where(first, lo, hi)], axis=1)

    def z_down(a):
        lo = pltpu.roll(a[:, :128], 127, 1)
        hi = pltpu.roll(a[:, 128:], 127, 1)
        return jnp.concatenate([jnp.where(final, hi, lo), jnp.where(final, 0.0, hi)], axis=1)

    def coefficients(x, carry):
        k, kx_low = carry
        k_next = c_s[jnp.minimum(x + 1, EX - 1)]
        kx = 0.05 * (k + k_next)
        ky = 0.05 * (k + pltpu.roll(k, EY - 1, 0))
        kyd = pltpu.roll(ky, 1, 0)
        kz = 0.05 * (k + z_down(k))
        kzd = 0.05 * (k + z_up(k))
        kx_s[x] = kx
        ky_s[x] = ky
        kyd_s[x] = kyd
        kz_s[x] = kz
        kzd_s[x] = kzd
        c_s[x] = 1.0 - ((kx + kx_low) + (ky + kyd) + (kz + kzd))
        return k_next, kx

    lax.fori_loop(0, EX, coefficients, (c_s[0], jnp.zeros((EY, NZ), f32)), unroll=4)

    row = lax.broadcasted_iota(jnp.int32, (EY, NZ), 0)
    row_mask = jnp.where(row < BY, 1.0, jnp.where(row < BY + W, from_high_y, from_low_y))

    for step in range(STEPS):
        lo = step
        hi = EX - 1 - step

        def one_plane(x, carry, step=step):
            partial, up = carry
            u = u_s[x]
            w = 0.025 * u
            g0 = v0_s[x] * w
            g1 = v1_s[x] * w
            g2 = v2_s[x] * w
            done = partial + u * (kx_s[x - 1] - g0)
            prev = x - 1
            plane_mask = jnp.where(prev < W, from_low_x, jnp.where(prev >= BX + W, from_high_x, 1.0))
            u_s[prev] = done * (row_mask * plane_mask)
            up_next = u * (kx_s[x] + g0)
            total = u * c_s[x] + up
            total = total + pltpu.roll(u * (ky_s[x] + g1), 1, 0)
            total = total + pltpu.roll(u * (kyd_s[x] - g1), EY - 1, 0)
            total = total + z_up(u * (kz_s[x] + g2))
            total = total + z_down(u * (kzd_s[x] - g2))
            return total, up_next

        first_u = u_s[lo]
        first_up = first_u * (kx_s[lo] + v0_s[lo] * (0.025 * first_u))
        lax.fori_loop(lo + 1, hi + 1, one_plane, (jnp.zeros((EY, NZ), f32), first_up), unroll=4)

    fit_hi = fit_hi_ref[...]
    fit_lo = fit_lo_ref[...]

    def fit_planes(group, carry):
        at = group * 8
        part = u_s[pl.ds(at + W, 8), 0:BY]
        adv_ref[pl.ds(at, 8)] = part
        flat = part.reshape(8 * BY, NZ)
        flat_hi = flat.astype(jnp.bfloat16)
        flat_lo = (flat - flat_hi.astype(f32)).astype(jnp.bfloat16)
        dot = functools.partial(jnp.dot, preferred_element_type=f32)
        out = dot(flat_hi, fit_hi) + (dot(flat_hi, fit_lo) + dot(flat_lo, fit_hi))
        zfit_ref[pl.ds(at, 8)] = out.reshape(8, BY, MZ)
        return carry

    lax.fori_loop(0, BX // 8, fit_planes, 0, unroll=2)


def time_steps(masks, field, diffusivity, velocity, halos, fit_hi, fit_lo):
    vmem = pl.BlockSpec(memory_space=pltpu.VMEM)
    return pl.pallas_call(
        stencil_body,
        out_shape=(
            jax.ShapeDtypeStruct((BX, BY, NZ), jnp.float32),
            jax.ShapeDtypeStruct((BX, BY, MZ), jnp.float32),
        ),
        in_specs=[pl.BlockSpec(memory_space=pltpu.SMEM)] + [vmem] * 13,
        out_specs=(vmem, vmem),
        scratch_shapes=[pltpu.VMEM((EX, EY, NZ), jnp.float32)] * 10,
        compiler_params=pltpu.CompilerParams(vmem_limit_bytes=60 * 1024 * 1024),
        name="time_steps",
    )(masks, field, diffusivity, velocity, *halos, fit_hi, fit_lo)


def ring(n, d):
    return [(i, (i + d) % n) for i in range(n)]


def shift(a, axis, d):
    return lax.ppermute(a, axis, ring(lax.axis_size(axis), d))


def shift_both(a, dx, dy):
    nx = lax.axis_size("px")
    ny = lax.axis_size("py")
    pairs = [(i * ny + j, ((i + dx) % nx) * ny + (j + dy) % ny) for i in range(nx) for j in range(ny)]
    return lax.ppermute(a, ("px", "py"), pairs)


def pack_body(margin_ref, f_ref, k_ref, v_ref, ylo_ref, yhi_ref, xlo_ref, xhi_ref, ll_ref, lh_ref, hl_ref, hh_ref):
    f32 = jnp.float32
    bf16 = jnp.bfloat16
    step = pl.program_id(0)
    t = BY - W

    def rest(u):
        return u - u.astype(bf16).astype(f32)

    for g in range(PACK // 4):
        tails, heads = [], []
        for i in range(4):
            x = 4 * g + i
            u = f_ref[x]
            tails.append(u[t:])
            heads.append(u[:W])
            ur_t = rest(u[t - 4 :])
            ur_h = rest(u[:8])
            k, v0, v1, v2 = [r.astype(f32) for r in (k_ref[x], v_ref[0, x], v_ref[1, x], v_ref[2, x])]
            ylo_ref[g, i] = jnp.concatenate(
                [k[t:], ur_t[7:8], v0[t + 1 :], v1[t:], ur_t[6:7], v2[t + 1 :]], axis=0
            ).astype(bf16)
            yhi_ref[g, i] = jnp.concatenate(
                [k[:W], v0[: W - 1], ur_h[0:1], v1[:W], v2[: W - 1], ur_h[1:2]], axis=0
            ).astype(bf16)
        ylo_ref[g, 4] = jnp.concatenate(tails, axis=0).astype(bf16)
        yhi_ref[g, 4] = jnp.concatenate(heads, axis=0).astype(bf16)

    def x_side(at, out, near, outer, low, high):
        for i in range(W):
            out[i] = f_ref[at + i].astype(bf16)
            out[W + i] = k_ref[at + i]
            out[2 * W + i] = v_ref[0, at + i]
            if i == outer:
                out[3 * W + i] = rest(f_ref[at + near[0]]).astype(bf16)
                out[4 * W + i] = rest(f_ref[at + near[1]]).astype(bf16)
            else:
                out[3 * W + i] = v_ref[1, at + i]
                out[4 * W + i] = v_ref[2, at + i]
        half = jnp.zeros((16, NZ), f32)
        out[5 * W] = jnp.concatenate([half + margin_ref[0, 0].astype(f32), half + margin_ref[0, 1].astype(f32)], axis=0).astype(bf16)
        for n in range(5):
            planes = [
                (f_ref[at + i] if n == 0 else k_ref[at + i] if n == 1 else v_ref[n - 2, at + i]).astype(f32)
                for i in range(W)
            ]
            low[n] = jnp.concatenate([a[t:] for a in planes], axis=0).astype(bf16)
            high[n] = jnp.concatenate([a[:W] for a in planes], axis=0).astype(bf16)

    @pl.when(step == 0)
    def _():
        x_side(0, xhi_ref, (0, 1), W - 1, hl_ref, hh_ref)

    @pl.when(step == BX // PACK - 1)
    def _():
        x_side(PACK - W, xlo_ref, (W - 1, W - 2), 0, ll_ref, lh_ref)


PACK = 16


def halo_parts(field, diffusivity, velocity, margin):
    bf16 = jnp.bfloat16
    y_shape = (BX // 4, 5, 16, NZ)
    y_spec = pl.BlockSpec((PACK // 4, 5, 16, NZ), lambda g: (g, 0, 0, 0))
    x_shape = (5 * W + 1, BY, NZ)
    x_spec = pl.BlockSpec(x_shape, lambda g: (0, 0, 0))
    c_shape = (5, 16, NZ)
    c_spec = pl.BlockSpec(c_shape, lambda g: (0, 0, 0))
    planes = pl.BlockSpec((PACK, BY, NZ), lambda g: (g, 0, 0))
    ylo, yhi, xlo, xhi, ll, lh, hl, hh = pl.pallas_call(
        pack_body,
        grid=(BX // PACK,),
        out_shape=[jax.ShapeDtypeStruct(s, bf16) for s in [y_shape] * 2 + [x_shape] * 2 + [c_shape] * 4],
        in_specs=[
            pl.BlockSpec(memory_space=pltpu.SMEM),
            planes,
            planes,
            pl.BlockSpec((3, PACK, BY, NZ), lambda g: (0, g, 0, 0)),
        ],
        out_specs=[y_spec] * 2 + [x_spec] * 2 + [c_spec] * 4,
        compiler_params=pltpu.CompilerParams(vmem_limit_bytes=40 * 1024 * 1024),
        name="pack_faces",
    )(margin, field, diffusivity, velocity)
    return (
        shift(ylo, "py", 1),
        shift(yhi, "py", -1),
        shift(xlo, "px", 1),
        shift(xhi, "px", -1),
        shift_both(ll, 1, 1),
        shift_both(lh, 1, -1),
        shift_both(hl, -1, 1),
        shift_both(hh, -1, -1),
    )


def mm(a, b):
    return jnp.dot(a, b, precision=HIGH, preferred_element_type=jnp.float32)


def table_row(table, margins, owner, count):
    own = jnp.clip(owner, 0, count - 1)
    cls = jnp.where(own == 0, 0, jnp.where(own == count - 1, 2, 1))
    n = OVMAX + 1
    m = jnp.clip(margins, 0, OVMAX)
    return lax.dynamic_index_in_dim(jnp.asarray(table), (cls * n + m[0]) * n + m[1], 0, keepdims=False)


def x_operator(margin, low_margin, high_margin, tables, p, count):
    base, send, near = tables
    own = table_row(base, margin, p, count)
    pad = jnp.pad(own, ((0, 0), (0, 12)))
    as_low = table_row(near, low_margin, p - 1, count)[0]
    as_high = table_row(near, high_margin, p + 1, count)[1]
    return pad + mm(own[:, BX + 6 : BX + 13], as_low) + mm(own[:, BX + 19 : BX + 26], as_high)


def per_device(field, diffusivity, velocity, margin):
    count_x = lax.axis_size("px")
    count_y = lax.axis_size("py")
    p = lax.axis_index("px")
    q = lax.axis_index("py")
    masks = jnp.stack([p > 0, p < count_x - 1, q > 0, q < count_y - 1]).astype(jnp.float32)
    s_z = fit_matrix(NZ).T.astype(np.float32)
    fit_hi = s_z.astype(jnp.bfloat16)
    fit_lo = (s_z - fit_hi.astype(np.float32)).astype(jnp.bfloat16)
    halos = halo_parts(field, diffusivity, velocity, margin)
    tables = x_tables(count_x)
    send = table_row(tables[1], margin[0], p, count_x)
    low_margin, high_margin = [h[5 * W, 0:32:16, 0].astype(jnp.int32) for h in (halos[2], halos[3])]
    full = x_operator(margin[0], low_margin, high_margin, tables, p, count_x)
    diag, up, down, couple = [
        lax.dynamic_index_in_dim(jnp.asarray(t), q, 0, keepdims=False) for t in y_tables(count_y)
    ]
    advected, zfit = time_steps(masks, field, diffusivity, velocity, halos, jnp.asarray(fit_hi), jnp.asarray(fit_lo))

    lines = zfit.reshape(BX, BY * MZ)
    out = mm(send, lines)
    from_low = shift(out[:13], "px", 1)
    from_high = shift(out[13:], "px", -1)
    from_low2 = shift(out[:6].astype(jnp.bfloat16), "px", 2)
    from_high2 = shift(out[13:19].astype(jnp.bfloat16), "px", -2)
    stacked = jnp.concatenate(
        [lines, from_low, from_high, from_low2.astype(jnp.float32), from_high2.astype(jnp.float32)], axis=0
    )
    xfit = mm(full, stacked).reshape(BX // 2, BY, MZ)

    both = jnp.einsum("cy,xyz->cxz", jnp.concatenate([up, down], axis=0), xfit, precision=HIGH)
    head = lax.reduce_precision(both, 8, 7)
    rest = both - head
    target = jnp.arange(count_y)[:, None, None, None]
    carries = jnp.where(
        target > q,
        jnp.concatenate([head[:3], rest[:1]], axis=0)[None],
        jnp.concatenate([head[3:], rest[3:4]], axis=0)[None],
    ).astype(jnp.bfloat16)
    got = lax.all_to_all(carries, "py", split_axis=0, concat_axis=0, tiled=True)
    controls = jnp.einsum("my,xyz->xmz", diag, xfit, precision=HIGH)
    controls = controls + jnp.einsum(
        "mc,cxz->xmz", couple, got.astype(jnp.float32).reshape(count_y * 4, BX // 2, MZ), precision=HIGH
    )
    return advected, controls


def solution(mesh):
    placed = (P("px", "py", None), P("px", "py", None), P(None, "px", "py", None), P("px", None))
    return jax.shard_map(
        per_device,
        mesh=mesh,
        in_specs=placed,
        out_specs=(P("px", "py", None), P("px", "py", None)),
        check_vma=False,
    )
```

```python
import functools

import jax
import jax.numpy as jnp
import numpy as np
from jax import lax
from jax.experimental import pallas as pl
from jax.experimental.pallas import tpu as pltpu
from jax.sharding import PartitionSpec as P

STEPS = 4
OVMAX = 4
BX = 64
BY = 32
NZ = 256
MZ = 128
W = 4
EX = BX + 2 * W
EY = BY + 2 * W
HIGH = lax.Precision.HIGHEST


def bspline(t):
    m = np.abs(t)
    inner = (4.0 - 6.0 * m * m + 3.0 * m**3) / 6.0
    outer = np.maximum(2.0 - m, 0.0) ** 3 / 6.0
    return np.where(m < 1.0, inner, outer)


def basis(n):
    j = np.arange(n)[:, None]
    k = np.arange(n // 2)[None, :]
    return bspline((j - 2.0 * k - 0.5) / 2.0)


def fit_matrix(n):
    b = basis(n)
    return np.linalg.solve(b.T @ b, b.T)


def y_tables(count):
    total = count * BY
    s = fit_matrix(total)
    own = BY // 2
    diag = np.zeros((count, own, BY))
    up = np.zeros((count, 3, BY))
    down = np.zeros((count, 3, BY))
    couple = np.zeros((count, own, count, 3))
    for q in range(count):
        cols = s[:, q * BY : (q + 1) * BY]
        diag[q] = cols[q * own : (q + 1) * own]
        if q < count - 1:
            below = cols[(q + 1) * own :]
            u, sv, vt = np.linalg.svd(below, full_matrices=False)
            assert sv[3] < 1e-10 * sv[0]
            up[q] = vt[:3]
            left = u[:, :3] * sv[:3]
            for t in range(q + 1, count):
                couple[t, :, q] = left[(t - q - 1) * own : (t - q) * own]
        if q > 0:
            above = cols[: q * own]
            u, sv, vt = np.linalg.svd(above, full_matrices=False)
            assert sv[3] < 1e-10 * sv[0]
            down[q] = vt[:3]
            left = u[:, :3] * sv[:3]
            for t in range(q):
                couple[t, :, q] = left[t * own : (t + 1) * own]
    return [a.astype(np.float32) for a in (diag, up, down, np.concatenate([couple, couple[..., :1]], axis=3).reshape(count, own, count * 4))]


def x_tables(count):
    total = count * BX
    block = BX // 2
    ctrl = total // 2
    b = basis(total)
    width = block + 2 * OVMAX
    gpad = np.zeros((ctrl + 16, ctrl + 16))
    gpad[8:-8, 8:-8] = b.T @ b
    bt = bspline((np.arange(BX)[None] - 2.0 * (np.arange(block + 4)[:, None] - 2) - 0.5) / 2.0)
    base, send, near = [], [], []
    for cls, p in enumerate((0, 1, count - 1)):
        has_low = float(cls != 0)
        has_high = float(cls != 2)
        start = p * block
        knots = start - OVMAX + np.arange(width)
        lo = start - OVMAX + 8
        full = gpad[lo : lo + width, lo : lo + width]
        band = gpad[lo : lo + width, lo - 3 : lo + width + 3]
        for m0 in range(OVMAX + 1):
            for m1 in range(OVMAX + 1):
                inside = (knots >= start - m0) & (knots < start + block + m1) & (knots >= 0) & (knots < ctrl)
                w = inside.astype(np.float64)
                mat = full * w[:, None] * w[None, :] + np.diag(1.0 - w)
                e = (np.linalg.inv(mat) * w[None, :])[OVMAX : OVMAX + block]
                q = e @ band
                ql = q[:, :7] * has_low
                qr = q[:, 7 + block :] * has_high
                two = 2.0 * e - q[:, 7 : 7 + block] @ e
                low = two[:, 0:6] * has_low
                high = two[:, block + 2 :] * has_high
                base.append(np.concatenate([two[:, 2 : block + 6] @ bt, low, -ql, high, -qr], axis=1))
                send.append(
                    np.concatenate(
                        [bt[block - 2 :], e[block - 7 :, 2 : block + 6] @ bt, bt[:6], e[:7, 2 : block + 6] @ bt]
                    )
                )
                zero = np.zeros((7, 6))
                as_low = np.concatenate(
                    [e[block - 7 :, block + 2 :] @ bt[0:6], np.zeros((7, 26)), e[block - 7 :, 0:6] * has_low, zero], axis=1
                )
                as_high = np.concatenate(
                    [e[:7, 0:6] @ bt[block - 2 :], np.zeros((7, 26)), zero, e[:7, block + 2 :] * has_high], axis=1
                )
                near.append(np.stack([as_low, as_high]))
    return [np.stack(t).astype(np.float32) for t in (base, send, near)]


def stencil_body(mask_ref, f_ref, k_ref, v_ref, yl_ref, yh_ref, xl_ref, xh_ref, cl_ref, ch_ref, send_ref,
                 fit_hi_ref, fit_lo_ref, adv_ref, zfit_ref, out_ref, u_s, v0_s, v1_s, v2_s, kx_s, ky_s, kyd_s, kz_s, kzd_s, c_s):
    f32 = jnp.float32
    from_low_x = mask_ref[0]
    from_high_x = mask_ref[1]
    from_low_y = mask_ref[2]
    from_high_y = mask_ref[3]
    dest = (u_s, c_s, v0_s, v1_s, v2_s)

    def own_planes(group, carry):
        at = group * 4
        ul = yl_ref[group, 4].astype(f32) * from_low_y
        uh = yh_ref[group, 4].astype(f32) * from_high_y
        gap = jnp.zeros((4, NZ), f32)
        for i in range(4):
            x = at + i
            kl = yl_ref[group, i].astype(f32) * from_low_y
            kh = yh_ref[group, i].astype(f32) * from_high_y
            u_s[x + W, 0:BY] = f_ref[x]
            rest = jnp.concatenate([kh[7:8], kh[15:16], gap, kl[12:13], kl[4:5]], axis=0)
            u_s[x + W, BY:EY] = rest + jnp.concatenate([uh[4 * i : 4 * i + 4], ul[4 * i : 4 * i + 4]], axis=0)
            for n in range(4):
                ref = dest[1 + n]
                ref[x + W, 0:BY] = (k_ref[x] if n == 0 else v_ref[n - 1, x]).astype(f32)
                ref[x + W, BY:EY] = jnp.concatenate([kh[4 * n : 4 * n + 4], kl[4 * n : 4 * n + 4]], axis=0)
        return carry

    lax.fori_loop(0, BX // 4, own_planes, 0)
    for n in range(5):
        for base, ref, corner, scale, near, outer in (
            (0, xl_ref, 0, from_low_x, (W - 1, W - 2), 0),
            (BX + W, xh_ref, 5, from_high_x, (0, 1), W - 1),
        ):
            low = cl_ref[corner + n].astype(f32) * (scale * from_low_y)
            high = ch_ref[corner + n].astype(f32) * (scale * from_high_y)
            for i in range(W):
                value = ref[n * W + i].astype(f32)
                if n == 0 and i in near:
                    value = value + ref[(3 + near.index(i)) * W + outer].astype(f32)
                dest[n][base + i, 0:BY] = value * scale
                dest[n][base + i, BY:EY] = jnp.concatenate([high[4 * i : 4 * i + 4], low[4 * i : 4 * i + 4]], axis=0)

    lane = lax.broadcasted_iota(jnp.int32, (EY, 128), 1)
    first = lane == 0
    final = lane == 127

    def z_up(a):
        lo = pltpu.roll(a[:, :128], 1, 1)
        hi = pltpu.roll(a[:, 128:], 1, 1)
        return jnp.concatenate([jnp.where(first, 0.0, lo), jnp.where(first, lo, hi)], axis=1)

    def z_down(a):
        lo = pltpu.roll(a[:, :128], 127, 1)
        hi = pltpu.roll(a[:, 128:], 127, 1)
        return jnp.concatenate([jnp.where(final, hi, lo), jnp.where(final, 0.0, hi)], axis=1)

    def coefficients(x, carry):
        k, kx_low = carry
        k_next = c_s[jnp.minimum(x + 1, EX - 1)]
        kx = 0.05 * (k + k_next)
        ky = 0.05 * (k + pltpu.roll(k, EY - 1, 0))
        kyd = pltpu.roll(ky, 1, 0)
        kz = 0.05 * (k + z_down(k))
        kzd = 0.05 * (k + z_up(k))
        kx_s[x] = kx
        ky_s[x] = ky
        kyd_s[x] = kyd
        kz_s[x] = kz
        kzd_s[x] = kzd
        c_s[x] = 1.0 - ((kx + kx_low) + (ky + kyd) + (kz + kzd))
        return k_next, kx

    lax.fori_loop(0, EX, coefficients, (c_s[0], jnp.zeros((EY, NZ), f32)), unroll=4)

    row = lax.broadcasted_iota(jnp.int32, (EY, NZ), 0)
    row_mask = jnp.where(row < BY, 1.0, jnp.where(row < BY + W, from_high_y, from_low_y))

    for step in range(STEPS):
        lo = step
        hi = EX - 1 - step

        def one_plane(x, carry, step=step):
            partial, up = carry
            u = u_s[x]
            w = 0.025 * u
            g0 = v0_s[x] * w
            g1 = v1_s[x] * w
            g2 = v2_s[x] * w
            done = partial + u * (kx_s[x - 1] - g0)
            prev = x - 1
            plane_mask = jnp.where(prev < W, from_low_x, jnp.where(prev >= BX + W, from_high_x, 1.0))
            u_s[prev] = done * (row_mask * plane_mask)
            up_next = u * (kx_s[x] + g0)
            total = u * c_s[x] + up
            total = total + pltpu.roll(u * (ky_s[x] + g1), 1, 0)
            total = total + pltpu.roll(u * (kyd_s[x] - g1), EY - 1, 0)
            total = total + z_up(u * (kz_s[x] + g2))
            total = total + z_down(u * (kzd_s[x] - g2))
            return total, up_next

        first_u = u_s[lo]
        first_up = first_u * (kx_s[lo] + v0_s[lo] * (0.025 * first_u))
        lax.fori_loop(lo + 1, hi + 1, one_plane, (jnp.zeros((EY, NZ), f32), first_up), unroll=4)

    fit_hi = fit_hi_ref[...]
    fit_lo = fit_lo_ref[...]

    def fit_planes(group, carry):
        at = group * 8
        part = u_s[pl.ds(at + W, 8), 0:BY]
        adv_ref[pl.ds(at, 8)] = part
        flat = part.reshape(8 * BY, NZ)
        flat_hi = flat.astype(jnp.bfloat16)
        flat_lo = (flat - flat_hi.astype(f32)).astype(jnp.bfloat16)
        dot = functools.partial(jnp.dot, preferred_element_type=f32)
        out = dot(flat_hi, fit_hi) + (dot(flat_hi, fit_lo) + dot(flat_lo, fit_hi))
        zfit_ref[pl.ds(at, 8)] = out.reshape(8, BY, MZ)
        return carry

    lax.fori_loop(0, BX // 8, fit_planes, 0, unroll=2)

    half = OUT // 2
    for base, cells in ((0, range(BX - 11, BX)), (half, range(11))):
        rows = [jnp.zeros((BY, MZ), f32)] * 6
        for x in cells:
            plane = zfit_ref[x]
            rows = [a + send_ref[base + r, x] * plane for r, a in enumerate(rows)]
        for r in range(6):
            out_ref[base + r] = rows[r]

        def sweep(x, rows, base=base):
            plane = zfit_ref[x]
            return tuple(a + send_ref[base + 6 + r, x] * plane for r, a in enumerate(rows))

        rows = lax.fori_loop(0, BX, sweep, (jnp.zeros((BY, MZ), f32),) * 7, unroll=8)
        for r in range(7):
            out_ref[base + 6 + r] = rows[r]


OUT = 26


def time_steps(masks, field, diffusivity, velocity, halos, send, fit_hi, fit_lo):
    vmem = pl.BlockSpec(memory_space=pltpu.VMEM)
    smem = pl.BlockSpec(memory_space=pltpu.SMEM)
    return pl.pallas_call(
        stencil_body,
        out_shape=(
            jax.ShapeDtypeStruct((BX, BY, NZ), jnp.float32),
            jax.ShapeDtypeStruct((BX, BY, MZ), jnp.float32),
            jax.ShapeDtypeStruct((OUT, BY, MZ), jnp.float32),
        ),
        in_specs=[smem] + [vmem] * 9 + [smem] + [vmem] * 2,
        out_specs=(vmem, vmem, vmem),
        scratch_shapes=[pltpu.VMEM((EX, EY, NZ), jnp.float32)] * 10,
        compiler_params=pltpu.CompilerParams(vmem_limit_bytes=STEP_VMEM * 1024 * 1024),
        name="time_steps",
    )(masks, field, diffusivity, velocity, *halos, send, fit_hi, fit_lo)


def ring(n, d):
    return [(i, (i + d) % n) for i in range(n)]


def shift(a, axis, d):
    return lax.ppermute(a, axis, ring(lax.axis_size(axis), d))


def pack_body(margin_ref, f_hbm, k_hbm, v_hbm, ylo_ref, yhi_ref, xlo_ref, xhi_ref, f_ref, k_ref, v_ref, sems):
    f32 = jnp.float32
    bf16 = jnp.bfloat16
    t = BY - W
    copies = []
    for c in range(BX // PACK):
        part = pl.ds(c * PACK, PACK)
        copies.append(
            [
                pltpu.make_async_copy(f_hbm.at[part], f_ref.at[part], sems.at[0, c]),
                pltpu.make_async_copy(k_hbm.at[part], k_ref.at[part], sems.at[1, c]),
                pltpu.make_async_copy(v_hbm.at[:, part], v_ref.at[:, part], sems.at[2, c]),
            ]
        )
        for copy in copies[-1]:
            copy.start()

    def rest(u):
        return u - u.astype(bf16).astype(f32)

    def faces(g, carry):
        tails, heads = [], []
        for i in range(4):
            x = 4 * g + i
            u = f_ref[x]
            tails.append(u[t:])
            heads.append(u[:W])
            ur_t = rest(u[t - 4 :])
            ur_h = rest(u[:8])
            k, v0, v1, v2 = [r.astype(f32) for r in (k_ref[x], v_ref[0, x], v_ref[1, x], v_ref[2, x])]
            ylo_ref[g, i] = jnp.concatenate(
                [k[t:], ur_t[7:8], v0[t + 1 :], v1[t:], ur_t[6:7], v2[t + 1 :]], axis=0
            ).astype(bf16)
            yhi_ref[g, i] = jnp.concatenate(
                [k[:W], v0[: W - 1], ur_h[0:1], v1[:W], v2[: W - 1], ur_h[1:2]], axis=0
            ).astype(bf16)
        ylo_ref[g, 4] = jnp.concatenate(tails, axis=0).astype(bf16)
        yhi_ref[g, 4] = jnp.concatenate(heads, axis=0).astype(bf16)
        return carry

    def x_side(at, out, near, outer):
        for i in range(W):
            out[i] = f_ref[at + i].astype(bf16)
            out[W + i] = k_ref[at + i]
            out[2 * W + i] = v_ref[0, at + i]
            if i == outer:
                out[3 * W + i] = rest(f_ref[at + near[0]]).astype(bf16)
                out[4 * W + i] = rest(f_ref[at + near[1]]).astype(bf16)
            else:
                out[3 * W + i] = v_ref[1, at + i]
                out[4 * W + i] = v_ref[2, at + i]
        half = jnp.zeros((16, NZ), f32)
        out[5 * W] = jnp.concatenate([half + margin_ref[0, 0].astype(f32), half + margin_ref[0, 1].astype(f32)], axis=0).astype(bf16)

    for c in range(BX // PACK):
        for copy in copies[c]:
            copy.wait()
        lax.fori_loop(c * PACK // 4, (c + 1) * PACK // 4, faces, 0)
        if c == 0:
            x_side(0, xhi_ref, (0, 1), W - 1)
    x_side(BX - W, xlo_ref, (W - 1, W - 2), 0)


def corner_body(xl_ref, xh_ref, up_ref, down_ref):
    f32 = jnp.float32
    for side, ref in enumerate((xl_ref, xh_ref)):
        for n in range(5):
            planes = [ref[n * W + i].astype(f32) for i in range(W)]
            up_ref[side * 5 + n] = jnp.concatenate([a[BY - W :] for a in planes], axis=0).astype(jnp.bfloat16)
            down_ref[side * 5 + n] = jnp.concatenate([a[:W] for a in planes], axis=0).astype(jnp.bfloat16)


PACK = 16
PACK_VMEM = 61
STEP_VMEM = 48


def halo_parts(field, diffusivity, velocity, margin):
    bf16 = jnp.bfloat16
    y_shape = (BX // 4, 5, 16, NZ)
    x_shape = (5 * W + 1, BY, NZ)
    c_shape = (10, 16, NZ)
    vmem = pl.BlockSpec(memory_space=pltpu.VMEM)
    hbm = pl.BlockSpec(memory_space=pltpu.HBM)
    ylo, yhi, xlo, xhi = pl.pallas_call(
        pack_body,
        out_shape=[jax.ShapeDtypeStruct(s, bf16) for s in [y_shape] * 2 + [x_shape] * 2],
        in_specs=[pl.BlockSpec(memory_space=pltpu.SMEM), hbm, hbm, hbm],
        out_specs=[vmem] * 4,
        scratch_shapes=[
            pltpu.VMEM((BX, BY, NZ), jnp.float32),
            pltpu.VMEM((BX, BY, NZ), bf16),
            pltpu.VMEM((3, BX, BY, NZ), bf16),
            pltpu.SemaphoreType.DMA((3, BX // PACK)),
        ],
        compiler_params=pltpu.CompilerParams(vmem_limit_bytes=PACK_VMEM * 1024 * 1024),
        name="pack_faces",
    )(margin, field, diffusivity, velocity)
    xl = shift(xlo, "px", 1)
    xh = shift(xhi, "px", -1)
    yl = shift(ylo, "py", 1)
    yh = shift(yhi, "py", -1)
    c_up, c_down = pl.pallas_call(
        corner_body,
        out_shape=[jax.ShapeDtypeStruct(c_shape, bf16)] * 2,
        in_specs=[vmem] * 2,
        out_specs=[vmem] * 2,
        compiler_params=pltpu.CompilerParams(vmem_limit_bytes=4 * 1024 * 1024),
        name="pack_corners",
    )(xl, xh)
    return yl, yh, xl, xh, shift(c_up, "py", 1), shift(c_down, "py", -1)


def mm(a, b):
    return jnp.dot(a, b, precision=HIGH, preferred_element_type=jnp.float32)


def table_row(table, margins, owner, count):
    own = jnp.clip(owner, 0, count - 1)
    cls = jnp.where(own == 0, 0, jnp.where(own == count - 1, 2, 1))
    n = OVMAX + 1
    m = jnp.clip(margins, 0, OVMAX)
    return lax.dynamic_index_in_dim(jnp.asarray(table), (cls * n + m[0]) * n + m[1], 0, keepdims=False)


def x_operator(margin, low_margin, high_margin, tables, p, count):
    base, send, near = tables
    own = table_row(base, margin, p, count)
    pad = jnp.pad(own, ((0, 0), (0, 12)))
    as_low = table_row(near, low_margin, p - 1, count)[0]
    as_high = table_row(near, high_margin, p + 1, count)[1]
    return pad + mm(own[:, BX + 6 : BX + 13], as_low) + mm(own[:, BX + 19 : BX + 26], as_high)


def per_device(field, diffusivity, velocity, margin):
    count_x = lax.axis_size("px")
    count_y = lax.axis_size("py")
    p = lax.axis_index("px")
    q = lax.axis_index("py")
    masks = jnp.stack([p > 0, p < count_x - 1, q > 0, q < count_y - 1]).astype(jnp.float32)
    s_z = fit_matrix(NZ).T.astype(np.float32)
    fit_hi = s_z.astype(jnp.bfloat16)
    fit_lo = (s_z - fit_hi.astype(np.float32)).astype(jnp.bfloat16)
    halos = halo_parts(field, diffusivity, velocity, margin)
    tables = x_tables(count_x)
    send = table_row(tables[1], margin[0], p, count_x)
    low_margin, high_margin = [h[5 * W, 0:32:16, 0].astype(jnp.int32) for h in (halos[2], halos[3])]
    full = x_operator(margin[0], low_margin, high_margin, tables, p, count_x)
    diag, up, down, couple = [
        lax.dynamic_index_in_dim(jnp.asarray(t), q, 0, keepdims=False) for t in y_tables(count_y)
    ]
    advected, zfit, out = time_steps(
        masks, field, diffusivity, velocity, halos, send, jnp.asarray(fit_hi), jnp.asarray(fit_lo)
    )

    from_low = shift(out[:13], "px", 1)
    from_high = shift(out[13:], "px", -1)
    from_low2 = shift(out[:6].astype(jnp.bfloat16), "px", 2)
    from_high2 = shift(out[13:19].astype(jnp.bfloat16), "px", -2)
    stacked = jnp.concatenate(
        [zfit, from_low, from_high, from_low2.astype(jnp.float32), from_high2.astype(jnp.float32)], axis=0
    )
    xfit = jnp.einsum("kx,xyz->kyz", full, stacked, precision=HIGH)

    both = jnp.einsum("cy,xyz->cxz", jnp.concatenate([up, down], axis=0), xfit, precision=HIGH)
    head = lax.reduce_precision(both, 8, 7)
    rest = both - head
    target = jnp.arange(count_y)[:, None, None, None]
    carries = jnp.where(
        target > q,
        jnp.concatenate([head[:3], rest[:1]], axis=0)[None],
        jnp.concatenate([head[3:], rest[3:4]], axis=0)[None],
    ).astype(jnp.bfloat16)
    got = lax.all_to_all(carries, "py", split_axis=0, concat_axis=0, tiled=True)
    controls = jnp.einsum("my,xyz->xmz", diag, xfit, precision=HIGH)
    controls = controls + jnp.einsum(
        "mc,cxz->xmz", couple, got.astype(jnp.float32).reshape(count_y * 4, BX // 2, MZ), precision=HIGH
    )
    return advected, controls


def solution(mesh):
    placed = (P("px", "py", None), P("px", "py", None), P(None, "px", "py", None), P("px", None))
    return jax.shard_map(
        per_device,
        mesh=mesh,
        in_specs=placed,
        out_specs=(P("px", "py", None), P("px", "py", None)),
        check_vma=False,
    )
```

```python
import functools

import jax
import jax.numpy as jnp
import numpy as np
from jax import lax
from jax.experimental import pallas as pl
from jax.experimental.pallas import tpu as pltpu
from jax.sharding import PartitionSpec as P

STEPS = 4
OVMAX = 4
BX = 64
BY = 32
NZ = 256
MZ = 128
W = 4
EX = BX + 2 * W
EY = BY + 2 * W
YR = BY // 2 + 6
LINES = YR * 128


PACK = 16
PACK_VMEM = 12
STEP_VMEM = 16


def bspline(t):
    m = np.abs(t)
    inner = (4.0 - 6.0 * m * m + 3.0 * m**3) / 6.0
    outer = np.maximum(2.0 - m, 0.0) ** 3 / 6.0
    return np.where(m < 1.0, inner, outer)


def basis(n):
    j = np.arange(n)[:, None]
    k = np.arange(n // 2)[None, :]
    return bspline((j - 2.0 * k - 0.5) / 2.0)


def fit_matrix(n):
    b = basis(n)
    return np.linalg.solve(b.T @ b, b.T)


def split(a):
    a = a.astype(np.float32)
    hi = a.astype(jnp.bfloat16)
    return hi, (a - hi.astype(np.float32)).astype(jnp.bfloat16)


def y_tables(count):
    total = count * BY
    s = fit_matrix(total)
    own = BY // 2
    rows = np.zeros((count, YR, BY))
    couple = np.zeros((count, own, count, 4))
    for q in range(count):
        cols = s[:, q * BY : (q + 1) * BY]
        rows[q, :own] = cols[q * own : (q + 1) * own]
        for at, far, targets in ((own, cols[(q + 1) * own :], range(q + 1, count)), (own + 3, cols[: q * own], range(q))):
            if len(targets) == 0:
                continue
            u, sv, vt = np.linalg.svd(far, full_matrices=False)
            assert sv[3] < 1e-10 * sv[0]
            rows[q, at : at + 3] = vt[:3]
            left = (u[:, :3] * sv[:3]).reshape(len(targets), own, 3)
            for i, t in enumerate(targets):
                couple[t, :, q, :3] = left[i]
                couple[t, :, q, 3] = left[i, :, 0]
    table = np.einsum("qry,xw->qrxwy", rows, np.eye(8)).reshape(count, YR * 8, 8 * BY)
    return np.stack(split(table), axis=1), couple.reshape(count, own, count * 4).astype(np.float32)


def x_tables(count):
    total = count * BX
    block = BX // 2
    ctrl = total // 2
    b = basis(total)
    width = block + 2 * OVMAX
    gpad = np.zeros((ctrl + 16, ctrl + 16))
    gpad[8:-8, 8:-8] = b.T @ b
    bt = bspline((np.arange(BX)[None] - 2.0 * (np.arange(block + 4)[:, None] - 2) - 0.5) / 2.0)
    base, send, near = [], [], []
    for cls, p in enumerate((0, 1, count - 1)):
        has_low = float(cls != 0)
        has_high = float(cls != 2)
        start = p * block
        knots = start - OVMAX + np.arange(width)
        lo = start - OVMAX + 8
        full = gpad[lo : lo + width, lo : lo + width]
        band = gpad[lo : lo + width, lo - 3 : lo + width + 3]
        for m0 in range(OVMAX + 1):
            for m1 in range(OVMAX + 1):
                inside = (knots >= start - m0) & (knots < start + block + m1) & (knots >= 0) & (knots < ctrl)
                w = inside.astype(np.float64)
                mat = full * w[:, None] * w[None, :] + np.diag(1.0 - w)
                e = (np.linalg.inv(mat) * w[None, :])[OVMAX : OVMAX + block]
                q = e @ band
                ql = q[:, :7] * has_low
                qr = q[:, 7 + block :] * has_high
                two = 2.0 * e - q[:, 7 : 7 + block] @ e
                low = two[:, 0:6] * has_low
                high = two[:, block + 2 :] * has_high
                gap3 = np.zeros((block, 3))
                gap32 = np.zeros((block, 32))
                base.append(np.concatenate([two[:, 2 : block + 6] @ bt, low, -ql, gap3, high, -qr, gap3, gap32], axis=1))
                pad = np.zeros((3, BX))
                send.append(
                    np.concatenate(
                        [bt[block - 2 :], e[block - 7 :, 2 : block + 6] @ bt, pad, bt[:6], e[:7, 2 : block + 6] @ bt, pad]
                    )
                )
                both = np.zeros((2, 8, 128))
                both[0, :7, :BX] = e[block - 7 :, block + 2 :] @ bt[0:6]
                both[0, :7, 96:102] = e[block - 7 :, 0:6] * has_low
                both[1, :7, :BX] = e[:7, 0:6] @ bt[block - 2 :]
                both[1, :7, 112:118] = e[:7, block + 2 :] * has_high
                near.append(both)
    return [np.stack(t).astype(np.float32) for t in (base, send, near)]


def z_shifts(rows):
    lane = lax.broadcasted_iota(jnp.int32, (rows, 128), 1)
    first = lane == 0
    final = lane == 127

    def z_up(a):
        lo = pltpu.roll(a[:, :128], 1, 1)
        hi = pltpu.roll(a[:, 128:], 1, 1)
        return jnp.concatenate([jnp.where(first, 0.0, lo), jnp.where(first, lo, hi)], axis=1)

    def z_down(a):
        lo = pltpu.roll(a[:, :128], 127, 1)
        hi = pltpu.roll(a[:, 128:], 127, 1)
        return jnp.concatenate([jnp.where(final, hi, lo), jnp.where(final, 0.0, hi)], axis=1)

    return z_up, z_down


def own_rows(k, kx_low, kx, refs, x):
    kx_s, ky_s, kyd_s, kz_s, kzd_s, c_s = refs
    z_up, z_down = z_shifts(BY)
    row = lax.broadcasted_iota(jnp.int32, (BY, NZ), 0)
    own = slice(0, BY)
    ky = jnp.where(row < BY - 1, 0.05 * (k + pltpu.roll(k, BY - 1, 0)), 0.0)
    kyd = pltpu.roll(ky, 1, 0)
    kz = 0.05 * (k + z_down(k))
    kzd = 0.05 * (k + z_up(k))
    kx_s[x, own] = kx
    ky_s[x, own] = ky
    kyd_s[x, own] = kyd
    kz_s[x, own] = kz
    kzd_s[x, own] = kzd
    c_s[x, own] = 1.0 - ((kx + kx_low) + (ky + kyd) + (kz + kzd))


def load(sources, targets, sems):
    copies = []
    for c in range(BX // PACK):
        part = pl.ds(c * PACK, PACK)
        copies.append([])
        for n, (src, dst) in enumerate(zip(sources, targets)):
            at = (slice(None), part) if len(src.shape) == 4 else (part,)
            copies[-1].append(pltpu.make_async_copy(src.at[at], dst.at[at], sems.at[n, c]))
            copies[-1][-1].start()
    return copies


def own_body(f_hbm, k_hbm, v_hbm, after_ref, u_s, v0_s, v1_s, v2_s, kx_s, ky_s, kyd_s, kz_s, kzd_s, c_s, edge_s, end_ref,
             f_ref, k_ref, v_ref, sems):
    f32 = jnp.float32
    for part in load((f_hbm, k_hbm, v_hbm), (f_ref, k_ref, v_ref), sems):
        for copy in part:
            copy.wait()
    refs = (kx_s, ky_s, kyd_s, kz_s, kzd_s, c_s)

    def plane(x, carry):
        k, kx_low = carry
        k_next = k_ref[jnp.minimum(x + 1, BX - 1)].astype(f32)
        kx = jnp.where(x < BX - 1, 0.05, 0.0) * (k + k_next)
        u_s[x + W, 0:BY] = f_ref[x]
        for n, ref in enumerate((v0_s, v1_s, v2_s)):
            ref[x + W, 0:BY] = v_ref[n, x].astype(f32)
        edge_s[x + W, 0:8] = k[0:8]
        edge_s[x + W, 8:16] = k[BY - 8 :]
        own_rows(k, kx_low, kx, refs, x + W)
        return k_next, kx

    lax.fori_loop(0, BX, plane, (k_ref[0].astype(f32), jnp.zeros((BY, NZ), f32)), unroll=4)
    end_ref[0] = k_ref[0].astype(f32)
    end_ref[1] = k_ref[BX - 1].astype(f32)


def dot3(a, b):
    dot = functools.partial(jnp.dot, preferred_element_type=jnp.float32)
    return dot(a[0], b[0]) + (dot(a[0], b[1]) + dot(a[1], b[0]))


def halves(a):
    hi = a.astype(jnp.bfloat16)
    return hi, (a - hi.astype(jnp.float32)).astype(jnp.bfloat16)


def place_of(owner, count, m0, m1):
    own = jnp.clip(owner, 0, count - 1)
    cls = jnp.where(own == 0, 0, jnp.where(own == count - 1, 2, 1))
    n = OVMAX + 1
    return (cls * n + jnp.clip(m0, 0, OVMAX)) * n + jnp.clip(m1, 0, OVMAX)


def stencil_body(count_x, count_y, margin_ref, yl_ref, yh_ref, xl_ref, xh_ref, cl_ref, ch_ref, fit_ref, base_hbm, send_hbm,
                 near_hbm, ytab_hbm, end_ref, *rest_refs):
    f32 = jnp.float32
    outs = rest_refs[KEPT:]
    adv_ref, zt_ref, lo_ref, hi_ref, lo2_ref, hi2_ref, full_ref = outs[:7]
    u_s, v0_s, v1_s, v2_s, kx_s, ky_s, kyd_s, kz_s, kzd_s, c_s, edge_s = outs[7 : 7 + KEPT]
    kh_s, kp_s, base_s, send_s, near_s, ytab_s, sems = outs[7 + KEPT :]
    p = lax.axis_index("px")
    q = lax.axis_index("py")

    def margins(ref):
        part = ref[5 * W].astype(f32)
        return [jnp.max(a).astype(jnp.int32) for a in (part[0:8], part[16:24])]

    mine = place_of(p, count_x, margin_ref[0, 0], margin_ref[0, 1])
    low = place_of(p - 1, count_x, *margins(xl_ref))
    high = place_of(p + 1, count_x, *margins(xh_ref))
    copies = [
        pltpu.make_async_copy(base_hbm.at[mine], base_s, sems.at[0]),
        pltpu.make_async_copy(send_hbm.at[mine], send_s, sems.at[1]),
        pltpu.make_async_copy(near_hbm.at[low, 0], near_s.at[0], sems.at[2]),
        pltpu.make_async_copy(near_hbm.at[high, 1], near_s.at[1], sems.at[3]),
        pltpu.make_async_copy(ytab_hbm.at[q], ytab_s, sems.at[4]),
    ]
    for copy in copies:
        copy.start()
    refs = (kx_s, ky_s, kyd_s, kz_s, kzd_s, c_s)
    from_low_x = jnp.where(p > 0, 1.0, 0.0)
    from_high_x = jnp.where(p < count_x - 1, 1.0, 0.0)
    from_low_y = jnp.where(q > 0, 1.0, 0.0)
    from_high_y = jnp.where(q < count_y - 1, 1.0, 0.0)
    beyond = slice(BY, EY)

    def halo_rows(group, carry):
        at = group * 4
        ul = yl_ref[group, 4].astype(f32) * from_low_y
        uh = yh_ref[group, 4].astype(f32) * from_high_y
        gap = jnp.zeros((4, NZ), f32)
        for i in range(4):
            x = at + i + W
            kl = yl_ref[group, i].astype(f32) * from_low_y
            kh = yh_ref[group, i].astype(f32) * from_high_y
            rest = jnp.concatenate([kh[7:8], kh[15:16], gap, kl[12:13], kl[4:5]], axis=0)
            u_s[x, beyond] = rest + jnp.concatenate([uh[4 * i : 4 * i + 4], ul[4 * i : 4 * i + 4]], axis=0)
            kh_s[x] = jnp.concatenate([kh[0:4], kl[0:4]], axis=0)
            for n, ref in enumerate((v0_s, v1_s, v2_s)):
                m = 4 * n + 4
                ref[x, beyond] = jnp.concatenate([kh[m : m + 4], kl[m : m + 4]], axis=0)
        return carry

    lax.fori_loop(0, BX // 4, halo_rows, 0)
    dest = (u_s, None, v0_s, v1_s, v2_s)
    for n in range(5):
        for base, ref, corner, scale, near, outer in (
            (0, xl_ref, 0, from_low_x, (W - 1, W - 2), 0),
            (BX + W, xh_ref, 5, from_high_x, (0, 1), W - 1),
        ):
            low = cl_ref[corner + n].astype(f32) * (scale * from_low_y)
            high = ch_ref[corner + n].astype(f32) * (scale * from_high_y)
            for i in range(W):
                value = ref[n * W + i].astype(f32)
                if n == 0 and i in near:
                    value = value + ref[(3 + near.index(i)) * W + outer].astype(f32)
                value = value * scale
                tile = jnp.concatenate([high[4 * i : 4 * i + 4], low[4 * i : 4 * i + 4]], axis=0)
                if n == 1:
                    kp_s[base % BX + i] = value
                    kh_s[base + i] = tile
                    edge_s[base + i, 0:8] = value[0:8]
                    edge_s[base + i, 8:16] = value[BY - 8 :]
                else:
                    dest[n][base + i, 0:BY] = value
                    dest[n][base + i, beyond] = tile

    kx_low = jnp.zeros((BY, NZ), f32)
    for i in range(W):
        k = kp_s[i]
        kx = 0.05 * (k + (kp_s[i + 1] if i < W - 1 else end_ref[0]))
        own_rows(k, kx_low, kx, refs, i)
        kx_low = kx
    c_s[W, 0:BY] = c_s[W, 0:BY] - kx_low
    kx_low = 0.05 * (end_ref[1] + kp_s[W])
    kx_s[BX + W - 1, 0:BY] = kx_low
    c_s[BX + W - 1, 0:BY] = c_s[BX + W - 1, 0:BY] - kx_low
    for i in range(W):
        k = kp_s[W + i]
        kx = 0.05 * (k + kp_s[min(W + i + 1, 2 * W - 1)])
        own_rows(k, kx_low, kx, refs, BX + W + i)
        kx_low = kx

    sub = lax.broadcasted_iota(jnp.int32, (8, NZ), 0)
    zt_up, zt_down = z_shifts(8)

    def halo_coefficients(x, carry):
        k, kx_low = carry
        k_next = kh_s[jnp.minimum(x + 1, EX - 1)]
        kx = 0.05 * (k + k_next)
        up = 0.05 * (edge_s[x, 8:16] + pltpu.roll(k, 7, 0))
        down = 0.05 * (edge_s[x, 0:8] + pltpu.roll(k, 1, 0))
        up = jnp.where(sub == 7, up, 0.0)
        down = jnp.where(sub == 0, down, 0.0)
        ky = jnp.where(sub == 7, pltpu.roll(down, 7, 0), 0.05 * (k + pltpu.roll(k, 7, 0)))
        kyd = jnp.where(sub == 0, pltpu.roll(up, 1, 0), pltpu.roll(ky, 1, 0))
        kz = 0.05 * (k + zt_down(k))
        kzd = 0.05 * (k + zt_up(k))
        kx_s[x, beyond] = kx
        ky_s[x, beyond] = ky
        kyd_s[x, beyond] = kyd
        kz_s[x, beyond] = kz
        kzd_s[x, beyond] = kzd
        c_s[x, beyond] = 1.0 - ((kx + kx_low) + (ky + kyd) + (kz + kzd))
        ky_s[x, BY - 8 : BY] = ky_s[x, BY - 8 : BY] + up
        kyd_s[x, 0:8] = kyd_s[x, 0:8] + down
        c_s[x, 0:8] = c_s[x, 0:8] - down
        c_s[x, BY - 8 : BY] = c_s[x, BY - 8 : BY] - up
        return k_next, kx

    lax.fori_loop(0, EX, halo_coefficients, (kh_s[0], jnp.zeros((8, NZ), f32)), unroll=4)
    z_up, z_down = z_shifts(EY)

    row = lax.broadcasted_iota(jnp.int32, (EY, NZ), 0)
    row_mask = jnp.where(row < BY, 1.0, jnp.where(row < BY + W, from_high_y, from_low_y))

    for step in range(STEPS):
        lo = step
        hi = EX - 1 - step

        def one_plane(x, carry, step=step):
            partial, up = carry
            u = u_s[x]
            w = 0.025 * u
            g0 = v0_s[x] * w
            g1 = v1_s[x] * w
            g2 = v2_s[x] * w
            done = partial + u * (kx_s[x - 1] - g0)
            prev = x - 1
            plane_mask = jnp.where(prev < W, from_low_x, jnp.where(prev >= BX + W, from_high_x, 1.0))
            u_s[prev] = done * (row_mask * plane_mask)
            up_next = u * (kx_s[x] + g0)
            total = u * c_s[x] + up
            total = total + pltpu.roll(u * (ky_s[x] + g1), 1, 0)
            total = total + pltpu.roll(u * (kyd_s[x] - g1), EY - 1, 0)
            total = total + z_up(u * (kz_s[x] + g2))
            total = total + z_down(u * (kzd_s[x] - g2))
            return total, up_next

        first_u = u_s[lo]
        first_up = first_u * (kx_s[lo] + v0_s[lo] * (0.025 * first_u))
        lax.fori_loop(lo + 1, hi + 1, one_plane, (jnp.zeros((EY, NZ), f32), first_up), unroll=4)

    for copy in copies:
        copy.wait()
    fit = (fit_ref[0], fit_ref[1])
    ytab = (ytab_s[0], ytab_s[1])

    def fit_planes(group, carry):
        at = pl.multiple_of(group * 8, 8)
        part = u_s[pl.ds(at + W, 8), 0:BY]
        adv_ref[pl.ds(at, 8)] = part
        rows = dot3(ytab, halves(part.reshape(8 * BY, NZ)))
        rows = dot3(halves(rows), fit)
        for r in range(YR):
            zt_ref[r, pl.ds(at, 8)] = rows[8 * r : 8 * r + 8]
        return carry

    lax.fori_loop(0, BX // 8, fit_planes, 0, unroll=2)

    send = halves(send_s[...])
    for r in range(0, YR, 2):
        lines = slice(r * MZ, (r + 2) * MZ)
        rows = dot3(send, halves(jnp.concatenate([zt_ref[r], zt_ref[r + 1]], axis=1)))
        lo_ref[:, lines] = rows[0:16]
        hi_ref[:, lines] = rows[16:32]
        lo2_ref[:, lines] = rows[0:16].astype(jnp.bfloat16)
        hi2_ref[:, lines] = rows[16:32].astype(jnp.bfloat16)
    base = base_s[...]
    full = base
    for j in range(7):
        full = full + base[:, 70 + j : 71 + j] * near_s[0, j : j + 1, :]
        full = full + base[:, 86 + j : 87 + j] * near_s[1, j : j + 1, :]
    full_ref[...] = full


def combine_body(zt_ref, lo_ref, hi_ref, lo2_ref, hi2_ref, full_ref, own_ref, carry_ref):
    f32 = jnp.float32
    q = lax.axis_index("py")
    full = halves(full_ref[...])
    carries = []
    for r in range(0, YR, 2):
        lines = slice(r * MZ, (r + 2) * MZ)
        rows = jnp.concatenate(
            [jnp.concatenate([zt_ref[r], zt_ref[r + 1]], axis=1), lo_ref[:, lines], hi_ref[:, lines]]
            + [ref[:, lines].astype(f32) for ref in (lo2_ref, hi2_ref)],
            axis=0,
        )
        out = dot3(full, halves(rows))
        for i in range(2):
            part = out[:, i * MZ : (i + 1) * MZ]
            if r + i < BY // 2:
                own_ref[r + i] = part
            else:
                carries.append(part)

    def coded(part):
        head = part[0].astype(jnp.bfloat16)
        rest = (part[0] - head.astype(f32)).astype(jnp.bfloat16)
        return jnp.concatenate([head, part[1].astype(jnp.bfloat16), part[2].astype(jnp.bfloat16), rest], axis=0)

    up = coded(carries[:3])
    down = coded(carries[3:])
    for t in range(carry_ref.shape[0]):

        @pl.when(t > q)
        def _():
            carry_ref[t] = up

        @pl.when(t <= q)
        def _():
            carry_ref[t] = down


def couple_body(own_ref, got_ref, couple_hbm, out_ref, couple_s, sem):
    f32 = jnp.float32
    q = lax.axis_index("py")
    copy = pltpu.make_async_copy(couple_hbm.at[q], couple_s, sem)
    copy.start()
    copy.wait()
    block = BX // 2
    for base in range(0, BY // 2, 8):

        def one(t, acc, base=base):
            for c in range(4):
                part = got_ref[t, c * block : (c + 1) * block].astype(f32)
                acc = tuple(a + couple_s[base + m, t * 4 + c] * part for m, a in enumerate(acc))
            return acc

        acc = lax.fori_loop(0, got_ref.shape[0], one, tuple(own_ref[base + m] for m in range(8)), unroll=2)
        for m in range(8):
            out_ref[:, base + m, :] = acc[m]


KEPT = 11


def in_hbm(a):
    return pltpu.with_memory_space_constraint(a, pltpu.HBM)


def own_coefficients(field, diffusivity, velocity, after):
    vmem = pl.BlockSpec(memory_space=pltpu.VMEM)
    f32 = jnp.float32
    return pl.pallas_call(
        own_body,
        out_shape=[pltpu.VMEM((EX, EY, NZ), f32)] * (KEPT - 1)
        + [pltpu.VMEM((EX, 16, NZ), f32), pltpu.VMEM((2, BY, NZ), f32)],
        in_specs=[pl.BlockSpec(memory_space=pltpu.HBM)] * 3 + [pl.BlockSpec(memory_space=pl.ANY)],
        out_specs=[vmem] * (KEPT + 1),
        scratch_shapes=[pltpu.VMEM(a.shape, a.dtype) for a in (field, diffusivity, velocity)]
        + [pltpu.SemaphoreType.DMA((3, BX // PACK))],
        compiler_params=pltpu.CompilerParams(vmem_limit_bytes=12 * 1024 * 1024),
        name="own_coefficients",
    )(*[in_hbm(a) for a in (field, diffusivity, velocity)], after)


def time_steps(counts, margin, halos, fit, tables, end, kept):
    vmem = pl.BlockSpec(memory_space=pltpu.VMEM)
    smem = pl.BlockSpec(memory_space=pltpu.SMEM)
    hbm = pl.BlockSpec(memory_space=pltpu.HBM)
    f32 = jnp.float32
    bf16 = jnp.bfloat16
    shapes = [((BX, BY, NZ), f32), ((YR, BX, MZ), f32)] + [((16, LINES), f32)] * 2 + [((16, LINES), bf16)] * 2
    shapes += [((BX // 2, 128), f32)]
    return pl.pallas_call(
        functools.partial(stencil_body, *counts),
        out_shape=[jax.ShapeDtypeStruct(s, t) for s, t in shapes] + [pltpu.VMEM(a.shape, f32) for a in kept],
        in_specs=[smem] + [vmem] * 7 + [hbm] * 4 + [vmem] * (1 + KEPT),
        out_specs=[vmem] * (7 + KEPT),
        input_output_aliases={13 + i: 7 + i for i in range(KEPT)},
        scratch_shapes=[
            pltpu.VMEM((EX, 8, NZ), f32),
            pltpu.VMEM((2 * W, BY, NZ), f32),
            pltpu.VMEM((BX // 2, 128), f32),
            pltpu.VMEM((BX // 2, BX), f32),
            pltpu.VMEM((2, 8, 128), f32),
            pltpu.VMEM((2, YR * 8, 8 * BY), bf16),
            pltpu.SemaphoreType.DMA((5,)),
        ],
        compiler_params=pltpu.CompilerParams(vmem_limit_bytes=STEP_VMEM * 1024 * 1024),
        name="time_steps",
    )(margin, *halos, fit, *[in_hbm(t) for t in tables], end, *kept)[:7]


def combine(count_y, rows):
    vmem = pl.BlockSpec(memory_space=pltpu.VMEM)
    return pl.pallas_call(
        combine_body,
        out_shape=[
            jax.ShapeDtypeStruct((BY // 2, BX // 2, MZ), jnp.float32),
            jax.ShapeDtypeStruct((count_y, 2 * BX, MZ), jnp.bfloat16),
        ],
        in_specs=[vmem] * 6,
        out_specs=[vmem] * 2,
        compiler_params=pltpu.CompilerParams(vmem_limit_bytes=12 * 1024 * 1024),
        name="combine",
    )(*rows)


def add_carries(own, got, couple):
    vmem = pl.BlockSpec(memory_space=pltpu.VMEM)
    return pl.pallas_call(
        couple_body,
        out_shape=jax.ShapeDtypeStruct((BX // 2, BY // 2, MZ), jnp.float32),
        in_specs=[vmem, vmem, pl.BlockSpec(memory_space=pltpu.HBM)],
        out_specs=vmem,
        scratch_shapes=[pltpu.SMEM(couple.shape[1:], jnp.float32), pltpu.SemaphoreType.DMA(())],
        compiler_params=pltpu.CompilerParams(vmem_limit_bytes=8 * 1024 * 1024),
        name="add_carries",
    )(own, got, in_hbm(couple))


def ring(n, d):
    return [(i, (i + d) % n) for i in range(n)]


def shift(a, axis, d):
    return lax.ppermute(a, axis, ring(lax.axis_size(axis), d))


def pack_body(margin_ref, f_hbm, k_hbm, v_hbm, ylo_ref, yhi_ref, xlo_ref, xhi_ref, f_ref, k_ref, v_ref, sems):
    f32 = jnp.float32
    bf16 = jnp.bfloat16
    t = BY - W
    copies = load((f_hbm, k_hbm, v_hbm), (f_ref, k_ref, v_ref), sems)

    def rest(u):
        return u - u.astype(bf16).astype(f32)

    def faces(g, carry):
        tails, heads = [], []
        for i in range(4):
            x = 4 * g + i
            u = f_ref[x]
            tails.append(u[t:])
            heads.append(u[:W])
            ur_t = rest(u[t - 4 :])
            ur_h = rest(u[:8])
            k, v0, v1, v2 = [r.astype(f32) for r in (k_ref[x], v_ref[0, x], v_ref[1, x], v_ref[2, x])]
            ylo_ref[g, i] = jnp.concatenate(
                [k[t:], ur_t[7:8], v0[t + 1 :], v1[t:], ur_t[6:7], v2[t + 1 :]], axis=0
            ).astype(bf16)
            yhi_ref[g, i] = jnp.concatenate(
                [k[:W], v0[: W - 1], ur_h[0:1], v1[:W], v2[: W - 1], ur_h[1:2]], axis=0
            ).astype(bf16)
        ylo_ref[g, 4] = jnp.concatenate(tails, axis=0).astype(bf16)
        yhi_ref[g, 4] = jnp.concatenate(heads, axis=0).astype(bf16)
        return carry

    def x_side(at, out, near, outer):
        for i in range(W):
            out[i] = f_ref[at + i].astype(bf16)
            out[W + i] = k_ref[at + i]
            out[2 * W + i] = v_ref[0, at + i]
            if i == outer:
                out[3 * W + i] = rest(f_ref[at + near[0]]).astype(bf16)
                out[4 * W + i] = rest(f_ref[at + near[1]]).astype(bf16)
            else:
                out[3 * W + i] = v_ref[1, at + i]
                out[4 * W + i] = v_ref[2, at + i]
        half = jnp.zeros((16, NZ), f32)
        out[5 * W] = jnp.concatenate([half + margin_ref[0, 0].astype(f32), half + margin_ref[0, 1].astype(f32)], axis=0).astype(bf16)

    for c in range(BX // PACK):
        for copy in copies[c]:
            copy.wait()
        lax.fori_loop(c * PACK // 4, (c + 1) * PACK // 4, faces, 0)
        if c == 0:
            x_side(0, xhi_ref, (0, 1), W - 1)
    x_side(BX - W, xlo_ref, (W - 1, W - 2), 0)


def corner_body(xl_ref, xh_ref, up_ref, down_ref):
    f32 = jnp.float32
    for side, ref in enumerate((xl_ref, xh_ref)):
        for n in range(5):
            planes = [ref[n * W + i].astype(f32) for i in range(W)]
            up_ref[side * 5 + n] = jnp.concatenate([a[BY - W :] for a in planes], axis=0).astype(jnp.bfloat16)
            down_ref[side * 5 + n] = jnp.concatenate([a[:W] for a in planes], axis=0).astype(jnp.bfloat16)


def halo_parts(field, diffusivity, velocity, margin):
    bf16 = jnp.bfloat16
    y_shape = (BX // 4, 5, 16, NZ)
    x_shape = (5 * W + 1, BY, NZ)
    c_shape = (10, 16, NZ)
    vmem = pl.BlockSpec(memory_space=pltpu.VMEM)
    hbm = pl.BlockSpec(memory_space=pltpu.HBM)
    ylo, yhi, xlo, xhi = pl.pallas_call(
        pack_body,
        out_shape=[jax.ShapeDtypeStruct(s, bf16) for s in [y_shape] * 2 + [x_shape] * 2],
        in_specs=[pl.BlockSpec(memory_space=pltpu.SMEM), hbm, hbm, hbm],
        out_specs=[vmem] * 4,
        scratch_shapes=[pltpu.VMEM(a.shape, a.dtype) for a in (field, diffusivity, velocity)]
        + [pltpu.SemaphoreType.DMA((3, BX // PACK))],
        compiler_params=pltpu.CompilerParams(vmem_limit_bytes=PACK_VMEM * 1024 * 1024),
        name="pack_faces",
    )(margin, *[in_hbm(a) for a in (field, diffusivity, velocity)])
    xl = shift(xlo, "px", 1)
    xh = shift(xhi, "px", -1)
    yl = shift(ylo, "py", 1)
    yh = shift(yhi, "py", -1)
    c_up, c_down = pl.pallas_call(
        corner_body,
        out_shape=[jax.ShapeDtypeStruct(c_shape, bf16)] * 2,
        in_specs=[vmem] * 2,
        out_specs=[vmem] * 2,
        compiler_params=pltpu.CompilerParams(vmem_limit_bytes=4 * 1024 * 1024),
        name="pack_corners",
    )(xl, xh)
    halos = (yl, yh, xl, xh, shift(c_up, "py", 1), shift(c_down, "py", -1))
    return halos, own_coefficients(field, diffusivity, velocity, ylo)


def per_device(field, diffusivity, velocity, margin):
    count_x = lax.axis_size("px")
    count_y = lax.axis_size("py")
    fit = jnp.asarray(np.stack(split(fit_matrix(NZ).T)))
    ytab, couple = y_tables(count_y)
    tables = [jnp.asarray(t) for t in x_tables(count_x) + [ytab]]
    halos, kept = halo_parts(field, diffusivity, velocity, margin)
    advected, zt, lo, hi, lo2, hi2, full = time_steps(
        (count_x, count_y), margin, halos, fit, tables, kept[KEPT], kept[:KEPT]
    )
    rows = (zt, shift(lo, "px", 1), shift(hi, "px", -1), shift(lo2, "px", 2), shift(hi2, "px", -2), full)
    own, carries = combine(count_y, rows)
    got = lax.all_to_all(carries, "py", split_axis=0, concat_axis=0, tiled=True)
    return advected, add_carries(own, got, jnp.asarray(couple))


def solution(mesh):
    placed = (P("px", "py", None), P("px", "py", None), P(None, "px", "py", None), P("px", None))
    return jax.shard_map(
        per_device,
        mesh=mesh,
        in_specs=placed,
        out_specs=(P("px", "py", None), P("px", "py", None)),
        check_vma=False,
    )
```

```python
import functools

import jax
import jax.numpy as jnp
import numpy as np
from jax import lax
from jax.experimental import pallas as pl
from jax.experimental.pallas import tpu as pltpu
from jax.sharding import PartitionSpec as P

STEPS = 4
OVMAX = 4
BX = 64
BY = 32
NZ = 256
MZ = 128
W = 4
EX = BX + 2 * W
EY = BY + 2 * W
YR = BY // 2 + 6
LINES = YR * 128


PACK = 16
PACK_VMEM = 12
STEP_VMEM = 16


def bspline(t):
    m = np.abs(t)
    inner = (4.0 - 6.0 * m * m + 3.0 * m**3) / 6.0
    outer = np.maximum(2.0 - m, 0.0) ** 3 / 6.0
    return np.where(m < 1.0, inner, outer)


def basis(n):
    j = np.arange(n)[:, None]
    k = np.arange(n // 2)[None, :]
    return bspline((j - 2.0 * k - 0.5) / 2.0)


def fit_matrix(n):
    b = basis(n)
    return np.linalg.solve(b.T @ b, b.T)


def split(a):
    a = a.astype(np.float32)
    hi = a.astype(jnp.bfloat16)
    return hi, (a - hi.astype(np.float32)).astype(jnp.bfloat16)


def y_tables(count):
    total = count * BY
    s = fit_matrix(total)
    own = BY // 2
    rows = np.zeros((count, YR, BY))
    couple = np.zeros((count, own, count, 4))
    for q in range(count):
        cols = s[:, q * BY : (q + 1) * BY]
        rows[q, :own] = cols[q * own : (q + 1) * own]
        for at, far, targets in ((own, cols[(q + 1) * own :], range(q + 1, count)), (own + 3, cols[: q * own], range(q))):
            if len(targets) == 0:
                continue
            u, sv, vt = np.linalg.svd(far, full_matrices=False)
            assert sv[3] < 1e-10 * sv[0]
            rows[q, at : at + 3] = vt[:3]
            left = (u[:, :3] * sv[:3]).reshape(len(targets), own, 3)
            for i, t in enumerate(targets):
                couple[t, :, q, :3] = left[i]
                couple[t, :, q, 3] = left[i, :, 0]
    table = np.einsum("qry,xw->qrxwy", rows, np.eye(8)).reshape(count, YR * 8, 8 * BY)
    spaced = np.einsum("qmtc,xw->qxmtwc", couple, np.eye(8)).reshape(count, own * 8, count * 32)
    return np.stack(split(table), axis=1), np.stack(split(spaced), axis=1)


def x_tables(count):
    total = count * BX
    block = BX // 2
    ctrl = total // 2
    b = basis(total)
    width = block + 2 * OVMAX
    gpad = np.zeros((ctrl + 16, ctrl + 16))
    gpad[8:-8, 8:-8] = b.T @ b
    bt = bspline((np.arange(BX)[None] - 2.0 * (np.arange(block + 4)[:, None] - 2) - 0.5) / 2.0)
    base, send, near = [], [], []
    for cls, p in enumerate((0, 1, count - 1)):
        has_low = float(cls != 0)
        has_high = float(cls != 2)
        start = p * block
        knots = start - OVMAX + np.arange(width)
        lo = start - OVMAX + 8
        full = gpad[lo : lo + width, lo : lo + width]
        band = gpad[lo : lo + width, lo - 3 : lo + width + 3]
        for m0 in range(OVMAX + 1):
            for m1 in range(OVMAX + 1):
                inside = (knots >= start - m0) & (knots < start + block + m1) & (knots >= 0) & (knots < ctrl)
                w = inside.astype(np.float64)
                mat = full * w[:, None] * w[None, :] + np.diag(1.0 - w)
                e = (np.linalg.inv(mat) * w[None, :])[OVMAX : OVMAX + block]
                q = e @ band
                ql = q[:, :7] * has_low
                qr = q[:, 7 + block :] * has_high
                two = 2.0 * e - q[:, 7 : 7 + block] @ e
                low = two[:, 0:6] * has_low
                high = two[:, block + 2 :] * has_high
                gap3 = np.zeros((block, 3))
                gap32 = np.zeros((block, 32))
                base.append(np.concatenate([two[:, 2 : block + 6] @ bt, low, -ql, gap3, high, -qr, gap3, gap32], axis=1))
                pad = np.zeros((3, BX))
                send.append(
                    np.concatenate(
                        [bt[block - 2 :], e[block - 7 :, 2 : block + 6] @ bt, pad, bt[:6], e[:7, 2 : block + 6] @ bt, pad]
                    )
                )
                both = np.zeros((2, 8, 128))
                both[0, :7, :BX] = e[block - 7 :, block + 2 :] @ bt[0:6]
                both[0, :7, 96:102] = e[block - 7 :, 0:6] * has_low
                both[1, :7, :BX] = e[:7, 0:6] @ bt[block - 2 :]
                both[1, :7, 112:118] = e[:7, block + 2 :] * has_high
                near.append(both)
    return [np.stack(t).astype(np.float32) for t in (base, send, near)]


def z_shifts(rows):
    lane = lax.broadcasted_iota(jnp.int32, (rows, 128), 1)
    first = lane == 0
    final = lane == 127

    def z_up(a):
        lo = pltpu.roll(a[:, :128], 1, 1)
        hi = pltpu.roll(a[:, 128:], 1, 1)
        return jnp.concatenate([jnp.where(first, 0.0, lo), jnp.where(first, lo, hi)], axis=1)

    def z_down(a):
        lo = pltpu.roll(a[:, :128], 127, 1)
        hi = pltpu.roll(a[:, 128:], 127, 1)
        return jnp.concatenate([jnp.where(final, hi, lo), jnp.where(final, 0.0, hi)], axis=1)

    return z_up, z_down


def own_rows(k, kx_low, kx, refs, x):
    kx_s, ky_s, kyd_s, kz_s, kzd_s, c_s = refs
    z_up, z_down = z_shifts(BY)
    row = lax.broadcasted_iota(jnp.int32, (BY, NZ), 0)
    own = slice(0, BY)
    ky = jnp.where(row < BY - 1, 0.05 * (k + pltpu.roll(k, BY - 1, 0)), 0.0)
    kyd = pltpu.roll(ky, 1, 0)
    kz = 0.05 * (k + z_down(k))
    kzd = 0.05 * (k + z_up(k))
    kx_s[x, own] = kx
    ky_s[x, own] = ky
    kyd_s[x, own] = kyd
    kz_s[x, own] = kz
    kzd_s[x, own] = kzd
    c_s[x, own] = 1.0 - ((kx + kx_low) + (ky + kyd) + (kz + kzd))


def load(sources, targets, sems):
    copies = []
    for c in range(BX // PACK):
        part = pl.ds(c * PACK, PACK)
        copies.append([])
        for n, (src, dst) in enumerate(zip(sources, targets)):
            at = (slice(None), part) if len(src.shape) == 4 else (part,)
            copies[-1].append(pltpu.make_async_copy(src.at[at], dst.at[at], sems.at[n, c]))
            copies[-1][-1].start()
    return copies


def own_body(f_hbm, k_hbm, v_hbm, after_ref, u_s, v0_s, v1_s, v2_s, kx_s, ky_s, kyd_s, kz_s, kzd_s, c_s, edge_s, end_ref,
             f_ref, k_ref, v_ref, sems):
    f32 = jnp.float32
    for part in load((f_hbm, k_hbm, v_hbm), (f_ref, k_ref, v_ref), sems):
        for copy in part:
            copy.wait()
    refs = (kx_s, ky_s, kyd_s, kz_s, kzd_s, c_s)

    def plane(x, carry):
        k, kx_low = carry
        k_next = k_ref[jnp.minimum(x + 1, BX - 1)].astype(f32)
        kx = jnp.where(x < BX - 1, 0.05, 0.0) * (k + k_next)
        u_s[x + W, 0:BY] = f_ref[x]
        for n, ref in enumerate((v0_s, v1_s, v2_s)):
            ref[x + W, 0:BY] = v_ref[n, x].astype(f32)
        edge_s[x + W, 0:8] = k[0:8]
        edge_s[x + W, 8:16] = k[BY - 8 :]
        own_rows(k, kx_low, kx, refs, x + W)
        return k_next, kx

    lax.fori_loop(0, BX, plane, (k_ref[0].astype(f32), jnp.zeros((BY, NZ), f32)), unroll=4)
    end_ref[0] = k_ref[0].astype(f32)
    end_ref[1] = k_ref[BX - 1].astype(f32)


def dot3(a, b):
    dot = functools.partial(jnp.dot, preferred_element_type=jnp.float32)
    return dot(a[0], b[0]) + (dot(a[0], b[1]) + dot(a[1], b[0]))


def halves(a):
    hi = a.astype(jnp.bfloat16)
    return hi, (a - hi.astype(jnp.float32)).astype(jnp.bfloat16)


def place_of(owner, count, m0, m1):
    own = jnp.clip(owner, 0, count - 1)
    cls = jnp.where(own == 0, 0, jnp.where(own == count - 1, 2, 1))
    n = OVMAX + 1
    return (cls * n + jnp.clip(m0, 0, OVMAX)) * n + jnp.clip(m1, 0, OVMAX)


def stencil_body(count_x, count_y, margin_ref, yl_ref, yh_ref, xl_ref, xh_ref, cl_ref, ch_ref, fit_ref, base_hbm, send_hbm,
                 near_hbm, ytab_hbm, couple_hbm, end_ref,
                 *rest_refs):
    f32 = jnp.float32
    outs = rest_refs[KEPT:]
    adv_hbm, zt_ref, lo_ref, hi_ref, lo2_ref, hi2_ref, full_ref, couple_ref = outs[:8]
    u_s, v0_s, v1_s, v2_s, kx_s, ky_s, kyd_s, kz_s, kzd_s, c_s, edge_s = outs[8 : 8 + KEPT]
    kh_s, kp_s, base_s, send_s, near_s, ytab_s, sems = outs[8 + KEPT :]
    p = lax.axis_index("px")
    q = lax.axis_index("py")

    def margins(ref):
        part = ref[5 * W].astype(f32)
        return [jnp.max(a).astype(jnp.int32) for a in (part[0:8], part[16:24])]

    mine = place_of(p, count_x, margin_ref[0, 0], margin_ref[0, 1])
    low = place_of(p - 1, count_x, *margins(xl_ref))
    high = place_of(p + 1, count_x, *margins(xh_ref))
    copies = [
        pltpu.make_async_copy(base_hbm.at[mine], base_s, sems.at[0]),
        pltpu.make_async_copy(send_hbm.at[mine], send_s, sems.at[1]),
        pltpu.make_async_copy(near_hbm.at[low, 0], near_s.at[0], sems.at[2]),
        pltpu.make_async_copy(near_hbm.at[high, 1], near_s.at[1], sems.at[3]),
        pltpu.make_async_copy(ytab_hbm.at[q], ytab_s, sems.at[4]),
        pltpu.make_async_copy(couple_hbm.at[q], couple_ref, sems.at[5]),
    ]
    for copy in copies:
        copy.start()
    refs = (kx_s, ky_s, kyd_s, kz_s, kzd_s, c_s)
    from_low_x = jnp.where(p > 0, 1.0, 0.0)
    from_high_x = jnp.where(p < count_x - 1, 1.0, 0.0)
    from_low_y = jnp.where(q > 0, 1.0, 0.0)
    from_high_y = jnp.where(q < count_y - 1, 1.0, 0.0)
    beyond = slice(BY, EY)

    def halo_rows(group, carry):
        at = group * 4
        ul = yl_ref[group, 4].astype(f32) * from_low_y
        uh = yh_ref[group, 4].astype(f32) * from_high_y
        gap = jnp.zeros((4, NZ), f32)
        for i in range(4):
            x = at + i + W
            kl = yl_ref[group, i].astype(f32) * from_low_y
            kh = yh_ref[group, i].astype(f32) * from_high_y
            rest = jnp.concatenate([kh[7:8], kh[15:16], gap, kl[12:13], kl[4:5]], axis=0)
            u_s[x, beyond] = rest + jnp.concatenate([uh[4 * i : 4 * i + 4], ul[4 * i : 4 * i + 4]], axis=0)
            kh_s[x] = jnp.concatenate([kh[0:4], kl[0:4]], axis=0)
            for n, ref in enumerate((v0_s, v1_s, v2_s)):
                m = 4 * n + 4
                ref[x, beyond] = jnp.concatenate([kh[m : m + 4], kl[m : m + 4]], axis=0)
        return carry

    lax.fori_loop(0, BX // 4, halo_rows, 0)
    dest = (u_s, None, v0_s, v1_s, v2_s)
    for n in range(5):
        for base, ref, corner, scale, near, outer in (
            (0, xl_ref, 0, from_low_x, (W - 1, W - 2), 0),
            (BX + W, xh_ref, 5, from_high_x, (0, 1), W - 1),
        ):
            low = cl_ref[corner + n].astype(f32) * (scale * from_low_y)
            high = ch_ref[corner + n].astype(f32) * (scale * from_high_y)
            for i in range(W):
                value = ref[n * W + i].astype(f32)
                if n == 0 and i in near:
                    value = value + ref[(3 + near.index(i)) * W + outer].astype(f32)
                value = value * scale
                tile = jnp.concatenate([high[4 * i : 4 * i + 4], low[4 * i : 4 * i + 4]], axis=0)
                if n == 1:
                    kp_s[base % BX + i] = value
                    kh_s[base + i] = tile
                    edge_s[base + i, 0:8] = value[0:8]
                    edge_s[base + i, 8:16] = value[BY - 8 :]
                else:
                    dest[n][base + i, 0:BY] = value
                    dest[n][base + i, beyond] = tile

    kx_low = jnp.zeros((BY, NZ), f32)
    for i in range(W):
        k = kp_s[i]
        kx = 0.05 * (k + (kp_s[i + 1] if i < W - 1 else end_ref[0]))
        own_rows(k, kx_low, kx, refs, i)
        kx_low = kx
    c_s[W, 0:BY] = c_s[W, 0:BY] - kx_low
    kx_low = 0.05 * (end_ref[1] + kp_s[W])
    kx_s[BX + W - 1, 0:BY] = kx_low
    c_s[BX + W - 1, 0:BY] = c_s[BX + W - 1, 0:BY] - kx_low
    for i in range(W):
        k = kp_s[W + i]
        kx = 0.05 * (k + kp_s[min(W + i + 1, 2 * W - 1)])
        own_rows(k, kx_low, kx, refs, BX + W + i)
        kx_low = kx

    sub = lax.broadcasted_iota(jnp.int32, (8, NZ), 0)
    zt_up, zt_down = z_shifts(8)

    def halo_coefficients(x, carry):
        k, kx_low = carry
        k_next = kh_s[jnp.minimum(x + 1, EX - 1)]
        kx = 0.05 * (k + k_next)
        up = 0.05 * (edge_s[x, 8:16] + pltpu.roll(k, 7, 0))
        down = 0.05 * (edge_s[x, 0:8] + pltpu.roll(k, 1, 0))
        up = jnp.where(sub == 7, up, 0.0)
        down = jnp.where(sub == 0, down, 0.0)
        ky = jnp.where(sub == 7, pltpu.roll(down, 7, 0), 0.05 * (k + pltpu.roll(k, 7, 0)))
        kyd = jnp.where(sub == 0, pltpu.roll(up, 1, 0), pltpu.roll(ky, 1, 0))
        kz = 0.05 * (k + zt_down(k))
        kzd = 0.05 * (k + zt_up(k))
        kx_s[x, beyond] = kx
        ky_s[x, beyond] = ky
        kyd_s[x, beyond] = kyd
        kz_s[x, beyond] = kz
        kzd_s[x, beyond] = kzd
        c_s[x, beyond] = 1.0 - ((kx + kx_low) + (ky + kyd) + (kz + kzd))
        ky_s[x, BY - 8 : BY] = ky_s[x, BY - 8 : BY] + up
        kyd_s[x, 0:8] = kyd_s[x, 0:8] + down
        c_s[x, 0:8] = c_s[x, 0:8] - down
        c_s[x, BY - 8 : BY] = c_s[x, BY - 8 : BY] - up
        return k_next, kx

    lax.fori_loop(0, EX, halo_coefficients, (kh_s[0], jnp.zeros((8, NZ), f32)), unroll=4)
    z_up, z_down = z_shifts(EY)

    row = lax.broadcasted_iota(jnp.int32, (EY, NZ), 0)
    row_mask = jnp.where(row < BY, 1.0, jnp.where(row < BY + W, from_high_y, from_low_y))

    for step in range(STEPS):
        lo = step
        hi = EX - 1 - step

        def one_plane(x, carry, step=step):
            partial, up = carry
            u = u_s[x]
            w = 0.025 * u
            g0 = v0_s[x] * w
            g1 = v1_s[x] * w
            g2 = v2_s[x] * w
            done = partial + u * (kx_s[x - 1] - g0)
            prev = x - 1
            plane_mask = jnp.where(prev < W, from_low_x, jnp.where(prev >= BX + W, from_high_x, 1.0))
            u_s[prev] = done * (row_mask * plane_mask)
            up_next = u * (kx_s[x] + g0)
            total = u * c_s[x] + up
            total = total + pltpu.roll(u * (ky_s[x] + g1), 1, 0)
            total = total + pltpu.roll(u * (kyd_s[x] - g1), EY - 1, 0)
            total = total + z_up(u * (kz_s[x] + g2))
            total = total + z_down(u * (kzd_s[x] - g2))
            return total, up_next

        first_u = u_s[lo]
        first_up = first_u * (kx_s[lo] + v0_s[lo] * (0.025 * first_u))
        lax.fori_loop(lo + 1, hi + 1, one_plane, (jnp.zeros((EY, NZ), f32), first_up), unroll=4)

    result = pltpu.make_async_copy(u_s.at[pl.ds(W, BX), pl.ds(0, BY)], adv_hbm, sems.at[6])
    result.start()
    for copy in copies:
        copy.wait()
    fit = (fit_ref[0], fit_ref[1])
    ytab = (ytab_s[0], ytab_s[1])

    def fit_planes(group, carry):
        at = pl.multiple_of(group * 8, 8)
        part = u_s[pl.ds(at + W, 8), 0:BY]
        rows = dot3(ytab, halves(part.reshape(8 * BY, NZ)))
        rows = dot3(halves(rows), fit)
        for r in range(YR):
            zt_ref[r, pl.ds(at, 8)] = rows[8 * r : 8 * r + 8]
        return carry

    lax.fori_loop(0, BX // 8, fit_planes, 0, unroll=2)

    send = halves(send_s[...])
    for r in range(0, YR, 2):
        lines = slice(r * MZ, (r + 2) * MZ)
        rows = dot3(send, halves(jnp.concatenate([zt_ref[r], zt_ref[r + 1]], axis=1)))
        lo_ref[:, lines] = rows[0:16]
        hi_ref[:, lines] = rows[16:32]
        lo2_ref[:, lines] = rows[0:16].astype(jnp.bfloat16)
        hi2_ref[:, lines] = rows[16:32].astype(jnp.bfloat16)
    base = base_s[...]
    full = base
    for j in range(7):
        full = full + base[:, 70 + j : 71 + j] * near_s[0, j : j + 1, :]
        full = full + base[:, 86 + j : 87 + j] * near_s[1, j : j + 1, :]
    full_ref[...] = full
    result.wait()


def combine_body(zt_ref, lo_ref, hi_ref, lo2_ref, hi2_ref, full_ref, own_ref, carry_ref):
    f32 = jnp.float32
    q = lax.axis_index("py")
    full = halves(full_ref[...])

    def stack(first, last):
        lines = slice(first * MZ, last * MZ)
        return jnp.concatenate(
            [jnp.concatenate([zt_ref[r] for r in range(first, last)], axis=1), lo_ref[:, lines], hi_ref[:, lines]]
            + [ref[:, lines].astype(f32) for ref in (lo2_ref, hi2_ref)],
            axis=0,
        )

    own = BY // 2
    for r in range(0, own, 2):
        out = dot3(full, halves(stack(r, r + 2)))
        for i in range(2):
            own_ref[:, r + i, :] = out[:, i * MZ : (i + 1) * MZ]

    block = BX // 2
    part = lax.broadcasted_iota(jnp.int32, (4 * block, 128), 0) % 4
    spread = lax.broadcasted_iota(jnp.int32, (4 * block, block), 0) // 4
    spread = jnp.where(spread == lax.broadcasted_iota(jnp.int32, (4 * block, block), 1), 1.0, 0.0).astype(jnp.bfloat16)
    spaced = []
    for f in full:
        rows = jnp.dot(spread, f, preferred_element_type=f32)
        spaced.append(
            jnp.concatenate(
                [jnp.where(part % 3 == 0, rows, 0.0), jnp.where(part == 1, rows, 0.0), jnp.where(part == 2, rows, 0.0)],
                axis=1,
            ).astype(jnp.bfloat16)
        )
    carries = stack(own, YR)
    carries = jnp.concatenate(
        [jnp.concatenate([carries[:, n * MZ : (n + 1) * MZ], carries[:, (n + 3) * MZ : (n + 4) * MZ]], axis=1) for n in range(3)],
        axis=0,
    )
    carries = dot3(spaced, halves(carries))
    coded = []
    for n in range(2):
        value = carries[:, n * MZ : (n + 1) * MZ]
        head = value.astype(jnp.bfloat16).astype(f32)
        coded.append(jnp.where(part == 3, value - head, value).astype(jnp.bfloat16))
    for t in range(carry_ref.shape[0]):

        @pl.when(t > q)
        def _():
            carry_ref[t] = coded[0]

        @pl.when(t <= q)
        def _():
            carry_ref[t] = coded[1]


def couple_body(own_ref, got_ref, couple_ref, out_ref):
    dot = functools.partial(jnp.dot, preferred_element_type=jnp.float32)
    head = couple_ref[0]
    rest = couple_ref[1]
    for x in range(0, BX // 2, 8):
        got = got_ref[:, 4 * x : 4 * x + 32].reshape(-1, MZ)
        out_ref[x : x + 8] = own_ref[x : x + 8] + (dot(head, got) + dot(rest, got)).reshape(8, BY // 2, MZ)


KEPT = 11


def in_hbm(a):
    return pltpu.with_memory_space_constraint(a, pltpu.HBM)


def own_coefficients(field, diffusivity, velocity, after):
    vmem = pl.BlockSpec(memory_space=pltpu.VMEM)
    f32 = jnp.float32
    return pl.pallas_call(
        own_body,
        out_shape=[pltpu.VMEM((EX, EY, NZ), f32)] * (KEPT - 1)
        + [pltpu.VMEM((EX, 16, NZ), f32), pltpu.VMEM((2, BY, NZ), f32)],
        in_specs=[pl.BlockSpec(memory_space=pltpu.HBM)] * 3 + [pl.BlockSpec(memory_space=pl.ANY)],
        out_specs=[vmem] * (KEPT + 1),
        scratch_shapes=[pltpu.VMEM(a.shape, a.dtype) for a in (field, diffusivity, velocity)]
        + [pltpu.SemaphoreType.DMA((3, BX // PACK))],
        compiler_params=pltpu.CompilerParams(vmem_limit_bytes=12 * 1024 * 1024),
        name="own_coefficients",
    )(*[in_hbm(a) for a in (field, diffusivity, velocity)], after)


def time_steps(counts, margin, halos, fit, tables, end, kept):
    vmem = pl.BlockSpec(memory_space=pltpu.VMEM)
    smem = pl.BlockSpec(memory_space=pltpu.SMEM)
    hbm = pl.BlockSpec(memory_space=pltpu.HBM)
    f32 = jnp.float32
    bf16 = jnp.bfloat16
    shapes = [((BX, BY, NZ), f32), ((YR, BX, MZ), f32)] + [((16, LINES), f32)] * 2 + [((16, LINES), bf16)] * 2
    shapes += [((BX // 2, 128), f32)]
    return pl.pallas_call(
        functools.partial(stencil_body, *counts),
        out_shape=[jax.ShapeDtypeStruct(s, t) for s, t in shapes]
        + [pltpu.VMEM(tables[-1].shape[1:], bf16)]
        + [pltpu.VMEM(a.shape, f32) for a in kept],
        in_specs=[smem] + [vmem] * 7 + [hbm] * 5 + [vmem] * (1 + KEPT),
        out_specs=[hbm] + [vmem] * (7 + KEPT),
        input_output_aliases={14 + i: 8 + i for i in range(KEPT)},
        scratch_shapes=[
            pltpu.VMEM((EX, 8, NZ), f32),
            pltpu.VMEM((2 * W, BY, NZ), f32),
            pltpu.VMEM((BX // 2, 128), f32),
            pltpu.VMEM((BX // 2, BX), f32),
            pltpu.VMEM((2, 8, 128), f32),
            pltpu.VMEM((2, YR * 8, 8 * BY), bf16),
            pltpu.SemaphoreType.DMA((7,)),
        ],
        compiler_params=pltpu.CompilerParams(vmem_limit_bytes=STEP_VMEM * 1024 * 1024),
        name="time_steps",
    )(margin, *halos, fit, *[in_hbm(t) for t in tables], end, *kept)[:8]


def combine(count_y, rows):
    vmem = pl.BlockSpec(memory_space=pltpu.VMEM)
    return pl.pallas_call(
        combine_body,
        out_shape=[
            jax.ShapeDtypeStruct((BX // 2, BY // 2, MZ), jnp.float32),
            jax.ShapeDtypeStruct((count_y, 2 * BX, MZ), jnp.bfloat16),
        ],
        in_specs=[vmem] * 6,
        out_specs=[vmem] * 2,
        compiler_params=pltpu.CompilerParams(vmem_limit_bytes=12 * 1024 * 1024),
        name="combine",
    )(*rows)


def add_carries(own, got, couple):
    vmem = pl.BlockSpec(memory_space=pltpu.VMEM)
    return pl.pallas_call(
        couple_body,
        out_shape=jax.ShapeDtypeStruct((BX // 2, BY // 2, MZ), jnp.float32),
        in_specs=[vmem] * 3,
        out_specs=vmem,
        compiler_params=pltpu.CompilerParams(vmem_limit_bytes=8 * 1024 * 1024),
        name="add_carries",
    )(own, got, couple)


def ring(n, d):
    return [(i, (i + d) % n) for i in range(n)]


def shift(a, axis, d):
    return lax.ppermute(a, axis, ring(lax.axis_size(axis), d))


def pack_body(margin_hbm, f_hbm, k_hbm, v_hbm, ylo_ref, yhi_ref, xlo_ref, xhi_ref, f_ref, k_ref, v_ref, margin_ref, sems,
              margin_sem):
    f32 = jnp.float32
    bf16 = jnp.bfloat16
    t = BY - W
    margin_copy = pltpu.make_async_copy(margin_hbm, margin_ref, margin_sem)
    margin_copy.start()
    copies = load((f_hbm, k_hbm, v_hbm), (f_ref, k_ref, v_ref), sems)

    def rest(u):
        return u - u.astype(bf16).astype(f32)

    def faces(g, carry):
        tails, heads = [], []
        for i in range(4):
            x = 4 * g + i
            u = f_ref[x]
            tails.append(u[t:])
            heads.append(u[:W])
            ur_t = rest(u[t - 4 :])
            ur_h = rest(u[:8])
            k, v0, v1, v2 = [r.astype(f32) for r in (k_ref[x], v_ref[0, x], v_ref[1, x], v_ref[2, x])]
            ylo_ref[g, i] = jnp.concatenate(
                [k[t:], ur_t[7:8], v0[t + 1 :], v1[t:], ur_t[6:7], v2[t + 1 :]], axis=0
            ).astype(bf16)
            yhi_ref[g, i] = jnp.concatenate(
                [k[:W], v0[: W - 1], ur_h[0:1], v1[:W], v2[: W - 1], ur_h[1:2]], axis=0
            ).astype(bf16)
        ylo_ref[g, 4] = jnp.concatenate(tails, axis=0).astype(bf16)
        yhi_ref[g, 4] = jnp.concatenate(heads, axis=0).astype(bf16)
        return carry

    def x_side(at, out, near, outer):
        for i in range(W):
            out[i] = f_ref[at + i].astype(bf16)
            out[W + i] = k_ref[at + i]
            out[2 * W + i] = v_ref[0, at + i]
            if i == outer:
                out[3 * W + i] = rest(f_ref[at + near[0]]).astype(bf16)
                out[4 * W + i] = rest(f_ref[at + near[1]]).astype(bf16)
            else:
                out[3 * W + i] = v_ref[1, at + i]
                out[4 * W + i] = v_ref[2, at + i]
        half = jnp.zeros((16, NZ), f32)
        out[5 * W] = jnp.concatenate([half + margin_ref[0, 0].astype(f32), half + margin_ref[0, 1].astype(f32)], axis=0).astype(bf16)

    margin_copy.wait()
    for c in range(BX // PACK):
        for copy in copies[c]:
            copy.wait()
        lax.fori_loop(c * PACK // 4, (c + 1) * PACK // 4, faces, 0)
        if c == 0:
            x_side(0, xhi_ref, (0, 1), W - 1)
    x_side(BX - W, xlo_ref, (W - 1, W - 2), 0)


def corner_body(xl_ref, xh_ref, up_ref, down_ref):
    f32 = jnp.float32
    for side, ref in enumerate((xl_ref, xh_ref)):
        for n in range(5):
            planes = [ref[n * W + i].astype(f32) for i in range(W)]
            up_ref[side * 5 + n] = jnp.concatenate([a[BY - W :] for a in planes], axis=0).astype(jnp.bfloat16)
            down_ref[side * 5 + n] = jnp.concatenate([a[:W] for a in planes], axis=0).astype(jnp.bfloat16)


def halo_parts(field, diffusivity, velocity, margin):
    bf16 = jnp.bfloat16
    y_shape = (BX // 4, 5, 16, NZ)
    x_shape = (5 * W + 1, BY, NZ)
    c_shape = (10, 16, NZ)
    vmem = pl.BlockSpec(memory_space=pltpu.VMEM)
    hbm = pl.BlockSpec(memory_space=pltpu.HBM)
    ylo, yhi, xlo, xhi = pl.pallas_call(
        pack_body,
        out_shape=[jax.ShapeDtypeStruct(s, bf16) for s in [y_shape] * 2 + [x_shape] * 2],
        in_specs=[hbm] * 4,
        out_specs=[vmem] * 4,
        scratch_shapes=[pltpu.VMEM(a.shape, a.dtype) for a in (field, diffusivity, velocity)]
        + [pltpu.SMEM(margin.shape, jnp.int32), pltpu.SemaphoreType.DMA((3, BX // PACK)), pltpu.SemaphoreType.DMA(())],
        compiler_params=pltpu.CompilerParams(vmem_limit_bytes=PACK_VMEM * 1024 * 1024),
        name="pack_faces",
    )(*[in_hbm(a) for a in (margin, field, diffusivity, velocity)])
    xl = shift(xlo, "px", 1)
    xh = shift(xhi, "px", -1)
    yl = shift(ylo, "py", 1)
    yh = shift(yhi, "py", -1)
    kept = own_coefficients(field, diffusivity, velocity, ylo)
    xl, xh, kept = lax.optimization_barrier((xl, xh, kept))
    c_up, c_down = pl.pallas_call(
        corner_body,
        out_shape=[jax.ShapeDtypeStruct(c_shape, bf16)] * 2,
        in_specs=[vmem] * 2,
        out_specs=[vmem] * 2,
        compiler_params=pltpu.CompilerParams(vmem_limit_bytes=4 * 1024 * 1024),
        name="pack_corners",
    )(xl, xh)
    halos = (yl, yh, xl, xh, shift(c_up, "py", 1), shift(c_down, "py", -1))
    return halos, kept


def per_device(field, diffusivity, velocity, margin):
    count_x = lax.axis_size("px")
    count_y = lax.axis_size("py")
    fit = jnp.asarray(np.stack(split(fit_matrix(NZ).T)))
    ytab, couple = y_tables(count_y)
    tables = [jnp.asarray(t) for t in x_tables(count_x) + [ytab, couple]]
    halos, kept = halo_parts(field, diffusivity, velocity, margin)
    advected, zt, lo, hi, lo2, hi2, full, couple = time_steps(
        (count_x, count_y), margin, halos, fit, tables, kept[KEPT], kept[:KEPT]
    )
    rows = (zt, shift(lo, "px", 1), shift(hi, "px", -1), shift(lo2, "px", 2), shift(hi2, "px", -2), full)
    own, carries = combine(count_y, rows)
    got = lax.all_to_all(carries, "py", split_axis=0, concat_axis=0, tiled=True)
    return advected, add_carries(own, got, couple)


def solution(mesh):
    placed = (P("px", "py", None), P("px", "py", None), P(None, "px", "py", None), P("px", None))
    return jax.shard_map(
        per_device,
        mesh=mesh,
        in_specs=placed,
        out_specs=(P("px", "py", None), P("px", "py", None)),
        check_vma=False,
    )
```

```python
import functools

import jax
import jax.numpy as jnp
import numpy as np
from jax import lax
from jax.experimental import pallas as pl
from jax.experimental.pallas import tpu as pltpu
from jax.sharding import PartitionSpec as P

STEPS = 4
OVMAX = 4
BX = 64
BY = 32
NZ = 256
MZ = 128
W = 4
EX = BX + 2 * W
EY = BY + 2 * W
YR = BY // 2 + 6
LINES = YR * 128


PACK = 16
PACK_VMEM = 12
STEP_VMEM = 16


def bspline(t):
    m = np.abs(t)
    inner = (4.0 - 6.0 * m * m + 3.0 * m**3) / 6.0
    outer = np.maximum(2.0 - m, 0.0) ** 3 / 6.0
    return np.where(m < 1.0, inner, outer)


def basis(n):
    j = np.arange(n)[:, None]
    k = np.arange(n // 2)[None, :]
    return bspline((j - 2.0 * k - 0.5) / 2.0)


def fit_matrix(n):
    b = basis(n)
    return np.linalg.solve(b.T @ b, b.T)


def split(a):
    a = a.astype(np.float32)
    hi = a.astype(jnp.bfloat16)
    return hi, (a - hi.astype(np.float32)).astype(jnp.bfloat16)


def y_tables(count):
    total = count * BY
    s = fit_matrix(total)
    own = BY // 2
    rows = np.zeros((count, YR, BY))
    couple = np.zeros((count, own, count, 4))
    for q in range(count):
        cols = s[:, q * BY : (q + 1) * BY]
        rows[q, :own] = cols[q * own : (q + 1) * own]
        for at, far, targets in ((own, cols[(q + 1) * own :], range(q + 1, count)), (own + 3, cols[: q * own], range(q))):
            if len(targets) == 0:
                continue
            u, sv, vt = np.linalg.svd(far, full_matrices=False)
            assert sv[3] < 1e-10 * sv[0]
            rows[q, at : at + 3] = vt[:3]
            left = (u[:, :3] * sv[:3]).reshape(len(targets), own, 3)
            for i, t in enumerate(targets):
                couple[t, :, q, :3] = left[i]
                couple[t, :, q, 3] = left[i, :, 0]
    table = np.einsum("qry,xw->qrxwy", rows, np.eye(8)).reshape(count, YR * 8, 8 * BY)
    spaced = np.einsum("qmtc,xw->qxmtwc", couple, np.eye(8)).reshape(count, own * 8, count * 32)
    return np.stack(split(table), axis=1), np.stack(split(spaced), axis=1)


def x_tables(count):
    total = count * BX
    block = BX // 2
    ctrl = total // 2
    b = basis(total)
    width = block + 2 * OVMAX
    gpad = np.zeros((ctrl + 16, ctrl + 16))
    gpad[8:-8, 8:-8] = b.T @ b
    bt = bspline((np.arange(BX)[None] - 2.0 * (np.arange(block + 4)[:, None] - 2) - 0.5) / 2.0)
    base, send, near = [], [], []
    for cls, p in enumerate((0, 1, count - 1)):
        has_low = float(cls != 0)
        has_high = float(cls != 2)
        start = p * block
        knots = start - OVMAX + np.arange(width)
        lo = start - OVMAX + 8
        full = gpad[lo : lo + width, lo : lo + width]
        band = gpad[lo : lo + width, lo - 3 : lo + width + 3]
        for m0 in range(OVMAX + 1):
            for m1 in range(OVMAX + 1):
                inside = (knots >= start - m0) & (knots < start + block + m1) & (knots >= 0) & (knots < ctrl)
                w = inside.astype(np.float64)
                mat = full * w[:, None] * w[None, :] + np.diag(1.0 - w)
                e = (np.linalg.inv(mat) * w[None, :])[OVMAX : OVMAX + block]
                q = e @ band
                ql = q[:, :7] * has_low
                qr = q[:, 7 + block :] * has_high
                two = 2.0 * e - q[:, 7 : 7 + block] @ e
                low = two[:, 0:6] * has_low
                high = two[:, block + 2 :] * has_high
                gap3 = np.zeros((block, 3))
                gap32 = np.zeros((block, 32))
                base.append(np.concatenate([two[:, 2 : block + 6] @ bt, low, -ql, gap3, high, -qr, gap3, gap32], axis=1))
                pad = np.zeros((3, BX))
                send.append(
                    np.concatenate(
                        [bt[block - 2 :], e[block - 7 :, 2 : block + 6] @ bt, pad, bt[:6], e[:7, 2 : block + 6] @ bt, pad]
                    )
                )
                both = np.zeros((2, 8, 128))
                both[0, :7, :BX] = e[block - 7 :, block + 2 :] @ bt[0:6]
                both[0, :7, 96:102] = e[block - 7 :, 0:6] * has_low
                both[1, :7, :BX] = e[:7, 0:6] @ bt[block - 2 :]
                both[1, :7, 112:118] = e[:7, block + 2 :] * has_high
                near.append(both)
    return [np.stack(t).astype(np.float32) for t in (base, send, near)]


def z_shifts(rows):
    lane = lax.broadcasted_iota(jnp.int32, (rows, 128), 1)
    first = lane == 0
    final = lane == 127

    def z_up(a):
        lo = pltpu.roll(a[:, :128], 1, 1)
        hi = pltpu.roll(a[:, 128:], 1, 1)
        return jnp.concatenate([jnp.where(first, 0.0, lo), jnp.where(first, lo, hi)], axis=1)

    def z_down(a):
        lo = pltpu.roll(a[:, :128], 127, 1)
        hi = pltpu.roll(a[:, 128:], 127, 1)
        return jnp.concatenate([jnp.where(final, hi, lo), jnp.where(final, 0.0, hi)], axis=1)

    return z_up, z_down


def own_rows(k, kx_low, kx, refs, x):
    kx_s, ky_s, kyd_s, kz_s, kzd_s, c_s = refs
    z_up, z_down = z_shifts(BY)
    row = lax.broadcasted_iota(jnp.int32, (BY, NZ), 0)
    own = slice(0, BY)
    ky = jnp.where(row < BY - 1, 0.05 * (k + pltpu.roll(k, BY - 1, 0)), 0.0)
    kyd = pltpu.roll(ky, 1, 0)
    kz = 0.05 * (k + z_down(k))
    kzd = 0.05 * (k + z_up(k))
    kx_s[x, own] = kx
    ky_s[x, own] = ky
    kyd_s[x, own] = kyd
    kz_s[x, own] = kz
    kzd_s[x, own] = kzd
    c_s[x, own] = 1.0 - ((kx + kx_low) + (ky + kyd) + (kz + kzd))


def load(sources, targets, sems):
    copies = []
    for c in range(BX // PACK):
        part = pl.ds(c * PACK, PACK)
        copies.append([])
        for n, (src, dst) in enumerate(zip(sources, targets)):
            at = (slice(None), part) if len(src.shape) == 4 else (part,)
            copies[-1].append(pltpu.make_async_copy(src.at[at], dst.at[at], sems.at[n, c]))
            copies[-1][-1].start()
    return copies


def own_body(f_hbm, k_hbm, v_hbm, after_ref, u_s, v0_s, v1_s, v2_s, kx_s, ky_s, kyd_s, kz_s, kzd_s, c_s, edge_s, end_ref,
             f_ref, k_ref, v_ref, sems):
    f32 = jnp.float32
    for part in load((f_hbm, k_hbm, v_hbm), (f_ref, k_ref, v_ref), sems):
        for copy in part:
            copy.wait()
    refs = (kx_s, ky_s, kyd_s, kz_s, kzd_s, c_s)

    def plane(x, carry):
        k, kx_low = carry
        k_next = k_ref[jnp.minimum(x + 1, BX - 1)].astype(f32)
        kx = jnp.where(x < BX - 1, 0.05, 0.0) * (k + k_next)
        u_s[x + W, 0:BY] = f_ref[x]
        for n, ref in enumerate((v0_s, v1_s, v2_s)):
            ref[x + W, 0:BY] = v_ref[n, x].astype(f32)
        edge_s[x + W, 0:8] = k[0:8]
        edge_s[x + W, 8:16] = k[BY - 8 :]
        own_rows(k, kx_low, kx, refs, x + W)
        return k_next, kx

    lax.fori_loop(0, BX, plane, (k_ref[0].astype(f32), jnp.zeros((BY, NZ), f32)), unroll=4)
    end_ref[0] = k_ref[0].astype(f32)
    end_ref[1] = k_ref[BX - 1].astype(f32)


def x_planes_body(count_x, xl_ref, xh_ref, end_ref, *rest_refs):
    f32 = jnp.float32
    u_s, v0_s, v1_s, v2_s, kx_s, ky_s, kyd_s, kz_s, kzd_s, c_s, edge_s = rest_refs[KEPT : 2 * KEPT]
    kp_s = rest_refs[2 * KEPT]
    refs = (kx_s, ky_s, kyd_s, kz_s, kzd_s, c_s)
    p = lax.axis_index("px")
    from_low_x = jnp.where(p > 0, 1.0, 0.0)
    from_high_x = jnp.where(p < count_x - 1, 1.0, 0.0)
    dest = (u_s, None, v0_s, v1_s, v2_s)
    for n in range(5):
        for base, ref, scale, near, outer in (
            (0, xl_ref, from_low_x, (W - 1, W - 2), 0),
            (BX + W, xh_ref, from_high_x, (0, 1), W - 1),
        ):
            for i in range(W):
                value = ref[n * W + i].astype(f32)
                if n == 0 and i in near:
                    value = value + ref[(3 + near.index(i)) * W + outer].astype(f32)
                value = value * scale
                if n == 1:
                    kp_s[base % BX + i] = value
                    edge_s[base + i, 0:8] = value[0:8]
                    edge_s[base + i, 8:16] = value[BY - 8 :]
                else:
                    dest[n][base + i, 0:BY] = value

    kx_low = jnp.zeros((BY, NZ), f32)
    for i in range(W):
        k = kp_s[i]
        kx = 0.05 * (k + (kp_s[i + 1] if i < W - 1 else end_ref[0]))
        own_rows(k, kx_low, kx, refs, i)
        kx_low = kx
    c_s[W, 0:BY] = c_s[W, 0:BY] - kx_low
    kx_low = 0.05 * (end_ref[1] + kp_s[W])
    kx_s[BX + W - 1, 0:BY] = kx_low
    c_s[BX + W - 1, 0:BY] = c_s[BX + W - 1, 0:BY] - kx_low
    for i in range(W):
        k = kp_s[W + i]
        kx = 0.05 * (k + kp_s[min(W + i + 1, 2 * W - 1)])
        own_rows(k, kx_low, kx, refs, BX + W + i)
        kx_low = kx


def dot3(a, b):
    dot = functools.partial(jnp.dot, preferred_element_type=jnp.float32)
    return dot(a[0], b[0]) + (dot(a[0], b[1]) + dot(a[1], b[0]))


def halves(a):
    hi = a.astype(jnp.bfloat16)
    return hi, (a - hi.astype(jnp.float32)).astype(jnp.bfloat16)


def place_of(owner, count, m0, m1):
    own = jnp.clip(owner, 0, count - 1)
    cls = jnp.where(own == 0, 0, jnp.where(own == count - 1, 2, 1))
    n = OVMAX + 1
    return (cls * n + jnp.clip(m0, 0, OVMAX)) * n + jnp.clip(m1, 0, OVMAX)


def stencil_body(count_x, count_y, margin_ref, yl_ref, yh_ref, xl_ref, xh_ref, cl_ref, ch_ref, fit_ref, base_hbm, send_hbm,
                 near_hbm, ytab_hbm, couple_hbm,
                 *rest_refs):
    f32 = jnp.float32
    outs = rest_refs[KEPT:]
    adv_hbm, zt_ref, lo_ref, hi_ref, lo2_ref, hi2_ref, full_ref, couple_ref = outs[:8]
    u_s, v0_s, v1_s, v2_s, kx_s, ky_s, kyd_s, kz_s, kzd_s, c_s, edge_s = outs[8 : 8 + KEPT]
    kh_s, base_s, send_s, near_s, ytab_s, sems = outs[8 + KEPT :]
    p = lax.axis_index("px")
    q = lax.axis_index("py")

    def margins(ref):
        part = ref[5 * W].astype(f32)
        return [jnp.max(a).astype(jnp.int32) for a in (part[0:8], part[16:24])]

    mine = place_of(p, count_x, margin_ref[0, 0], margin_ref[0, 1])
    low = place_of(p - 1, count_x, *margins(xl_ref))
    high = place_of(p + 1, count_x, *margins(xh_ref))
    copies = [
        pltpu.make_async_copy(base_hbm.at[mine], base_s, sems.at[0]),
        pltpu.make_async_copy(send_hbm.at[mine], send_s, sems.at[1]),
        pltpu.make_async_copy(near_hbm.at[low, 0], near_s.at[0], sems.at[2]),
        pltpu.make_async_copy(near_hbm.at[high, 1], near_s.at[1], sems.at[3]),
        pltpu.make_async_copy(ytab_hbm.at[q], ytab_s, sems.at[4]),
        pltpu.make_async_copy(couple_hbm.at[q], couple_ref, sems.at[5]),
    ]
    for copy in copies:
        copy.start()
    refs = (kx_s, ky_s, kyd_s, kz_s, kzd_s, c_s)
    from_low_x = jnp.where(p > 0, 1.0, 0.0)
    from_high_x = jnp.where(p < count_x - 1, 1.0, 0.0)
    from_low_y = jnp.where(q > 0, 1.0, 0.0)
    from_high_y = jnp.where(q < count_y - 1, 1.0, 0.0)
    beyond = slice(BY, EY)

    def halo_rows(group, carry):
        at = group * 4
        ul = yl_ref[group, 4].astype(f32) * from_low_y
        uh = yh_ref[group, 4].astype(f32) * from_high_y
        gap = jnp.zeros((4, NZ), f32)
        for i in range(4):
            x = at + i + W
            kl = yl_ref[group, i].astype(f32) * from_low_y
            kh = yh_ref[group, i].astype(f32) * from_high_y
            rest = jnp.concatenate([kh[7:8], kh[15:16], gap, kl[12:13], kl[4:5]], axis=0)
            u_s[x, beyond] = rest + jnp.concatenate([uh[4 * i : 4 * i + 4], ul[4 * i : 4 * i + 4]], axis=0)
            kh_s[x] = jnp.concatenate([kh[0:4], kl[0:4]], axis=0)
            for n, ref in enumerate((v0_s, v1_s, v2_s)):
                m = 4 * n + 4
                ref[x, beyond] = jnp.concatenate([kh[m : m + 4], kl[m : m + 4]], axis=0)
        return carry

    lax.fori_loop(0, BX // 4, halo_rows, 0)
    dest = (u_s, kh_s, v0_s, v1_s, v2_s)
    for n in range(5):
        at = slice(0, 8) if n == 1 else beyond
        for base, corner, scale in ((0, 0, from_low_x), (BX + W, 5, from_high_x)):
            low = cl_ref[corner + n].astype(f32) * (scale * from_low_y)
            high = ch_ref[corner + n].astype(f32) * (scale * from_high_y)
            for i in range(W):
                tile = jnp.concatenate([high[4 * i : 4 * i + 4], low[4 * i : 4 * i + 4]], axis=0)
                dest[n][base + i, at] = tile

    sub = lax.broadcasted_iota(jnp.int32, (8, NZ), 0)
    zt_up, zt_down = z_shifts(8)

    def halo_coefficients(x, carry):
        k, kx_low = carry
        k_next = kh_s[jnp.minimum(x + 1, EX - 1)]
        kx = 0.05 * (k + k_next)
        up = 0.05 * (edge_s[x, 8:16] + pltpu.roll(k, 7, 0))
        down = 0.05 * (edge_s[x, 0:8] + pltpu.roll(k, 1, 0))
        up = jnp.where(sub == 7, up, 0.0)
        down = jnp.where(sub == 0, down, 0.0)
        ky = jnp.where(sub == 7, pltpu.roll(down, 7, 0), 0.05 * (k + pltpu.roll(k, 7, 0)))
        kyd = jnp.where(sub == 0, pltpu.roll(up, 1, 0), pltpu.roll(ky, 1, 0))
        kz = 0.05 * (k + zt_down(k))
        kzd = 0.05 * (k + zt_up(k))
        kx_s[x, beyond] = kx
        ky_s[x, beyond] = ky
        kyd_s[x, beyond] = kyd
        kz_s[x, beyond] = kz
        kzd_s[x, beyond] = kzd
        c_s[x, beyond] = 1.0 - ((kx + kx_low) + (ky + kyd) + (kz + kzd))
        ky_s[x, BY - 8 : BY] = ky_s[x, BY - 8 : BY] + up
        kyd_s[x, 0:8] = kyd_s[x, 0:8] + down
        c_s[x, 0:8] = c_s[x, 0:8] - down
        c_s[x, BY - 8 : BY] = c_s[x, BY - 8 : BY] - up
        return k_next, kx

    lax.fori_loop(0, EX, halo_coefficients, (kh_s[0], jnp.zeros((8, NZ), f32)), unroll=8)

    row = lax.broadcasted_iota(jnp.int32, (EY, NZ), 0)
    row_mask = jnp.where(row < BY, 1.0, jnp.where(row < BY + W, from_high_y, from_low_y))

    for step in range(STEPS):
        lo = step
        hi = EX - 1 - step

        rows = EY if step < STEPS - 1 else BY
        z_up, z_down = z_shifts(rows)

        def one_plane(x, carry, rows=rows, z_up=z_up, z_down=z_down):
            partial, up = carry
            full = u_s[x]
            w = 0.025 * full
            g1 = v1_s[x] * w
            y_part = pltpu.roll(full * (ky_s[x] + g1), 1, 0) + pltpu.roll(full * (kyd_s[x] - g1), EY - 1, 0)
            u = full[:rows]
            g0 = v0_s[x, 0:rows] * w[:rows]
            g2 = v2_s[x, 0:rows] * w[:rows]
            prev = x - 1
            done = partial + u * (kx_s[prev, 0:rows] - g0)
            if rows == EY:
                plane_mask = jnp.where(prev < W, from_low_x, jnp.where(prev >= BX + W, from_high_x, 1.0))
                done = done * (row_mask * plane_mask)
            u_s[prev, 0:rows] = done
            up_next = u * (kx_s[x, 0:rows] + g0)
            total = u * c_s[x, 0:rows] + up + y_part[:rows]
            total = total + z_up(u * (kz_s[x, 0:rows] + g2))
            total = total + z_down(u * (kzd_s[x, 0:rows] - g2))
            return total, up_next

        first_u = u_s[lo, 0:rows]
        first_up = first_u * (kx_s[lo, 0:rows] + v0_s[lo, 0:rows] * (0.025 * first_u))
        lax.fori_loop(lo + 1, hi + 1, one_plane, (jnp.zeros((rows, NZ), f32), first_up), unroll=4)

    result = pltpu.make_async_copy(u_s.at[pl.ds(W, BX), pl.ds(0, BY)], adv_hbm, sems.at[6])
    result.start()
    for copy in copies:
        copy.wait()
    fit = (fit_ref[0], fit_ref[1])
    ytab = (ytab_s[0], ytab_s[1])

    def fit_planes(group, carry):
        at = pl.multiple_of(group * 8, 8)
        part = u_s[pl.ds(at + W, 8), 0:BY]
        rows = dot3(ytab, halves(part.reshape(8 * BY, NZ)))
        rows = dot3(halves(rows), fit)
        for r in range(YR):
            zt_ref[r, pl.ds(at, 8)] = rows[8 * r : 8 * r + 8]
        return carry

    lax.fori_loop(0, BX // 8, fit_planes, 0, unroll=8)

    send = halves(send_s[...])
    for r in range(0, YR, 2):
        lines = slice(r * MZ, (r + 2) * MZ)
        rows = dot3(send, halves(jnp.concatenate([zt_ref[r], zt_ref[r + 1]], axis=1)))
        lo_ref[:, lines] = rows[0:16]
        hi_ref[:, lines] = rows[16:32]
        lo2_ref[:, lines] = rows[0:16].astype(jnp.bfloat16)
        hi2_ref[:, lines] = rows[16:32].astype(jnp.bfloat16)
    base = base_s[...]
    full = base
    for j in range(7):
        full = full + base[:, 70 + j : 71 + j] * near_s[0, j : j + 1, :]
        full = full + base[:, 86 + j : 87 + j] * near_s[1, j : j + 1, :]
    full_ref[...] = full
    result.wait()


def combine_body(zt_ref, lo_ref, hi_ref, lo2_ref, hi2_ref, full_ref, own_ref, carry_ref):
    f32 = jnp.float32
    q = lax.axis_index("py")
    full = halves(full_ref[...])

    def stack(first, last):
        lines = slice(first * MZ, last * MZ)
        return jnp.concatenate(
            [jnp.concatenate([zt_ref[r] for r in range(first, last)], axis=1), lo_ref[:, lines], hi_ref[:, lines]]
            + [ref[:, lines].astype(f32) for ref in (lo2_ref, hi2_ref)],
            axis=0,
        )

    own = BY // 2
    for r in range(0, own, 2):
        out = dot3(full, halves(stack(r, r + 2)))
        for i in range(2):
            own_ref[:, r + i, :] = out[:, i * MZ : (i + 1) * MZ]

    block = BX // 2
    part = lax.broadcasted_iota(jnp.int32, (4 * block, 128), 0) % 4
    spread = lax.broadcasted_iota(jnp.int32, (4 * block, block), 0) // 4
    spread = jnp.where(spread == lax.broadcasted_iota(jnp.int32, (4 * block, block), 1), 1.0, 0.0).astype(jnp.bfloat16)
    spaced = []
    for f in full:
        rows = jnp.dot(spread, f, preferred_element_type=f32)
        spaced.append(
            jnp.concatenate(
                [jnp.where(part % 3 == 0, rows, 0.0), jnp.where(part == 1, rows, 0.0), jnp.where(part == 2, rows, 0.0)],
                axis=1,
            ).astype(jnp.bfloat16)
        )
    carries = stack(own, YR)
    carries = jnp.concatenate(
        [jnp.concatenate([carries[:, n * MZ : (n + 1) * MZ], carries[:, (n + 3) * MZ : (n + 4) * MZ]], axis=1) for n in range(3)],
        axis=0,
    )
    carries = dot3(spaced, halves(carries))
    coded = []
    for n in range(2):
        value = carries[:, n * MZ : (n + 1) * MZ]
        head = value.astype(jnp.bfloat16).astype(f32)
        coded.append(jnp.where(part == 3, value - head, value).astype(jnp.bfloat16))
    for t in range(carry_ref.shape[0]):

        @pl.when(t > q)
        def _():
            carry_ref[t] = coded[0]

        @pl.when(t <= q)
        def _():
            carry_ref[t] = coded[1]


def couple_body(own_ref, got_ref, couple_ref, out_ref):
    dot = functools.partial(jnp.dot, preferred_element_type=jnp.float32)
    head = couple_ref[0]
    rest = couple_ref[1]
    for x in range(0, BX // 2, 8):
        got = got_ref[:, 4 * x : 4 * x + 32].reshape(-1, MZ)
        out_ref[x : x + 8] = own_ref[x : x + 8] + (dot(head, got) + dot(rest, got)).reshape(8, BY // 2, MZ)


KEPT = 11


def in_hbm(a):
    return pltpu.with_memory_space_constraint(a, pltpu.HBM)


def own_coefficients(field, diffusivity, velocity, after):
    vmem = pl.BlockSpec(memory_space=pltpu.VMEM)
    f32 = jnp.float32
    return pl.pallas_call(
        own_body,
        out_shape=[pltpu.VMEM((EX, EY, NZ), f32)] * (KEPT - 1)
        + [pltpu.VMEM((EX, 16, NZ), f32), pltpu.VMEM((2, BY, NZ), f32)],
        in_specs=[pl.BlockSpec(memory_space=pltpu.HBM)] * 3 + [pl.BlockSpec(memory_space=pl.ANY)],
        out_specs=[vmem] * (KEPT + 1),
        scratch_shapes=[pltpu.VMEM(a.shape, a.dtype) for a in (field, diffusivity, velocity)]
        + [pltpu.SemaphoreType.DMA((3, BX // PACK))],
        compiler_params=pltpu.CompilerParams(vmem_limit_bytes=12 * 1024 * 1024),
        name="own_coefficients",
    )(*[in_hbm(a) for a in (field, diffusivity, velocity)], after)


def x_planes(count_x, xl, xh, end, kept):
    vmem = pl.BlockSpec(memory_space=pltpu.VMEM)
    f32 = jnp.float32
    return pl.pallas_call(
        functools.partial(x_planes_body, count_x),
        out_shape=[pltpu.VMEM(a.shape, f32) for a in kept],
        in_specs=[vmem] * (3 + KEPT),
        out_specs=[vmem] * KEPT,
        input_output_aliases={3 + i: i for i in range(KEPT)},
        scratch_shapes=[pltpu.VMEM((2 * W, BY, NZ), f32)],
        compiler_params=pltpu.CompilerParams(vmem_limit_bytes=8 * 1024 * 1024),
        name="x_planes",
    )(xl, xh, end, *kept)


def time_steps(counts, margin, halos, fit, tables, kept):
    vmem = pl.BlockSpec(memory_space=pltpu.VMEM)
    smem = pl.BlockSpec(memory_space=pltpu.SMEM)
    hbm = pl.BlockSpec(memory_space=pltpu.HBM)
    f32 = jnp.float32
    bf16 = jnp.bfloat16
    shapes = [((BX, BY, NZ), f32), ((YR, BX, MZ), f32)] + [((16, LINES), f32)] * 2 + [((16, LINES), bf16)] * 2
    shapes += [((BX // 2, 128), f32)]
    return pl.pallas_call(
        functools.partial(stencil_body, *counts),
        out_shape=[jax.ShapeDtypeStruct(s, t) for s, t in shapes]
        + [pltpu.VMEM(tables[-1].shape[1:], bf16)]
        + [pltpu.VMEM(a.shape, f32) for a in kept],
        in_specs=[smem] + [vmem] * 7 + [hbm] * 5 + [vmem] * KEPT,
        out_specs=[hbm] + [vmem] * (7 + KEPT),
        input_output_aliases={13 + i: 8 + i for i in range(KEPT)},
        scratch_shapes=[
            pltpu.VMEM((EX, 8, NZ), f32),
            pltpu.VMEM((BX // 2, 128), f32),
            pltpu.VMEM((BX // 2, BX), f32),
            pltpu.VMEM((2, 8, 128), f32),
            pltpu.VMEM((2, YR * 8, 8 * BY), bf16),
            pltpu.SemaphoreType.DMA((7,)),
        ],
        compiler_params=pltpu.CompilerParams(vmem_limit_bytes=STEP_VMEM * 1024 * 1024),
        name="time_steps",
    )(margin, *halos, fit, *[in_hbm(t) for t in tables], *kept)[:8]


def combine(count_y, rows):
    vmem = pl.BlockSpec(memory_space=pltpu.VMEM)
    return pl.pallas_call(
        combine_body,
        out_shape=[
            jax.ShapeDtypeStruct((BX // 2, BY // 2, MZ), jnp.float32),
            jax.ShapeDtypeStruct((count_y, 2 * BX, MZ), jnp.bfloat16),
        ],
        in_specs=[vmem] * 6,
        out_specs=[vmem] * 2,
        compiler_params=pltpu.CompilerParams(vmem_limit_bytes=12 * 1024 * 1024),
        name="combine",
    )(*rows)


def add_carries(own, got, couple):
    vmem = pl.BlockSpec(memory_space=pltpu.VMEM)
    return pl.pallas_call(
        couple_body,
        out_shape=jax.ShapeDtypeStruct((BX // 2, BY // 2, MZ), jnp.float32),
        in_specs=[vmem] * 3,
        out_specs=vmem,
        compiler_params=pltpu.CompilerParams(vmem_limit_bytes=8 * 1024 * 1024),
        name="add_carries",
    )(own, got, couple)


def ring(n, d):
    return [(i, (i + d) % n) for i in range(n)]


def shift(a, axis, d):
    return lax.ppermute(a, axis, ring(lax.axis_size(axis), d))


def pack_body(margin_hbm, f_hbm, k_hbm, v_hbm, ylo_ref, yhi_ref, xlo_ref, xhi_ref, f_ref, k_ref, v_ref, margin_ref, sems,
              margin_sem):
    f32 = jnp.float32
    bf16 = jnp.bfloat16
    t = BY - W
    margin_copy = pltpu.make_async_copy(margin_hbm, margin_ref, margin_sem)
    margin_copy.start()
    copies = load((f_hbm, k_hbm, v_hbm), (f_ref, k_ref, v_ref), sems)

    def rest(u):
        return u - u.astype(bf16).astype(f32)

    def faces(g, carry):
        tails, heads = [], []
        for i in range(4):
            x = 4 * g + i
            u = f_ref[x]
            tails.append(u[t:])
            heads.append(u[:W])
            ur_t = rest(u[t - 4 :])
            ur_h = rest(u[:8])
            k, v0, v1, v2 = [r.astype(f32) for r in (k_ref[x], v_ref[0, x], v_ref[1, x], v_ref[2, x])]
            ylo_ref[g, i] = jnp.concatenate(
                [k[t:], ur_t[7:8], v0[t + 1 :], v1[t:], ur_t[6:7], v2[t + 1 :]], axis=0
            ).astype(bf16)
            yhi_ref[g, i] = jnp.concatenate(
                [k[:W], v0[: W - 1], ur_h[0:1], v1[:W], v2[: W - 1], ur_h[1:2]], axis=0
            ).astype(bf16)
        ylo_ref[g, 4] = jnp.concatenate(tails, axis=0).astype(bf16)
        yhi_ref[g, 4] = jnp.concatenate(heads, axis=0).astype(bf16)
        return carry

    def x_side(at, out, near, outer):
        for i in range(W):
            out[i] = f_ref[at + i].astype(bf16)
            out[W + i] = k_ref[at + i]
            out[2 * W + i] = v_ref[0, at + i]
            if i == outer:
                out[3 * W + i] = rest(f_ref[at + near[0]]).astype(bf16)
                out[4 * W + i] = rest(f_ref[at + near[1]]).astype(bf16)
            else:
                out[3 * W + i] = v_ref[1, at + i]
                out[4 * W + i] = v_ref[2, at + i]
        half = jnp.zeros((16, NZ), f32)
        out[5 * W] = jnp.concatenate([half + margin_ref[0, 0].astype(f32), half + margin_ref[0, 1].astype(f32)], axis=0).astype(bf16)

    margin_copy.wait()
    for c in range(BX // PACK):
        for copy in copies[c]:
            copy.wait()
        lax.fori_loop(c * PACK // 4, (c + 1) * PACK // 4, faces, 0)
        if c == 0:
            x_side(0, xhi_ref, (0, 1), W - 1)
    x_side(BX - W, xlo_ref, (W - 1, W - 2), 0)


def corner_body(xl_ref, xh_ref, up_ref, down_ref):
    f32 = jnp.float32
    for side, ref in enumerate((xl_ref, xh_ref)):
        for n in range(5):
            planes = [ref[n * W + i].astype(f32) for i in range(W)]
            up_ref[side * 5 + n] = jnp.concatenate([a[BY - W :] for a in planes], axis=0).astype(jnp.bfloat16)
            down_ref[side * 5 + n] = jnp.concatenate([a[:W] for a in planes], axis=0).astype(jnp.bfloat16)


def halo_parts(field, diffusivity, velocity, margin):
    bf16 = jnp.bfloat16
    y_shape = (BX // 4, 5, 16, NZ)
    x_shape = (5 * W + 1, BY, NZ)
    c_shape = (10, 16, NZ)
    vmem = pl.BlockSpec(memory_space=pltpu.VMEM)
    hbm = pl.BlockSpec(memory_space=pltpu.HBM)
    ylo, yhi, xlo, xhi = pl.pallas_call(
        pack_body,
        out_shape=[jax.ShapeDtypeStruct(s, bf16) for s in [y_shape] * 2 + [x_shape] * 2],
        in_specs=[hbm] * 4,
        out_specs=[vmem] * 4,
        scratch_shapes=[pltpu.VMEM(a.shape, a.dtype) for a in (field, diffusivity, velocity)]
        + [pltpu.SMEM(margin.shape, jnp.int32), pltpu.SemaphoreType.DMA((3, BX // PACK)), pltpu.SemaphoreType.DMA(())],
        compiler_params=pltpu.CompilerParams(vmem_limit_bytes=PACK_VMEM * 1024 * 1024),
        name="pack_faces",
    )(*[in_hbm(a) for a in (margin, field, diffusivity, velocity)])
    xl = shift(xlo, "px", 1)
    xh = shift(xhi, "px", -1)
    yl = shift(ylo, "py", 1)
    yh = shift(yhi, "py", -1)
    kept = own_coefficients(field, diffusivity, velocity, ylo)
    xl, xh, kept = lax.optimization_barrier((xl, xh, kept))
    c_up, c_down = pl.pallas_call(
        corner_body,
        out_shape=[jax.ShapeDtypeStruct(c_shape, bf16)] * 2,
        in_specs=[vmem] * 2,
        out_specs=[vmem] * 2,
        compiler_params=pltpu.CompilerParams(vmem_limit_bytes=4 * 1024 * 1024),
        name="pack_corners",
    )(xl, xh)
    halos = (yl, yh, xl, xh, shift(c_up, "py", 1), shift(c_down, "py", -1))
    _, kept = lax.optimization_barrier((c_up, kept))
    return halos, x_planes(lax.axis_size("px"), xl, xh, kept[KEPT], kept[:KEPT])


def per_device(field, diffusivity, velocity, margin):
    count_x = lax.axis_size("px")
    count_y = lax.axis_size("py")
    fit = jnp.asarray(np.stack(split(fit_matrix(NZ).T)))
    ytab, couple = y_tables(count_y)
    tables = [jnp.asarray(t) for t in x_tables(count_x) + [ytab, couple]]
    halos, kept = halo_parts(field, diffusivity, velocity, margin)
    advected, zt, lo, hi, lo2, hi2, full, couple = time_steps(
        (count_x, count_y), margin, halos, fit, tables, kept
    )
    rows = (zt, shift(lo, "px", 1), shift(hi, "px", -1), shift(lo2, "px", 2), shift(hi2, "px", -2), full)
    own, carries = combine(count_y, rows)
    got = lax.all_to_all(carries, "py", split_axis=0, concat_axis=0, tiled=True)
    return advected, add_carries(own, got, couple)


def solution(mesh):
    placed = (P("px", "py", None), P("px", "py", None), P(None, "px", "py", None), P("px", None))
    return jax.shard_map(
        per_device,
        mesh=mesh,
        in_specs=placed,
        out_specs=(P("px", "py", None), P("px", "py", None)),
        check_vma=False,
    )
```

```python
import functools

import jax
import jax.numpy as jnp
import numpy as np
from jax import lax
from jax.experimental import pallas as pl
from jax.experimental.pallas import tpu as pltpu
from jax.sharding import PartitionSpec as P

STEPS = 4
OVMAX = 4
BX = 64
BY = 32
NZ = 256
MZ = 128
W = 4
EX = BX + 2 * W
EY = BY + 2 * W
YR = BY // 2 + 6
LINES = YR * 128


PACK = 16
PACK_VMEM = 12
STEP_VMEM = 16


def bspline(t):
    m = np.abs(t)
    inner = (4.0 - 6.0 * m * m + 3.0 * m**3) / 6.0
    outer = np.maximum(2.0 - m, 0.0) ** 3 / 6.0
    return np.where(m < 1.0, inner, outer)


def basis(n):
    j = np.arange(n)[:, None]
    k = np.arange(n // 2)[None, :]
    return bspline((j - 2.0 * k - 0.5) / 2.0)


def fit_matrix(n):
    b = basis(n)
    return np.linalg.solve(b.T @ b, b.T)


def split(a):
    a = a.astype(np.float32)
    hi = a.astype(jnp.bfloat16)
    return hi, (a - hi.astype(np.float32)).astype(jnp.bfloat16)


def y_tables(count):
    total = count * BY
    s = fit_matrix(total)
    own = BY // 2
    rows = np.zeros((count, YR, BY))
    couple = np.zeros((count, own, count, 4))
    for q in range(count):
        cols = s[:, q * BY : (q + 1) * BY]
        rows[q, :own] = cols[q * own : (q + 1) * own]
        for at, far, targets in ((own, cols[(q + 1) * own :], range(q + 1, count)), (own + 3, cols[: q * own], range(q))):
            if len(targets) == 0:
                continue
            u, sv, vt = np.linalg.svd(far, full_matrices=False)
            assert sv[3] < 1e-10 * sv[0]
            rows[q, at : at + 3] = vt[:3]
            left = (u[:, :3] * sv[:3]).reshape(len(targets), own, 3)
            for i, t in enumerate(targets):
                couple[t, :, q, :3] = left[i]
                couple[t, :, q, 3] = left[i, :, 0]
    table = np.einsum("qry,xw->qrxwy", rows, np.eye(8)).reshape(count, YR * 8, 8 * BY)
    spaced = np.einsum("qmtc,xw->qxmtwc", couple, np.eye(8)).reshape(count, own * 8, count * 32)
    return np.stack(split(table), axis=1), np.stack(split(spaced), axis=1)


def x_tables(count):
    total = count * BX
    block = BX // 2
    ctrl = total // 2
    b = basis(total)
    width = block + 2 * OVMAX
    gpad = np.zeros((ctrl + 16, ctrl + 16))
    gpad[8:-8, 8:-8] = b.T @ b
    bt = bspline((np.arange(BX)[None] - 2.0 * (np.arange(block + 4)[:, None] - 2) - 0.5) / 2.0)
    base, send, near = [], [], []
    for cls, p in enumerate((0, 1, count - 1)):
        has_low = float(cls != 0)
        has_high = float(cls != 2)
        start = p * block
        knots = start - OVMAX + np.arange(width)
        lo = start - OVMAX + 8
        full = gpad[lo : lo + width, lo : lo + width]
        band = gpad[lo : lo + width, lo - 3 : lo + width + 3]
        for m0 in range(OVMAX + 1):
            for m1 in range(OVMAX + 1):
                inside = (knots >= start - m0) & (knots < start + block + m1) & (knots >= 0) & (knots < ctrl)
                w = inside.astype(np.float64)
                mat = full * w[:, None] * w[None, :] + np.diag(1.0 - w)
                e = (np.linalg.inv(mat) * w[None, :])[OVMAX : OVMAX + block]
                q = e @ band
                ql = q[:, :7] * has_low
                qr = q[:, 7 + block :] * has_high
                two = 2.0 * e - q[:, 7 : 7 + block] @ e
                low = two[:, 0:6] * has_low
                high = two[:, block + 2 :] * has_high
                gap3 = np.zeros((block, 3))
                gap32 = np.zeros((block, 32))
                base.append(np.concatenate([two[:, 2 : block + 6] @ bt, low, -ql, gap3, high, -qr, gap3, gap32], axis=1))
                pad = np.zeros((3, BX))
                send.append(
                    np.concatenate(
                        [bt[block - 2 :], e[block - 7 :, 2 : block + 6] @ bt, pad, bt[:6], e[:7, 2 : block + 6] @ bt, pad]
                    )
                )
                both = np.zeros((2, 8, 128))
                both[0, :7, :BX] = e[block - 7 :, block + 2 :] @ bt[0:6]
                both[0, :7, 96:102] = e[block - 7 :, 0:6] * has_low
                both[1, :7, :BX] = e[:7, 0:6] @ bt[block - 2 :]
                both[1, :7, 112:118] = e[:7, block + 2 :] * has_high
                near.append(both)
    return [np.stack(t).astype(np.float32) for t in (base, send, near)]


def z_shifts(rows):
    lane = lax.broadcasted_iota(jnp.int32, (rows, 128), 1)
    first = lane == 0
    final = lane == 127

    def z_up(a):
        lo = pltpu.roll(a[:, :128], 1, 1)
        hi = pltpu.roll(a[:, 128:], 1, 1)
        return jnp.concatenate([jnp.where(first, 0.0, lo), jnp.where(first, lo, hi)], axis=1)

    def z_down(a):
        lo = pltpu.roll(a[:, :128], 127, 1)
        hi = pltpu.roll(a[:, 128:], 127, 1)
        return jnp.concatenate([jnp.where(final, hi, lo), jnp.where(final, 0.0, hi)], axis=1)

    return z_up, z_down


def own_rows(k, kx_low, kx, refs, x):
    kx_s, ky_s, kyd_s, kz_s, kzd_s, c_s = refs
    z_up, z_down = z_shifts(BY)
    row = lax.broadcasted_iota(jnp.int32, (BY, NZ), 0)
    own = slice(0, BY)
    ky = jnp.where(row < BY - 1, 0.05 * (k + pltpu.roll(k, BY - 1, 0)), 0.0)
    kyd = pltpu.roll(ky, 1, 0)
    kz = 0.05 * (k + z_down(k))
    kzd = 0.05 * (k + z_up(k))
    kx_s[x, own] = kx
    ky_s[x, own] = ky
    kyd_s[x, own] = kyd
    kz_s[x, own] = kz
    kzd_s[x, own] = kzd
    c_s[x, own] = 1.0 - ((kx + kx_low) + (ky + kyd) + (kz + kzd))


def load(sources, targets, sems):
    copies = []
    for c in range(BX // PACK):
        part = pl.ds(c * PACK, PACK)
        copies.append([])
        for n, (src, dst) in enumerate(zip(sources, targets)):
            at = (slice(None), part) if len(src.shape) == 4 else (part,)
            copies[-1].append(pltpu.make_async_copy(src.at[at], dst.at[at], sems.at[n, c]))
            copies[-1][-1].start()
    return copies


def own_body(f_hbm, k_hbm, v_hbm, after_ref, u_s, v0_s, v1_s, v2_s, kx_s, ky_s, kyd_s, kz_s, kzd_s, c_s, edge_s, end_ref,
             f_ref, k_ref, v_ref, sems):
    f32 = jnp.float32
    for part in load((f_hbm, k_hbm, v_hbm), (f_ref, k_ref, v_ref), sems):
        for copy in part:
            copy.wait()
    refs = (kx_s, ky_s, kyd_s, kz_s, kzd_s, c_s)

    def plane(x, carry):
        k, kx_low = carry
        k_next = k_ref[jnp.minimum(x + 1, BX - 1)].astype(f32)
        kx = jnp.where(x < BX - 1, 0.05, 0.0) * (k + k_next)
        u_s[x + W, 0:BY] = f_ref[x]
        for n, ref in enumerate((v0_s, v1_s, v2_s)):
            ref[x + W, 0:BY] = v_ref[n, x].astype(f32)
        edge_s[x + W, 0:8] = k[0:8]
        edge_s[x + W, 8:16] = k[BY - 8 :]
        own_rows(k, kx_low, kx, refs, x + W)
        return k_next, kx

    lax.fori_loop(0, BX, plane, (k_ref[0].astype(f32), jnp.zeros((BY, NZ), f32)), unroll=4)
    end_ref[0] = k_ref[0].astype(f32)
    end_ref[1] = k_ref[BX - 1].astype(f32)


def x_planes_body(count_x, xl_ref, xh_ref, end_ref, *rest_refs):
    f32 = jnp.float32
    u_s, v0_s, v1_s, v2_s, kx_s, ky_s, kyd_s, kz_s, kzd_s, c_s, edge_s = rest_refs[KEPT : 2 * KEPT]
    kp_s = rest_refs[2 * KEPT]
    refs = (kx_s, ky_s, kyd_s, kz_s, kzd_s, c_s)
    p = lax.axis_index("px")
    from_low_x = jnp.where(p > 0, 1.0, 0.0)
    from_high_x = jnp.where(p < count_x - 1, 1.0, 0.0)
    dest = (u_s, None, v0_s, v1_s, v2_s)
    for n in range(5):
        for base, ref, scale, near, outer in (
            (0, xl_ref, from_low_x, (W - 1, W - 2), 0),
            (BX + W, xh_ref, from_high_x, (0, 1), W - 1),
        ):
            for i in range(W):
                value = ref[n * W + i].astype(f32)
                if n == 0 and i in near:
                    value = value + ref[(3 + near.index(i)) * W + outer].astype(f32)
                value = value * scale
                if n == 1:
                    kp_s[base % BX + i] = value
                    edge_s[base + i, 0:8] = value[0:8]
                    edge_s[base + i, 8:16] = value[BY - 8 :]
                else:
                    dest[n][base + i, 0:BY] = value

    kx_low = jnp.zeros((BY, NZ), f32)
    for i in range(W):
        k = kp_s[i]
        kx = 0.05 * (k + (kp_s[i + 1] if i < W - 1 else end_ref[0]))
        own_rows(k, kx_low, kx, refs, i)
        kx_low = kx
    c_s[W, 0:BY] = c_s[W, 0:BY] - kx_low
    kx_low = 0.05 * (end_ref[1] + kp_s[W])
    kx_s[BX + W - 1, 0:BY] = kx_low
    c_s[BX + W - 1, 0:BY] = c_s[BX + W - 1, 0:BY] - kx_low
    for i in range(W):
        k = kp_s[W + i]
        kx = 0.05 * (k + kp_s[min(W + i + 1, 2 * W - 1)])
        own_rows(k, kx_low, kx, refs, BX + W + i)
        kx_low = kx


def dot3(a, b):
    dot = functools.partial(jnp.dot, preferred_element_type=jnp.float32)
    return dot(a[0], b[0]) + (dot(a[0], b[1]) + dot(a[1], b[0]))


def halves(a):
    hi = a.astype(jnp.bfloat16)
    return hi, (a - hi.astype(jnp.float32)).astype(jnp.bfloat16)


def place_of(owner, count, m0, m1):
    own = jnp.clip(owner, 0, count - 1)
    cls = jnp.where(own == 0, 0, jnp.where(own == count - 1, 2, 1))
    n = OVMAX + 1
    return (cls * n + jnp.clip(m0, 0, OVMAX)) * n + jnp.clip(m1, 0, OVMAX)


def stencil_body(count_x, count_y, margin_ref, yl_ref, yh_ref, xl_ref, xh_ref, cl_ref, ch_ref, fit_ref, base_hbm, send_hbm,
                 near_hbm, ytab_hbm, couple_hbm,
                 *rest_refs):
    f32 = jnp.float32
    outs = rest_refs[KEPT:]
    adv_hbm, zt_ref, lo_ref, hi_ref, lo2_ref, hi2_ref, full_ref, couple_ref = outs[:8]
    u_s, v0_s, v1_s, v2_s, kx_s, ky_s, kyd_s, kz_s, kzd_s, c_s, edge_s = outs[8 : 8 + KEPT]
    kh_s, base_s, send_s, near_s, ytab_s, sems = outs[8 + KEPT :]
    p = lax.axis_index("px")
    q = lax.axis_index("py")

    def margins(ref):
        part = ref[5 * W].astype(f32)
        return [jnp.max(a).astype(jnp.int32) for a in (part[0:8], part[16:24])]

    mine = place_of(p, count_x, margin_ref[0, 0], margin_ref[0, 1])
    low = place_of(p - 1, count_x, *margins(xl_ref))
    high = place_of(p + 1, count_x, *margins(xh_ref))
    copies = [
        pltpu.make_async_copy(base_hbm.at[mine], base_s, sems.at[0]),
        pltpu.make_async_copy(send_hbm.at[mine], send_s, sems.at[1]),
        pltpu.make_async_copy(near_hbm.at[low, 0], near_s.at[0], sems.at[2]),
        pltpu.make_async_copy(near_hbm.at[high, 1], near_s.at[1], sems.at[3]),
        pltpu.make_async_copy(ytab_hbm.at[q], ytab_s, sems.at[4]),
        pltpu.make_async_copy(couple_hbm.at[q], couple_ref, sems.at[5]),
    ]
    for copy in copies:
        copy.start()
    refs = (kx_s, ky_s, kyd_s, kz_s, kzd_s, c_s)
    from_low_x = jnp.where(p > 0, 1.0, 0.0)
    from_high_x = jnp.where(p < count_x - 1, 1.0, 0.0)
    from_low_y = jnp.where(q > 0, 1.0, 0.0)
    from_high_y = jnp.where(q < count_y - 1, 1.0, 0.0)
    beyond = slice(BY, EY)

    def halo_rows(group, carry):
        at = group * 4
        ul = yl_ref[group, 4].astype(f32) * from_low_y
        uh = yh_ref[group, 4].astype(f32) * from_high_y
        gap = jnp.zeros((4, NZ), f32)
        for i in range(4):
            x = at + i + W
            kl = yl_ref[group, i].astype(f32) * from_low_y
            kh = yh_ref[group, i].astype(f32) * from_high_y
            rest = jnp.concatenate([kh[7:8], kh[15:16], gap, kl[12:13], kl[4:5]], axis=0)
            u_s[x, beyond] = rest + jnp.concatenate([uh[4 * i : 4 * i + 4], ul[4 * i : 4 * i + 4]], axis=0)
            kh_s[x] = jnp.concatenate([kh[0:4], kl[0:4]], axis=0)
            for n, ref in enumerate((v0_s, v1_s, v2_s)):
                m = 4 * n + 4
                ref[x, beyond] = jnp.concatenate([kh[m : m + 4], kl[m : m + 4]], axis=0)
        return carry

    lax.fori_loop(0, BX // 4, halo_rows, 0)
    dest = (u_s, kh_s, v0_s, v1_s, v2_s)
    none = jnp.zeros((1, NZ), f32)
    for base, corner, scale, near in ((0, 0, from_low_x, range(1, W)), (BX + W, 3, from_high_x, range(W - 1))):
        low = cl_ref[corner : corner + 3].astype(f32).reshape(48, NZ) * (scale * from_low_y)
        high = ch_ref[corner : corner + 3].astype(f32).reshape(48, NZ) * (scale * from_high_y)
        for n in range(5):
            at = slice(0, 8) if n == 1 else beyond
            for i in range(W):
                if i in near:
                    row = (n * 3 + near.index(i)) * 3
                    tile = jnp.concatenate([high[row : row + 3], none, none, low[row : row + 3]], axis=0)
                else:
                    tile = jnp.zeros((8, NZ), f32)
                dest[n][base + i, at] = tile

    sub = lax.broadcasted_iota(jnp.int32, (8, NZ), 0)
    zt_up, zt_down = z_shifts(8)

    def halo_coefficients(x, carry):
        k, kx_low = carry
        k_next = kh_s[jnp.minimum(x + 1, EX - 1)]
        kx = 0.05 * (k + k_next)
        up = 0.05 * (edge_s[x, 8:16] + pltpu.roll(k, 7, 0))
        down = 0.05 * (edge_s[x, 0:8] + pltpu.roll(k, 1, 0))
        up = jnp.where(sub == 7, up, 0.0)
        down = jnp.where(sub == 0, down, 0.0)
        ky = jnp.where(sub == 7, pltpu.roll(down, 7, 0), 0.05 * (k + pltpu.roll(k, 7, 0)))
        kyd = jnp.where(sub == 0, pltpu.roll(up, 1, 0), pltpu.roll(ky, 1, 0))
        kz = 0.05 * (k + zt_down(k))
        kzd = 0.05 * (k + zt_up(k))
        kx_s[x, beyond] = kx
        ky_s[x, beyond] = ky
        kyd_s[x, beyond] = kyd
        kz_s[x, beyond] = kz
        kzd_s[x, beyond] = kzd
        c_s[x, beyond] = 1.0 - ((kx + kx_low) + (ky + kyd) + (kz + kzd))
        ky_s[x, BY - 8 : BY] = ky_s[x, BY - 8 : BY] + up
        kyd_s[x, 0:8] = kyd_s[x, 0:8] + down
        c_s[x, 0:8] = c_s[x, 0:8] - down
        c_s[x, BY - 8 : BY] = c_s[x, BY - 8 : BY] - up
        return k_next, kx

    lax.fori_loop(0, EX, halo_coefficients, (kh_s[0], jnp.zeros((8, NZ), f32)), unroll=8)

    row = lax.broadcasted_iota(jnp.int32, (EY, NZ), 0)
    row_mask = jnp.where(row < BY, 1.0, jnp.where(row < BY + W, from_high_y, from_low_y))

    for step in range(STEPS):
        lo = step
        hi = EX - 1 - step

        rows = EY if step < STEPS - 1 else BY
        z_up, z_down = z_shifts(rows)

        def one_plane(x, carry, rows=rows, z_up=z_up, z_down=z_down):
            partial, up = carry
            full = u_s[x]
            w = 0.025 * full
            g1 = v1_s[x] * w
            y_part = pltpu.roll(full * (ky_s[x] + g1), 1, 0) + pltpu.roll(full * (kyd_s[x] - g1), EY - 1, 0)
            u = full[:rows]
            g0 = v0_s[x, 0:rows] * w[:rows]
            g2 = v2_s[x, 0:rows] * w[:rows]
            prev = x - 1
            done = partial + u * (kx_s[prev, 0:rows] - g0)
            if rows == EY:
                plane_mask = jnp.where(prev < W, from_low_x, jnp.where(prev >= BX + W, from_high_x, 1.0))
                done = done * (row_mask * plane_mask)
            u_s[prev, 0:rows] = done
            up_next = u * (kx_s[x, 0:rows] + g0)
            total = u * c_s[x, 0:rows] + up + y_part[:rows]
            total = total + z_up(u * (kz_s[x, 0:rows] + g2))
            total = total + z_down(u * (kzd_s[x, 0:rows] - g2))
            return total, up_next

        first_u = u_s[lo, 0:rows]
        first_up = first_u * (kx_s[lo, 0:rows] + v0_s[lo, 0:rows] * (0.025 * first_u))
        lax.fori_loop(lo + 1, hi + 1, one_plane, (jnp.zeros((rows, NZ), f32), first_up), unroll=4)

    result = pltpu.make_async_copy(u_s.at[pl.ds(W, BX), pl.ds(0, BY)], adv_hbm, sems.at[6])
    result.start()
    for copy in copies:
        copy.wait()
    fit = (fit_ref[0], fit_ref[1])
    ytab = (ytab_s[0], ytab_s[1])

    def fit_planes(group, carry):
        at = pl.multiple_of(group * 8, 8)
        part = u_s[pl.ds(at + W, 8), 0:BY]
        rows = dot3(ytab, halves(part.reshape(8 * BY, NZ)))
        rows = dot3(halves(rows), fit)
        for r in range(YR):
            zt_ref[r, pl.ds(at, 8)] = rows[8 * r : 8 * r + 8]
        return carry

    lax.fori_loop(0, BX // 8, fit_planes, 0, unroll=8)

    send = halves(send_s[...])
    for r in range(0, YR, 2):
        lines = slice(r * MZ, (r + 2) * MZ)
        rows = dot3(send, halves(jnp.concatenate([zt_ref[r], zt_ref[r + 1]], axis=1)))
        lo_ref[:, lines] = rows[0:16]
        hi_ref[:, lines] = rows[16:32]
        lo2_ref[:, lines] = rows[0:16].astype(jnp.bfloat16)
        hi2_ref[:, lines] = rows[16:32].astype(jnp.bfloat16)
    base = base_s[...]
    full = base
    for j in range(7):
        full = full + base[:, 70 + j : 71 + j] * near_s[0, j : j + 1, :]
        full = full + base[:, 86 + j : 87 + j] * near_s[1, j : j + 1, :]
    full_ref[...] = full
    result.wait()


def combine_body(zt_ref, lo_ref, hi_ref, lo2_ref, hi2_ref, full_ref, own_ref, carry_ref):
    f32 = jnp.float32
    q = lax.axis_index("py")
    full = halves(full_ref[...])

    def stack(first, last):
        lines = slice(first * MZ, last * MZ)
        return jnp.concatenate(
            [jnp.concatenate([zt_ref[r] for r in range(first, last)], axis=1), lo_ref[:, lines], hi_ref[:, lines]]
            + [ref[:, lines].astype(f32) for ref in (lo2_ref, hi2_ref)],
            axis=0,
        )

    own = BY // 2
    for r in range(0, own, 2):
        out = dot3(full, halves(stack(r, r + 2)))
        for i in range(2):
            own_ref[:, r + i, :] = out[:, i * MZ : (i + 1) * MZ]

    block = BX // 2
    part = lax.broadcasted_iota(jnp.int32, (4 * block, 128), 0) % 4
    spread = lax.broadcasted_iota(jnp.int32, (4 * block, block), 0) // 4
    spread = jnp.where(spread == lax.broadcasted_iota(jnp.int32, (4 * block, block), 1), 1.0, 0.0).astype(jnp.bfloat16)
    spaced = []
    for f in full:
        rows = jnp.dot(spread, f, preferred_element_type=f32)
        spaced.append(
            jnp.concatenate(
                [jnp.where(part % 3 == 0, rows, 0.0), jnp.where(part == 1, rows, 0.0), jnp.where(part == 2, rows, 0.0)],
                axis=1,
            ).astype(jnp.bfloat16)
        )
    carries = stack(own, YR)
    carries = jnp.concatenate(
        [jnp.concatenate([carries[:, n * MZ : (n + 1) * MZ], carries[:, (n + 3) * MZ : (n + 4) * MZ]], axis=1) for n in range(3)],
        axis=0,
    )
    carries = dot3(spaced, halves(carries))
    coded = []
    for n in range(2):
        value = carries[:, n * MZ : (n + 1) * MZ]
        head = value.astype(jnp.bfloat16).astype(f32)
        coded.append(jnp.where(part == 3, value - head, value).astype(jnp.bfloat16))
    for t in range(carry_ref.shape[0]):

        @pl.when(t > q)
        def _():
            carry_ref[t] = coded[0]

        @pl.when(t <= q)
        def _():
            carry_ref[t] = coded[1]


def couple_body(own_ref, got_ref, couple_ref, out_ref):
    dot = functools.partial(jnp.dot, preferred_element_type=jnp.float32)
    head = couple_ref[0]
    rest = couple_ref[1]
    for x in range(0, BX // 2, 8):
        got = got_ref[:, 4 * x : 4 * x + 32].reshape(-1, MZ)
        out_ref[x : x + 8] = own_ref[x : x + 8] + (dot(head, got) + dot(rest, got)).reshape(8, BY // 2, MZ)


KEPT = 11


def in_hbm(a):
    return pltpu.with_memory_space_constraint(a, pltpu.HBM)


def own_coefficients(field, diffusivity, velocity, after):
    vmem = pl.BlockSpec(memory_space=pltpu.VMEM)
    f32 = jnp.float32
    return pl.pallas_call(
        own_body,
        out_shape=[pltpu.VMEM((EX, EY, NZ), f32)] * (KEPT - 1)
        + [pltpu.VMEM((EX, 16, NZ), f32), pltpu.VMEM((2, BY, NZ), f32)],
        in_specs=[pl.BlockSpec(memory_space=pltpu.HBM)] * 3 + [pl.BlockSpec(memory_space=pl.ANY)],
        out_specs=[vmem] * (KEPT + 1),
        scratch_shapes=[pltpu.VMEM(a.shape, a.dtype) for a in (field, diffusivity, velocity)]
        + [pltpu.SemaphoreType.DMA((3, BX // PACK))],
        compiler_params=pltpu.CompilerParams(vmem_limit_bytes=12 * 1024 * 1024),
        name="own_coefficients",
    )(*[in_hbm(a) for a in (field, diffusivity, velocity)], after)


def x_planes(count_x, xl, xh, end, kept):
    vmem = pl.BlockSpec(memory_space=pltpu.VMEM)
    f32 = jnp.float32
    return pl.pallas_call(
        functools.partial(x_planes_body, count_x),
        out_shape=[pltpu.VMEM(a.shape, f32) for a in kept],
        in_specs=[vmem] * (3 + KEPT),
        out_specs=[vmem] * KEPT,
        input_output_aliases={3 + i: i for i in range(KEPT)},
        scratch_shapes=[pltpu.VMEM((2 * W, BY, NZ), f32)],
        compiler_params=pltpu.CompilerParams(vmem_limit_bytes=8 * 1024 * 1024),
        name="x_planes",
    )(xl, xh, end, *kept)


def time_steps(counts, margin, halos, fit, tables, kept):
    vmem = pl.BlockSpec(memory_space=pltpu.VMEM)
    smem = pl.BlockSpec(memory_space=pltpu.SMEM)
    hbm = pl.BlockSpec(memory_space=pltpu.HBM)
    f32 = jnp.float32
    bf16 = jnp.bfloat16
    shapes = [((BX, BY, NZ), f32), ((YR, BX, MZ), f32)] + [((16, LINES), f32)] * 2 + [((16, LINES), bf16)] * 2
    shapes += [((BX // 2, 128), f32)]
    return pl.pallas_call(
        functools.partial(stencil_body, *counts),
        out_shape=[jax.ShapeDtypeStruct(s, t) for s, t in shapes]
        + [pltpu.VMEM(tables[-1].shape[1:], bf16)]
        + [pltpu.VMEM(a.shape, f32) for a in kept],
        in_specs=[smem] + [vmem] * 7 + [hbm] * 5 + [vmem] * KEPT,
        out_specs=[hbm] + [vmem] * (7 + KEPT),
        input_output_aliases={13 + i: 8 + i for i in range(KEPT)},
        scratch_shapes=[
            pltpu.VMEM((EX, 8, NZ), f32),
            pltpu.VMEM((BX // 2, 128), f32),
            pltpu.VMEM((BX // 2, BX), f32),
            pltpu.VMEM((2, 8, 128), f32),
            pltpu.VMEM((2, YR * 8, 8 * BY), bf16),
            pltpu.SemaphoreType.DMA((7,)),
        ],
        compiler_params=pltpu.CompilerParams(vmem_limit_bytes=STEP_VMEM * 1024 * 1024),
        name="time_steps",
    )(margin, *halos, fit, *[in_hbm(t) for t in tables], *kept)[:8]


def combine(count_y, rows):
    vmem = pl.BlockSpec(memory_space=pltpu.VMEM)
    return pl.pallas_call(
        combine_body,
        out_shape=[
            jax.ShapeDtypeStruct((BX // 2, BY // 2, MZ), jnp.float32),
            jax.ShapeDtypeStruct((count_y, 2 * BX, MZ), jnp.bfloat16),
        ],
        in_specs=[vmem] * 6,
        out_specs=[vmem] * 2,
        compiler_params=pltpu.CompilerParams(vmem_limit_bytes=12 * 1024 * 1024),
        name="combine",
    )(*rows)


def add_carries(own, got, couple):
    vmem = pl.BlockSpec(memory_space=pltpu.VMEM)
    return pl.pallas_call(
        couple_body,
        out_shape=jax.ShapeDtypeStruct((BX // 2, BY // 2, MZ), jnp.float32),
        in_specs=[vmem] * 3,
        out_specs=vmem,
        compiler_params=pltpu.CompilerParams(vmem_limit_bytes=8 * 1024 * 1024),
        name="add_carries",
    )(own, got, couple)


def ring(n, d):
    return [(i, (i + d) % n) for i in range(n)]


def shift(a, axis, d):
    return lax.ppermute(a, axis, ring(lax.axis_size(axis), d))


def pack_body(margin_hbm, f_hbm, k_hbm, v_hbm, ylo_ref, yhi_ref, xlo_ref, xhi_ref, f_ref, k_ref, v_ref, margin_ref, sems,
              margin_sem):
    f32 = jnp.float32
    bf16 = jnp.bfloat16
    t = BY - W
    margin_copy = pltpu.make_async_copy(margin_hbm, margin_ref, margin_sem)
    margin_copy.start()
    copies = load((f_hbm, k_hbm, v_hbm), (f_ref, k_ref, v_ref), sems)

    def rest(u):
        return u - u.astype(bf16).astype(f32)

    def faces(g, carry):
        tails, heads = [], []
        for i in range(4):
            x = 4 * g + i
            u = f_ref[x]
            tails.append(u[t:])
            heads.append(u[:W])
            ur_t = rest(u[t - 4 :])
            ur_h = rest(u[:8])
            k, v0, v1, v2 = [r.astype(f32) for r in (k_ref[x], v_ref[0, x], v_ref[1, x], v_ref[2, x])]
            ylo_ref[g, i] = jnp.concatenate(
                [k[t:], ur_t[7:8], v0[t + 1 :], v1[t:], ur_t[6:7], v2[t + 1 :]], axis=0
            ).astype(bf16)
            yhi_ref[g, i] = jnp.concatenate(
                [k[:W], v0[: W - 1], ur_h[0:1], v1[:W], v2[: W - 1], ur_h[1:2]], axis=0
            ).astype(bf16)
        ylo_ref[g, 4] = jnp.concatenate(tails, axis=0).astype(bf16)
        yhi_ref[g, 4] = jnp.concatenate(heads, axis=0).astype(bf16)
        return carry

    def x_side(at, out, near, outer):
        for i in range(W):
            out[i] = f_ref[at + i].astype(bf16)
            out[W + i] = k_ref[at + i]
            out[2 * W + i] = v_ref[0, at + i]
            if i == outer:
                out[3 * W + i] = rest(f_ref[at + near[0]]).astype(bf16)
                out[4 * W + i] = rest(f_ref[at + near[1]]).astype(bf16)
            else:
                out[3 * W + i] = v_ref[1, at + i]
                out[4 * W + i] = v_ref[2, at + i]
        half = jnp.zeros((16, NZ), f32)
        out[5 * W] = jnp.concatenate([half + margin_ref[0, 0].astype(f32), half + margin_ref[0, 1].astype(f32)], axis=0).astype(bf16)

    margin_copy.wait()
    for c in range(BX // PACK):
        for copy in copies[c]:
            copy.wait()
        lax.fori_loop(c * PACK // 4, (c + 1) * PACK // 4, faces, 0)
        if c == 0:
            x_side(0, xhi_ref, (0, 1), W - 1)
    x_side(BX - W, xlo_ref, (W - 1, W - 2), 0)


def corner_body(xl_ref, xh_ref, up_ref, down_ref):
    f32 = jnp.float32
    for side, ref, near in ((0, xl_ref, range(1, W)), (1, xh_ref, range(W - 1))):
        planes = [ref[n * W + i].astype(f32) for n in range(5) for i in near]
        gap = [jnp.zeros((3, NZ), f32)]
        part = slice(side * 3, side * 3 + 3)
        for out, rows in ((up_ref, slice(BY - 3, BY)), (down_ref, slice(0, 3))):
            out[part] = jnp.concatenate([a[rows] for a in planes] + gap, axis=0).reshape(3, 16, NZ).astype(jnp.bfloat16)


def halo_parts(field, diffusivity, velocity, margin):
    bf16 = jnp.bfloat16
    y_shape = (BX // 4, 5, 16, NZ)
    x_shape = (5 * W + 1, BY, NZ)
    c_shape = (6, 16, NZ)
    vmem = pl.BlockSpec(memory_space=pltpu.VMEM)
    hbm = pl.BlockSpec(memory_space=pltpu.HBM)
    ylo, yhi, xlo, xhi = pl.pallas_call(
        pack_body,
        out_shape=[jax.ShapeDtypeStruct(s, bf16) for s in [y_shape] * 2 + [x_shape] * 2],
        in_specs=[hbm] * 4,
        out_specs=[vmem] * 4,
        scratch_shapes=[pltpu.VMEM(a.shape, a.dtype) for a in (field, diffusivity, velocity)]
        + [pltpu.SMEM(margin.shape, jnp.int32), pltpu.SemaphoreType.DMA((3, BX // PACK)), pltpu.SemaphoreType.DMA(())],
        compiler_params=pltpu.CompilerParams(vmem_limit_bytes=PACK_VMEM * 1024 * 1024),
        name="pack_faces",
    )(*[in_hbm(a) for a in (margin, field, diffusivity, velocity)])
    xl = shift(xlo, "px", 1)
    xh = shift(xhi, "px", -1)
    yl = shift(ylo, "py", 1)
    yh = shift(yhi, "py", -1)
    kept = own_coefficients(field, diffusivity, velocity, ylo)
    xl, xh, kept = lax.optimization_barrier((xl, xh, kept))
    c_up, c_down = pl.pallas_call(
        corner_body,
        out_shape=[jax.ShapeDtypeStruct(c_shape, bf16)] * 2,
        in_specs=[vmem] * 2,
        out_specs=[vmem] * 2,
        compiler_params=pltpu.CompilerParams(vmem_limit_bytes=4 * 1024 * 1024),
        name="pack_corners",
    )(xl, xh)
    halos = (yl, yh, xl, xh, shift(c_up, "py", 1), shift(c_down, "py", -1))
    _, kept = lax.optimization_barrier((c_up, kept))
    return halos, x_planes(lax.axis_size("px"), xl, xh, kept[KEPT], kept[:KEPT])


def per_device(field, diffusivity, velocity, margin):
    count_x = lax.axis_size("px")
    count_y = lax.axis_size("py")
    fit = jnp.asarray(np.stack(split(fit_matrix(NZ).T)))
    ytab, couple = y_tables(count_y)
    tables = [jnp.asarray(t) for t in x_tables(count_x) + [ytab, couple]]
    halos, kept = halo_parts(field, diffusivity, velocity, margin)
    advected, zt, lo, hi, lo2, hi2, full, couple = time_steps(
        (count_x, count_y), margin, halos, fit, tables, kept
    )
    rows = (zt, shift(lo, "px", 1), shift(hi, "px", -1), shift(lo2, "px", 2), shift(hi2, "px", -2), full)
    own, carries = combine(count_y, rows)
    got = lax.all_to_all(carries, "py", split_axis=0, concat_axis=0, tiled=True)
    return advected, add_carries(own, got, couple)


def solution(mesh):
    placed = (P("px", "py", None), P("px", "py", None), P(None, "px", "py", None), P("px", None))
    return jax.shard_map(
        per_device,
        mesh=mesh,
        in_specs=placed,
        out_specs=(P("px", "py", None), P("px", "py", None)),
        check_vma=False,
    )
```

```python
import functools

import jax
import jax.numpy as jnp
import numpy as np
from jax import lax
from jax.experimental import pallas as pl
from jax.experimental.pallas import tpu as pltpu
from jax.sharding import PartitionSpec as P

STEPS = 4
OVMAX = 4
BX = 64
BY = 32
NZ = 256
MZ = 128
W = 4
EX = BX + 2 * W
EY = BY + 2 * W
YR = BY // 2 + 6
LINES = YR * 128


PACK = 16
PACK_VMEM = 12
STEP_VMEM = 16


def bspline(t):
    m = np.abs(t)
    inner = (4.0 - 6.0 * m * m + 3.0 * m**3) / 6.0
    outer = np.maximum(2.0 - m, 0.0) ** 3 / 6.0
    return np.where(m < 1.0, inner, outer)


def basis(n):
    j = np.arange(n)[:, None]
    k = np.arange(n // 2)[None, :]
    return bspline((j - 2.0 * k - 0.5) / 2.0)


def fit_matrix(n):
    b = basis(n)
    return np.linalg.solve(b.T @ b, b.T)


def split(a):
    a = a.astype(np.float32)
    hi = a.astype(jnp.bfloat16)
    return hi, (a - hi.astype(np.float32)).astype(jnp.bfloat16)


def y_tables(count):
    total = count * BY
    s = fit_matrix(total)
    own = BY // 2
    rows = np.zeros((count, YR, BY))
    couple = np.zeros((count, own, count, 4))
    for q in range(count):
        cols = s[:, q * BY : (q + 1) * BY]
        rows[q, :own] = cols[q * own : (q + 1) * own]
        for at, far, targets in ((own, cols[(q + 1) * own :], range(q + 1, count)), (own + 3, cols[: q * own], range(q))):
            if len(targets) == 0:
                continue
            u, sv, vt = np.linalg.svd(far, full_matrices=False)
            assert sv[3] < 1e-10 * sv[0]
            rows[q, at : at + 3] = vt[:3]
            left = (u[:, :3] * sv[:3]).reshape(len(targets), own, 3)
            for i, t in enumerate(targets):
                couple[t, :, q, :3] = left[i]
                couple[t, :, q, 3] = left[i, :, 0]
    table = np.einsum("qry,xw->qrxwy", rows, np.eye(8)).reshape(count, YR * 8, 8 * BY)
    spaced = np.einsum("qmtc,xw->qxmtwc", couple, np.eye(8)).reshape(count, own * 8, count * 32)
    return np.stack(split(table), axis=1), np.stack(split(spaced), axis=1)


def x_tables(count):
    total = count * BX
    block = BX // 2
    ctrl = total // 2
    b = basis(total)
    width = block + 2 * OVMAX
    gpad = np.zeros((ctrl + 16, ctrl + 16))
    gpad[8:-8, 8:-8] = b.T @ b
    bt = bspline((np.arange(BX)[None] - 2.0 * (np.arange(block + 4)[:, None] - 2) - 0.5) / 2.0)
    base, send, near = [], [], []
    for cls, p in enumerate((0, 1, count - 1)):
        has_low = float(cls != 0)
        has_high = float(cls != 2)
        start = p * block
        knots = start - OVMAX + np.arange(width)
        lo = start - OVMAX + 8
        full = gpad[lo : lo + width, lo : lo + width]
        band = gpad[lo : lo + width, lo - 3 : lo + width + 3]
        for m0 in range(OVMAX + 1):
            for m1 in range(OVMAX + 1):
                inside = (knots >= start - m0) & (knots < start + block + m1) & (knots >= 0) & (knots < ctrl)
                w = inside.astype(np.float64)
                mat = full * w[:, None] * w[None, :] + np.diag(1.0 - w)
                e = (np.linalg.inv(mat) * w[None, :])[OVMAX : OVMAX + block]
                q = e @ band
                ql = q[:, :7] * has_low
                qr = q[:, 7 + block :] * has_high
                two = 2.0 * e - q[:, 7 : 7 + block] @ e
                low = two[:, 0:6] * has_low
                high = two[:, block + 2 :] * has_high
                gap3 = np.zeros((block, 3))
                gap32 = np.zeros((block, 32))
                base.append(np.concatenate([two[:, 2 : block + 6] @ bt, low, -ql, gap3, high, -qr, gap3, gap32], axis=1))
                pad = np.zeros((3, BX))
                send.append(
                    np.concatenate(
                        [bt[block - 2 :], e[block - 7 :, 2 : block + 6] @ bt, pad, bt[:6], e[:7, 2 : block + 6] @ bt, pad]
                    )
                )
                both = np.zeros((2, 8, 128))
                both[0, :7, :BX] = e[block - 7 :, block + 2 :] @ bt[0:6]
                both[0, :7, 96:102] = e[block - 7 :, 0:6] * has_low
                both[1, :7, :BX] = e[:7, 0:6] @ bt[block - 2 :]
                both[1, :7, 112:118] = e[:7, block + 2 :] * has_high
                near.append(both)
    return [np.stack(t).astype(np.float32) for t in (base, send, near)]


def z_shifts(rows):
    lane = lax.broadcasted_iota(jnp.int32, (rows, 128), 1)
    first = lane == 0
    final = lane == 127

    def z_up(a):
        lo = pltpu.roll(a[:, :128], 1, 1)
        hi = pltpu.roll(a[:, 128:], 1, 1)
        return jnp.concatenate([jnp.where(first, 0.0, lo), jnp.where(first, lo, hi)], axis=1)

    def z_down(a):
        lo = pltpu.roll(a[:, :128], 127, 1)
        hi = pltpu.roll(a[:, 128:], 127, 1)
        return jnp.concatenate([jnp.where(final, hi, lo), jnp.where(final, 0.0, hi)], axis=1)

    return z_up, z_down


def own_rows(k, kx_low, kx, refs, x):
    kx_s, ky_s, kyd_s, kz_s, kzd_s, c_s = refs
    z_up, z_down = z_shifts(BY)
    row = lax.broadcasted_iota(jnp.int32, (BY, NZ), 0)
    own = slice(0, BY)
    ky = jnp.where(row < BY - 1, 0.05 * (k + pltpu.roll(k, BY - 1, 0)), 0.0)
    kyd = pltpu.roll(ky, 1, 0)
    kz = 0.05 * (k + z_down(k))
    kzd = 0.05 * (k + z_up(k))
    kx_s[x, own] = kx
    ky_s[x, own] = ky
    kyd_s[x, own] = kyd
    kz_s[x, own] = kz
    kzd_s[x, own] = kzd
    c_s[x, own] = 1.0 - ((kx + kx_low) + (ky + kyd) + (kz + kzd))


def load(sources, targets, sems):
    copies = []
    for c in range(BX // PACK):
        part = pl.ds(c * PACK, PACK)
        copies.append([])
        for n, (src, dst) in enumerate(zip(sources, targets)):
            at = (slice(None), part) if len(src.shape) == 4 else (part,)
            copies[-1].append(pltpu.make_async_copy(src.at[at], dst.at[at], sems.at[n, c]))
            copies[-1][-1].start()
    return copies


def own_body(f_hbm, k_hbm, v_hbm, after_ref, u_s, v0_s, v1_s, v2_s, kx_s, ky_s, kyd_s, kz_s, kzd_s, c_s, edge_s, end_ref,
             f_ref, k_ref, v_ref, sems):
    f32 = jnp.float32
    for part in load((f_hbm, k_hbm, v_hbm), (f_ref, k_ref, v_ref), sems):
        for copy in part:
            copy.wait()
    refs = (kx_s, ky_s, kyd_s, kz_s, kzd_s, c_s)

    def plane(x, carry):
        k, kx_low = carry
        k_next = k_ref[jnp.minimum(x + 1, BX - 1)].astype(f32)
        kx = jnp.where(x < BX - 1, 0.05, 0.0) * (k + k_next)
        u_s[x + W, 0:BY] = f_ref[x]
        for n, ref in enumerate((v0_s, v1_s, v2_s)):
            ref[x + W, 0:BY] = v_ref[n, x].astype(f32)
        edge_s[x + W, 0:8] = k[0:8]
        edge_s[x + W, 8:16] = k[BY - 8 :]
        own_rows(k, kx_low, kx, refs, x + W)
        return k_next, kx

    lax.fori_loop(0, BX, plane, (k_ref[0].astype(f32), jnp.zeros((BY, NZ), f32)), unroll=4)
    end_ref[0] = k_ref[0].astype(f32)
    end_ref[1] = k_ref[BX - 1].astype(f32)


def x_planes_body(count_x, xl_ref, xh_ref, end_ref, *rest_refs):
    f32 = jnp.float32
    u_s, v0_s, v1_s, v2_s, kx_s, ky_s, kyd_s, kz_s, kzd_s, c_s, edge_s = rest_refs[KEPT : 2 * KEPT]
    kp_s = rest_refs[2 * KEPT]
    refs = (kx_s, ky_s, kyd_s, kz_s, kzd_s, c_s)
    p = lax.axis_index("px")
    from_low_x = jnp.where(p > 0, 1.0, 0.0)
    from_high_x = jnp.where(p < count_x - 1, 1.0, 0.0)
    dest = (u_s, None, v0_s, v1_s, v2_s)
    for n in range(5):
        for base, ref, scale, near, outer in (
            (0, xl_ref, from_low_x, (W - 1, W - 2), 0),
            (BX + W, xh_ref, from_high_x, (0, 1), W - 1),
        ):
            for i in range(W):
                value = ref[n * W + i].astype(f32)
                if n == 0 and i in near:
                    value = value + ref[(3 + near.index(i)) * W + outer].astype(f32)
                value = value * scale
                if n == 1:
                    kp_s[base % BX + i] = value
                    edge_s[base + i, 0:8] = value[0:8]
                    edge_s[base + i, 8:16] = value[BY - 8 :]
                else:
                    dest[n][base + i, 0:BY] = value

    kx_low = jnp.zeros((BY, NZ), f32)
    for i in range(W):
        k = kp_s[i]
        kx = 0.05 * (k + (kp_s[i + 1] if i < W - 1 else end_ref[0]))
        own_rows(k, kx_low, kx, refs, i)
        kx_low = kx
    c_s[W, 0:BY] = c_s[W, 0:BY] - kx_low
    kx_low = 0.05 * (end_ref[1] + kp_s[W])
    kx_s[BX + W - 1, 0:BY] = kx_low
    c_s[BX + W - 1, 0:BY] = c_s[BX + W - 1, 0:BY] - kx_low
    for i in range(W):
        k = kp_s[W + i]
        kx = 0.05 * (k + kp_s[min(W + i + 1, 2 * W - 1)])
        own_rows(k, kx_low, kx, refs, BX + W + i)
        kx_low = kx


def dot3(a, b):
    dot = functools.partial(jnp.dot, preferred_element_type=jnp.float32)
    return dot(a[0], b[0]) + (dot(a[0], b[1]) + dot(a[1], b[0]))


def halves(a):
    hi = a.astype(jnp.bfloat16)
    return hi, (a - hi.astype(jnp.float32)).astype(jnp.bfloat16)


def place_of(owner, count, m0, m1):
    own = jnp.clip(owner, 0, count - 1)
    cls = jnp.where(own == 0, 0, jnp.where(own == count - 1, 2, 1))
    n = OVMAX + 1
    return (cls * n + jnp.clip(m0, 0, OVMAX)) * n + jnp.clip(m1, 0, OVMAX)


def stencil_body(count_x, count_y, margin_ref, yl_ref, yh_ref, xl_ref, xh_ref, cl_ref, ch_ref, fit_ref, base_hbm, send_hbm,
                 near_hbm, ytab_hbm, couple_hbm,
                 *rest_refs):
    f32 = jnp.float32
    outs = rest_refs[KEPT:]
    adv_hbm, zt_ref, lo_ref, hi_ref, lo2_ref, hi2_ref, full_ref, couple_ref = outs[:8]
    u_s, v0_s, v1_s, v2_s, kx_s, ky_s, kyd_s, kz_s, kzd_s, c_s, edge_s = outs[8 : 8 + KEPT]
    kh_s, base_s, send_s, near_s, ytab_s, sems = outs[8 + KEPT :]
    p = lax.axis_index("px")
    q = lax.axis_index("py")

    def margins(ref):
        part = ref[5 * W].astype(f32)
        return [jnp.max(a).astype(jnp.int32) for a in (part[0:8], part[16:24])]

    mine = place_of(p, count_x, margin_ref[0, 0], margin_ref[0, 1])
    low = place_of(p - 1, count_x, *margins(xl_ref))
    high = place_of(p + 1, count_x, *margins(xh_ref))
    copies = [
        pltpu.make_async_copy(base_hbm.at[mine], base_s, sems.at[0]),
        pltpu.make_async_copy(send_hbm.at[mine], send_s, sems.at[1]),
        pltpu.make_async_copy(near_hbm.at[low, 0], near_s.at[0], sems.at[2]),
        pltpu.make_async_copy(near_hbm.at[high, 1], near_s.at[1], sems.at[3]),
        pltpu.make_async_copy(ytab_hbm.at[q], ytab_s, sems.at[4]),
        pltpu.make_async_copy(couple_hbm.at[q], couple_ref, sems.at[5]),
    ]
    for copy in copies:
        copy.start()
    refs = (kx_s, ky_s, kyd_s, kz_s, kzd_s, c_s)
    from_low_x = jnp.where(p > 0, 1.0, 0.0)
    from_high_x = jnp.where(p < count_x - 1, 1.0, 0.0)
    from_low_y = jnp.where(q > 0, 1.0, 0.0)
    from_high_y = jnp.where(q < count_y - 1, 1.0, 0.0)
    beyond = slice(BY, EY)

    def halo_rows(group, carry):
        at = group * 4
        ul = yl_ref[group, 4].astype(f32) * from_low_y
        uh = yh_ref[group, 4].astype(f32) * from_high_y
        gap = jnp.zeros((4, NZ), f32)
        for i in range(4):
            x = at + i + W
            kl = yl_ref[group, i].astype(f32) * from_low_y
            kh = yh_ref[group, i].astype(f32) * from_high_y
            rest = jnp.concatenate([kh[7:8], kh[15:16], gap, kl[12:13], kl[4:5]], axis=0)
            u_s[x, beyond] = rest + jnp.concatenate([uh[4 * i : 4 * i + 4], ul[4 * i : 4 * i + 4]], axis=0)
            kh_s[x] = jnp.concatenate([kh[0:4], kl[0:4]], axis=0)
            for n, ref in enumerate((v0_s, v1_s, v2_s)):
                m = 4 * n + 4
                ref[x, beyond] = jnp.concatenate([kh[m : m + 4], kl[m : m + 4]], axis=0)
        return carry

    lax.fori_loop(0, BX // 4, halo_rows, 0, unroll=2)
    dest = (u_s, kh_s, v0_s, v1_s, v2_s)
    none = jnp.zeros((1, NZ), f32)
    for base, corner, scale, near in ((0, 0, from_low_x, range(1, W)), (BX + W, 3, from_high_x, range(W - 1))):
        low = cl_ref[corner : corner + 3].astype(f32).reshape(48, NZ) * (scale * from_low_y)
        high = ch_ref[corner : corner + 3].astype(f32).reshape(48, NZ) * (scale * from_high_y)
        for n in range(5):
            at = slice(0, 8) if n == 1 else beyond
            for i in range(W):
                if i in near:
                    row = (n * 3 + near.index(i)) * 3
                    tile = jnp.concatenate([high[row : row + 3], none, none, low[row : row + 3]], axis=0)
                else:
                    tile = jnp.zeros((8, NZ), f32)
                dest[n][base + i, at] = tile

    sub = lax.broadcasted_iota(jnp.int32, (8, NZ), 0)
    zt_up, zt_down = z_shifts(8)

    def halo_coefficients(x, carry):
        k, kx_low = carry
        k_next = kh_s[jnp.minimum(x + 1, EX - 1)]
        kx = 0.05 * (k + k_next)
        up = 0.05 * (edge_s[x, 8:16] + pltpu.roll(k, 7, 0))
        down = 0.05 * (edge_s[x, 0:8] + pltpu.roll(k, 1, 0))
        up = jnp.where(sub == 7, up, 0.0)
        down = jnp.where(sub == 0, down, 0.0)
        ky = jnp.where(sub == 7, pltpu.roll(down, 7, 0), 0.05 * (k + pltpu.roll(k, 7, 0)))
        kyd = jnp.where(sub == 0, pltpu.roll(up, 1, 0), pltpu.roll(ky, 1, 0))
        kz = 0.05 * (k + zt_down(k))
        kzd = 0.05 * (k + zt_up(k))
        kx_s[x, beyond] = kx
        ky_s[x, beyond] = ky
        kyd_s[x, beyond] = kyd
        kz_s[x, beyond] = kz
        kzd_s[x, beyond] = kzd
        c_s[x, beyond] = 1.0 - ((kx + kx_low) + (ky + kyd) + (kz + kzd))
        ky_s[x, BY - 8 : BY] = ky_s[x, BY - 8 : BY] + up
        kyd_s[x, 0:8] = kyd_s[x, 0:8] + down
        c_s[x, 0:8] = c_s[x, 0:8] - down
        c_s[x, BY - 8 : BY] = c_s[x, BY - 8 : BY] - up
        return k_next, kx

    lax.fori_loop(0, EX, halo_coefficients, (kh_s[0], jnp.zeros((8, NZ), f32)), unroll=12)

    row = lax.broadcasted_iota(jnp.int32, (EY, NZ), 0)
    row_mask = jnp.where(row < BY, 1.0, jnp.where(row < BY + W, from_high_y, from_low_y))

    for step in range(STEPS):
        lo = step
        hi = EX - 1 - step

        rows = EY if step < STEPS - 1 else BY
        z_up, z_down = z_shifts(rows)

        def one_plane(x, carry, rows=rows, z_up=z_up, z_down=z_down):
            partial, up = carry
            full = u_s[x]
            w = 0.025 * full
            g1 = v1_s[x] * w
            y_part = pltpu.roll(full * (ky_s[x] + g1), 1, 0) + pltpu.roll(full * (kyd_s[x] - g1), EY - 1, 0)
            u = full[:rows]
            g0 = v0_s[x, 0:rows] * w[:rows]
            g2 = v2_s[x, 0:rows] * w[:rows]
            prev = x - 1
            done = partial + u * (kx_s[prev, 0:rows] - g0)
            if rows == EY:
                plane_mask = jnp.where(prev < W, from_low_x, jnp.where(prev >= BX + W, from_high_x, 1.0))
                done = done * (row_mask * plane_mask)
            u_s[prev, 0:rows] = done
            up_next = u * (kx_s[x, 0:rows] + g0)
            total = u * c_s[x, 0:rows] + up + y_part[:rows]
            total = total + z_up(u * (kz_s[x, 0:rows] + g2))
            total = total + z_down(u * (kzd_s[x, 0:rows] - g2))
            return total, up_next

        first_u = u_s[lo, 0:rows]
        first_up = first_u * (kx_s[lo, 0:rows] + v0_s[lo, 0:rows] * (0.025 * first_u))
        lax.fori_loop(lo + 1, hi + 1, one_plane, (jnp.zeros((rows, NZ), f32), first_up), unroll=4)

    result = pltpu.make_async_copy(u_s.at[pl.ds(W, BX), pl.ds(0, BY)], adv_hbm, sems.at[6])
    result.start()
    for copy in copies:
        copy.wait()
    fit = (fit_ref[0], fit_ref[1])
    ytab = (ytab_s[0], ytab_s[1])

    def fit_planes(group, carry):
        at = pl.multiple_of(group * 8, 8)
        part = u_s[pl.ds(at + W, 8), 0:BY]
        rows = dot3(ytab, halves(part.reshape(8 * BY, NZ)))
        rows = dot3(halves(rows), fit)
        for r in range(YR):
            zt_ref[r, pl.ds(at, 8)] = rows[8 * r : 8 * r + 8]
        return carry

    lax.fori_loop(0, BX // 8, fit_planes, 0, unroll=8)

    send = halves(send_s[...])
    for r in range(0, YR, 2):
        lines = slice(r * MZ, (r + 2) * MZ)
        rows = dot3(send, halves(jnp.concatenate([zt_ref[r], zt_ref[r + 1]], axis=1)))
        lo_ref[:, lines] = rows[0:16]
        hi_ref[:, lines] = rows[16:32]
        lo2_ref[:, lines] = rows[0:16].astype(jnp.bfloat16)
        hi2_ref[:, lines] = rows[16:32].astype(jnp.bfloat16)
    base = base_s[...]
    full = base
    for j in range(7):
        full = full + base[:, 70 + j : 71 + j] * near_s[0, j : j + 1, :]
        full = full + base[:, 86 + j : 87 + j] * near_s[1, j : j + 1, :]
    full_ref[...] = full
    result.wait()


def combine_body(zt_ref, lo_ref, hi_ref, lo2_ref, hi2_ref, full_ref, own_ref, carry_ref):
    f32 = jnp.float32
    q = lax.axis_index("py")
    full = halves(full_ref[...])

    def stack(first, last):
        lines = slice(first * MZ, last * MZ)
        return jnp.concatenate(
            [jnp.concatenate([zt_ref[r] for r in range(first, last)], axis=1), lo_ref[:, lines], hi_ref[:, lines]]
            + [ref[:, lines].astype(f32) for ref in (lo2_ref, hi2_ref)],
            axis=0,
        )

    own = BY // 2
    for r in range(0, own, 2):
        out = dot3(full, halves(stack(r, r + 2)))
        for i in range(2):
            own_ref[:, r + i, :] = out[:, i * MZ : (i + 1) * MZ]

    block = BX // 2
    part = lax.broadcasted_iota(jnp.int32, (4 * block, 128), 0) % 4
    spread = lax.broadcasted_iota(jnp.int32, (4 * block, block), 0) // 4
    spread = jnp.where(spread == lax.broadcasted_iota(jnp.int32, (4 * block, block), 1), 1.0, 0.0).astype(jnp.bfloat16)
    spaced = []
    for f in full:
        rows = jnp.dot(spread, f, preferred_element_type=f32)
        spaced.append(
            jnp.concatenate(
                [jnp.where(part % 3 == 0, rows, 0.0), jnp.where(part == 1, rows, 0.0), jnp.where(part == 2, rows, 0.0)],
                axis=1,
            ).astype(jnp.bfloat16)
        )
    carries = stack(own, YR)
    carries = jnp.concatenate(
        [jnp.concatenate([carries[:, n * MZ : (n + 1) * MZ], carries[:, (n + 3) * MZ : (n + 4) * MZ]], axis=1) for n in range(3)],
        axis=0,
    )
    carries = dot3(spaced, halves(carries))
    coded = []
    for n in range(2):
        value = carries[:, n * MZ : (n + 1) * MZ]
        head = value.astype(jnp.bfloat16).astype(f32)
        coded.append(jnp.where(part == 3, value - head, value).astype(jnp.bfloat16))
    for t in range(carry_ref.shape[0]):

        @pl.when(t > q)
        def _():
            carry_ref[t] = coded[0]

        @pl.when(t <= q)
        def _():
            carry_ref[t] = coded[1]


def couple_body(own_ref, got_ref, couple_ref, out_ref):
    dot = functools.partial(jnp.dot, preferred_element_type=jnp.float32)
    head = couple_ref[0]
    rest = couple_ref[1]
    for x in range(0, BX // 2, 8):
        got = got_ref[:, 4 * x : 4 * x + 32].reshape(-1, MZ)
        out_ref[x : x + 8] = own_ref[x : x + 8] + (dot(head, got) + dot(rest, got)).reshape(8, BY // 2, MZ)


KEPT = 11


def in_hbm(a):
    return pltpu.with_memory_space_constraint(a, pltpu.HBM)


def own_coefficients(field, diffusivity, velocity, after):
    vmem = pl.BlockSpec(memory_space=pltpu.VMEM)
    f32 = jnp.float32
    return pl.pallas_call(
        own_body,
        out_shape=[pltpu.VMEM((EX, EY, NZ), f32)] * (KEPT - 1)
        + [pltpu.VMEM((EX, 16, NZ), f32), pltpu.VMEM((2, BY, NZ), f32)],
        in_specs=[pl.BlockSpec(memory_space=pltpu.HBM)] * 3 + [pl.BlockSpec(memory_space=pl.ANY)],
        out_specs=[vmem] * (KEPT + 1),
        scratch_shapes=[pltpu.VMEM(a.shape, a.dtype) for a in (field, diffusivity, velocity)]
        + [pltpu.SemaphoreType.DMA((3, BX // PACK))],
        compiler_params=pltpu.CompilerParams(vmem_limit_bytes=12 * 1024 * 1024),
        name="own_coefficients",
    )(*[in_hbm(a) for a in (field, diffusivity, velocity)], after)


def x_planes(count_x, xl, xh, end, kept):
    vmem = pl.BlockSpec(memory_space=pltpu.VMEM)
    f32 = jnp.float32
    return pl.pallas_call(
        functools.partial(x_planes_body, count_x),
        out_shape=[pltpu.VMEM(a.shape, f32) for a in kept],
        in_specs=[vmem] * (3 + KEPT),
        out_specs=[vmem] * KEPT,
        input_output_aliases={3 + i: i for i in range(KEPT)},
        scratch_shapes=[pltpu.VMEM((2 * W, BY, NZ), f32)],
        compiler_params=pltpu.CompilerParams(vmem_limit_bytes=8 * 1024 * 1024),
        name="x_planes",
    )(xl, xh, end, *kept)


def time_steps(counts, margin, halos, fit, tables, kept):
    vmem = pl.BlockSpec(memory_space=pltpu.VMEM)
    smem = pl.BlockSpec(memory_space=pltpu.SMEM)
    hbm = pl.BlockSpec(memory_space=pltpu.HBM)
    f32 = jnp.float32
    bf16 = jnp.bfloat16
    shapes = [((BX, BY, NZ), f32), ((YR, BX, MZ), f32)] + [((16, LINES), f32)] * 2 + [((16, LINES), bf16)] * 2
    shapes += [((BX // 2, 128), f32)]
    return pl.pallas_call(
        functools.partial(stencil_body, *counts),
        out_shape=[jax.ShapeDtypeStruct(s, t) for s, t in shapes]
        + [pltpu.VMEM(tables[-1].shape[1:], bf16)]
        + [pltpu.VMEM(a.shape, f32) for a in kept],
        in_specs=[smem] + [vmem] * 7 + [hbm] * 5 + [vmem] * KEPT,
        out_specs=[hbm] + [vmem] * (7 + KEPT),
        input_output_aliases={13 + i: 8 + i for i in range(KEPT)},
        scratch_shapes=[
            pltpu.VMEM((EX, 8, NZ), f32),
            pltpu.VMEM((BX // 2, 128), f32),
            pltpu.VMEM((BX // 2, BX), f32),
            pltpu.VMEM((2, 8, 128), f32),
            pltpu.VMEM((2, YR * 8, 8 * BY), bf16),
            pltpu.SemaphoreType.DMA((7,)),
        ],
        compiler_params=pltpu.CompilerParams(vmem_limit_bytes=STEP_VMEM * 1024 * 1024),
        name="time_steps",
    )(margin, *halos, fit, *[in_hbm(t) for t in tables], *kept)[:8]


def combine(count_y, rows):
    vmem = pl.BlockSpec(memory_space=pltpu.VMEM)
    return pl.pallas_call(
        combine_body,
        out_shape=[
            jax.ShapeDtypeStruct((BX // 2, BY // 2, MZ), jnp.float32),
            jax.ShapeDtypeStruct((count_y, 2 * BX, MZ), jnp.bfloat16),
        ],
        in_specs=[vmem] * 6,
        out_specs=[vmem] * 2,
        compiler_params=pltpu.CompilerParams(vmem_limit_bytes=12 * 1024 * 1024),
        name="combine",
    )(*rows)


def add_carries(own, got, couple):
    vmem = pl.BlockSpec(memory_space=pltpu.VMEM)
    return pl.pallas_call(
        couple_body,
        out_shape=jax.ShapeDtypeStruct((BX // 2, BY // 2, MZ), jnp.float32),
        in_specs=[vmem] * 3,
        out_specs=vmem,
        compiler_params=pltpu.CompilerParams(vmem_limit_bytes=8 * 1024 * 1024),
        name="add_carries",
    )(own, got, couple)


def ring(n, d):
    return [(i, (i + d) % n) for i in range(n)]


def shift(a, axis, d):
    return lax.ppermute(a, axis, ring(lax.axis_size(axis), d))


def pack_body(margin_hbm, f_hbm, k_hbm, v_hbm, ylo_ref, yhi_ref, xlo_ref, xhi_ref, f_ref, k_ref, v_ref, margin_ref, sems,
              margin_sem):
    f32 = jnp.float32
    bf16 = jnp.bfloat16
    t = BY - W
    margin_copy = pltpu.make_async_copy(margin_hbm, margin_ref, margin_sem)
    margin_copy.start()
    copies = load((f_hbm, k_hbm, v_hbm), (f_ref, k_ref, v_ref), sems)

    def rest(u):
        return u - u.astype(bf16).astype(f32)

    def faces(g, carry):
        tails, heads = [], []
        for i in range(4):
            x = 4 * g + i
            u = f_ref[x]
            tails.append(u[t:])
            heads.append(u[:W])
            ur_t = rest(u[t - 4 :])
            ur_h = rest(u[:8])
            k, v0, v1, v2 = [r.astype(f32) for r in (k_ref[x], v_ref[0, x], v_ref[1, x], v_ref[2, x])]
            ylo_ref[g, i] = jnp.concatenate(
                [k[t:], ur_t[7:8], v0[t + 1 :], v1[t:], ur_t[6:7], v2[t + 1 :]], axis=0
            ).astype(bf16)
            yhi_ref[g, i] = jnp.concatenate(
                [k[:W], v0[: W - 1], ur_h[0:1], v1[:W], v2[: W - 1], ur_h[1:2]], axis=0
            ).astype(bf16)
        ylo_ref[g, 4] = jnp.concatenate(tails, axis=0).astype(bf16)
        yhi_ref[g, 4] = jnp.concatenate(heads, axis=0).astype(bf16)
        return carry

    def x_side(at, out, near, outer):
        for i in range(W):
            out[i] = f_ref[at + i].astype(bf16)
            out[W + i] = k_ref[at + i]
            out[2 * W + i] = v_ref[0, at + i]
            if i == outer:
                out[3 * W + i] = rest(f_ref[at + near[0]]).astype(bf16)
                out[4 * W + i] = rest(f_ref[at + near[1]]).astype(bf16)
            else:
                out[3 * W + i] = v_ref[1, at + i]
                out[4 * W + i] = v_ref[2, at + i]
        half = jnp.zeros((16, NZ), f32)
        out[5 * W] = jnp.concatenate([half + margin_ref[0, 0].astype(f32), half + margin_ref[0, 1].astype(f32)], axis=0).astype(bf16)

    margin_copy.wait()
    for c in range(BX // PACK):
        for copy in copies[c]:
            copy.wait()
        lax.fori_loop(c * PACK // 4, (c + 1) * PACK // 4, faces, 0)
        if c == 0:
            x_side(0, xhi_ref, (0, 1), W - 1)
    x_side(BX - W, xlo_ref, (W - 1, W - 2), 0)


def corner_body(xl_ref, xh_ref, up_ref, down_ref):
    f32 = jnp.float32
    for side, ref, near in ((0, xl_ref, range(1, W)), (1, xh_ref, range(W - 1))):
        planes = [ref[n * W + i].astype(f32) for n in range(5) for i in near]
        gap = [jnp.zeros((3, NZ), f32)]
        part = slice(side * 3, side * 3 + 3)
        for out, rows in ((up_ref, slice(BY - 3, BY)), (down_ref, slice(0, 3))):
            out[part] = jnp.concatenate([a[rows] for a in planes] + gap, axis=0).reshape(3, 16, NZ).astype(jnp.bfloat16)


def halo_parts(field, diffusivity, velocity, margin):
    bf16 = jnp.bfloat16
    y_shape = (BX // 4, 5, 16, NZ)
    x_shape = (5 * W + 1, BY, NZ)
    c_shape = (6, 16, NZ)
    vmem = pl.BlockSpec(memory_space=pltpu.VMEM)
    hbm = pl.BlockSpec(memory_space=pltpu.HBM)
    ylo, yhi, xlo, xhi = pl.pallas_call(
        pack_body,
        out_shape=[jax.ShapeDtypeStruct(s, bf16) for s in [y_shape] * 2 + [x_shape] * 2],
        in_specs=[hbm] * 4,
        out_specs=[vmem] * 4,
        scratch_shapes=[pltpu.VMEM(a.shape, a.dtype) for a in (field, diffusivity, velocity)]
        + [pltpu.SMEM(margin.shape, jnp.int32), pltpu.SemaphoreType.DMA((3, BX // PACK)), pltpu.SemaphoreType.DMA(())],
        compiler_params=pltpu.CompilerParams(vmem_limit_bytes=PACK_VMEM * 1024 * 1024),
        name="pack_faces",
    )(*[in_hbm(a) for a in (margin, field, diffusivity, velocity)])
    xl = shift(xlo, "px", 1)
    xh = shift(xhi, "px", -1)
    yl = shift(ylo, "py", 1)
    yh = shift(yhi, "py", -1)
    kept = own_coefficients(field, diffusivity, velocity, ylo)
    xl, xh, kept = lax.optimization_barrier((xl, xh, kept))
    c_up, c_down = pl.pallas_call(
        corner_body,
        out_shape=[jax.ShapeDtypeStruct(c_shape, bf16)] * 2,
        in_specs=[vmem] * 2,
        out_specs=[vmem] * 2,
        compiler_params=pltpu.CompilerParams(vmem_limit_bytes=4 * 1024 * 1024),
        name="pack_corners",
    )(xl, xh)
    halos = (yl, yh, xl, xh, shift(c_up, "py", 1), shift(c_down, "py", -1))
    _, kept = lax.optimization_barrier((c_up, kept))
    return halos, x_planes(lax.axis_size("px"), xl, xh, kept[KEPT], kept[:KEPT])


def per_device(field, diffusivity, velocity, margin):
    count_x = lax.axis_size("px")
    count_y = lax.axis_size("py")
    fit = jnp.asarray(np.stack(split(fit_matrix(NZ).T)))
    ytab, couple = y_tables(count_y)
    tables = [jnp.asarray(t) for t in x_tables(count_x) + [ytab, couple]]
    halos, kept = halo_parts(field, diffusivity, velocity, margin)
    advected, zt, lo, hi, lo2, hi2, full, couple = time_steps(
        (count_x, count_y), margin, halos, fit, tables, kept
    )
    rows = (zt, shift(lo, "px", 1), shift(hi, "px", -1), shift(lo2, "px", 2), shift(hi2, "px", -2), full)
    own, carries = combine(count_y, rows)
    got = lax.all_to_all(carries, "py", split_axis=0, concat_axis=0, tiled=True)
    return advected, add_carries(own, got, couple)


def solution(mesh):
    placed = (P("px", "py", None), P("px", "py", None), P(None, "px", "py", None), P("px", None))
    return jax.shard_map(
        per_device,
        mesh=mesh,
        in_specs=placed,
        out_specs=(P("px", "py", None), P("px", "py", None)),
        check_vma=False,
    )
```
